512 devices in a mesh: grp: 16 (over y, core), graph: 32 (over x, z).
Axes of the slice: x: 4, y: 8, z: 8, core: 2. Of those that a mesh axis runs over, the one named last changes fastest.
Arguments:
- atoms: bfloat16 [16, 128, 9, 512], P('grp', 'graph'), may hold values from -6 to 6
- cotangent: bfloat16 [16, 128, 9, 512], P('grp', 'graph'), may hold values from -0.75 to 0.75
- expert_weights: bfloat16 [32, 3, 512, 512], P('grp', None, 'graph'), may hold values from -1 to 1
- coefficients: int32 [16, 32], replicated, may hold values from 1 to 256, 1024 in all within a row
- src_owner: int32 [16, 4096, 1], P('grp', 'graph'), may hold values from 0 to 31; in each aligned block of 128 rows (0 to 127, 128 to 255, ..., all dimensions but the last counted through in order) at most 6 rows name the same one
- src_slot: int32 [16, 4096], P('grp', 'graph'), may hold values from 0 to 3
- tgt_slot: int32 [16, 4096], P('grp', 'graph'), may hold values from 0 to 3
- rot_index: int32 [16, 4096], P('grp', 'graph'), may hold values from 0 to 63
- rot_table: float32 [64, 9, 9], replicated, may hold values from -3 to 3, as said below
Outputs:
- grad_atoms: float32 [16, 128, 9, 512], P('grp', 'graph')
- grad_experts: float32 [32, 3, 512, 512], P('grp', None, 'graph')
The draws below stay inside these ranges and needn't reach their ends.
Inputs may be any that keep to these rules, and one draw needn't show every extreme that they name: `src_owner`: among the 128 edges of one index of graph (aligned blocks of rows), no owner is named more than 6 times, a bound that some block reaches. `coefficients`: each row sums to 1024. Every rot_table[r] is block diagonal with blocks over coefficients 0, 1..3 and 4..8.
All inputs are finite; a program needn't handle non-finite values.
Results may differ from the reference program's by a relative error of at most 0.035.
Values may be sent and summed in bfloat16 or wider, within the bound.
A program may use at most 64 MiB of HBM per device.

```python
import math
import jax
import jax.numpy as jnp
import numpy as np
from jax import lax

C = 512
E_DEV = 128
A_DEV = 4
NROT = 64
SYSTEMS = 16
ATOMS = 128
EDGES = 4096
EXPERTS = 32
CAP = 6
N_GRAPH = 32


def draw_rot_table(key, part):
    key = jax.random.fold_in(key, 11)
    indices = jnp.arange(9)
    degree_of = (indices >= 1).astype(jnp.int32) + (indices >= 4).astype(jnp.int32)
    within = (degree_of[:, None] == degree_of[None, :]).astype(jnp.float32)
    widths = (2 * degree_of + 1).astype(jnp.float32)
    entries = jnp.clip(jax.random.normal(key, (NROT, 9, 9), jnp.float32), -3.0, 3.0)
    return entries * within / jnp.sqrt(widths)[None, :, None]


def place_ends(drawn, own_key, least, high):
    extent = drawn.shape
    place = [jax.random.randint(jax.random.fold_in(own_key, axis), (), 0, extent[axis]) for axis in range(len(extent))]
    drawn = drawn.at[tuple(place)].set(least)
    longest = extent.index(max(extent))
    place[longest] = (place[longest] + 1) % extent[longest]
    return drawn.at[tuple(place)].set(high)


def steps_of(key, extent, cuts, least, high):
    gain, own = 1.0, jax.random.fold_in(key, 6)
    for axis_at, parts in cuts:
        heights = jnp.exp(jax.random.uniform(jax.random.fold_in(own, axis_at), (parts,), jnp.float32, least / len(cuts), high / len(cuts)))
        gain = gain * jnp.repeat(heights, extent[axis_at] // parts).reshape([-1 if axis == axis_at else 1 for axis in range(len(extent))])
    return gain


def length_profile(number_of, total, bound, slope):
    weights = [(1 << 20) // math.isqrt(rank ** slope) + 1 for rank in range(2, number_of + 1)]
    spare, given = total - bound - (number_of - 1), [1] * (number_of - 1)
    while spare > 0:
        movable = [i for i in range(number_of - 1) if given[i] < bound]
        pool, budget = sum([weights[i] for i in movable]), spare
        for i in movable:
            extra = min(bound - given[i], max(1, budget * weights[i] // pool), spare)
            given[i] = given[i] + extra
            spare = spare - extra
    return np.array([bound] + given)


def ragged(stream_key, count, total, bound, skew):
    if count == 2:
        one = jax.random.randint(stream_key, (), max(1, total - bound), min(bound, total - 1) + 1)
        return jnp.stack([one, total - one])
    lengths = jnp.asarray(length_profile(count, total, bound, skew), jnp.int32)
    twos = (count - 1) // 2
    source_of, taker = lengths[1:1 + 2 * twos:2], lengths[2:2 + 2 * twos:2]
    slack = jnp.minimum(source_of - 1, bound - taker)
    shifted = jax.random.randint(jax.random.fold_in(stream_key, 1), (twos,), 0, 1 << 20) % (slack + 1)
    lengths = lengths.at[1:1 + 2 * twos:2].set(source_of - shifted).at[2:2 + 2 * twos:2].set(taker + shifted)
    return lengths[jax.random.permutation(jax.random.fold_in(stream_key, 2), count)]


def assign_block(own_key, own, number, rows, count, top, reach, skew):
    order = jax.random.permutation(own_key, count)
    crowded, usual = load_shares(count, rows * top, reach, skew, True), load_shares(count, rows * top, reach, skew, False)
    places = jnp.arange(count)

    def named(sizes, turn):
        used = int((sizes > 0).sum())
        fixed = max(1, used // 4)
        passed = fixed + (places - fixed + turn * (used - fixed)) % max(1, count - fixed)
        return jnp.zeros((count,), jnp.int32).at[order[jnp.where(places < fixed, places, passed)]].set(jnp.asarray(sizes, jnp.int32))

    sizes = jnp.where(number % 4 == 0, named(crowded, number // 4), named(usual, number - number // 4 - 1))
    mixed = jax.random.permutation(jax.random.fold_in(own, 3), count)
    source_of, sink = mixed[0:count // 2 * 2:2], mixed[1:count // 2 * 2:2]
    slack = jnp.minimum(sizes[source_of] - 1, reach - sizes[sink]) // 2
    slack = jnp.where((source_of == order[0]) | (sink == order[0]) | (sizes[sink] == 0), 0, jnp.maximum(slack, 0))
    passed = jax.random.randint(jax.random.fold_in(own, 4), (count // 2,), 0, 1 << 20) % (slack + 1)
    sizes = sizes.at[source_of].add(-passed).at[sink].add(passed)
    items = jnp.searchsorted(jnp.cumsum(sizes), jnp.arange(rows * top), side="right").astype(jnp.int32)
    listing = items.reshape(top, rows).T
    listing = listing[jax.random.permutation(jax.random.fold_in(own, 1), rows)]
    turn = jax.random.randint(jax.random.fold_in(own, 2), (rows, 1), 0, top)
    return jnp.take_along_axis(listing, (jnp.arange(top)[None, :] + turn) % top, axis=1)


def load_shares(number_of, total, limit, skew, full):
    portions = [(1 << 20) // math.isqrt(standing ** skew) + 1 for standing in range(1, number_of + 1)]
    largest = limit if full else min(limit, max(-(-total // number_of), total * portions[0] // sum(portions)))
    least = 1 if total - largest >= number_of - 1 else 0
    counts, rest = [largest] + [least] * (number_of - 1), total - largest - least * (number_of - 1)
    while rest > 0:
        movable = [i for i in range(1, number_of) if counts[i] < largest] or [i for i in range(1, number_of) if counts[i] < limit]
        mass, remaining = sum([portions[i] for i in movable]), rest
        for i in movable:
            addition = min(limit - counts[i], max(1, remaining * portions[i] // mass), rest)
            counts[i] = counts[i] + addition
            rest = rest - addition
    return np.array(counts)


def noise(own_key, extent, spread, bound, split=(), held_as=jnp.bfloat16):
    result = spread * jax.random.normal(own_key, extent, jnp.float32)
    if split:
        result = result * steps_of(own_key, extent, split, -0.22, 0.18)
    return jnp.clip(result, -bound, bound).astype(held_as)


def setup_inputs(seed: int = 0) -> dict:
    arg_keys = jax.random.split(jax.random.key(seed), 10)
    atoms = noise(arg_keys[0], (SYSTEMS, ATOMS, 9, C), 1.0, 6.0, ((0, 16), (1, 32)))
    cotangent = noise(arg_keys[1], (SYSTEMS, ATOMS, 9, C), 0.125, 0.75, ((0, 16), (1, 32)))
    expert_weights = noise(arg_keys[2], (EXPERTS, 3, C, C), (C // 16) ** -0.5, 1.0, ((0, 16), (2, 32)))
    coefficients = jax.vmap(lambda own: ragged(own, EXPERTS, 1024, 256, 2))(jax.random.split(arg_keys[3], SYSTEMS)).reshape((SYSTEMS, EXPERTS)).astype(jnp.int32)
    src_owner_keys = jax.random.split(jax.random.fold_in(arg_keys[4], 1), SYSTEMS * EDGES // E_DEV)
    src_owner_turns = jax.random.permutation(jax.random.fold_in(arg_keys[4], 3), SYSTEMS * EDGES // E_DEV)
    src_owner = jax.vmap(lambda own, number: assign_block(jax.random.fold_in(arg_keys[4], 2), own, number, E_DEV, N_GRAPH, 1, CAP, 2))(src_owner_keys, src_owner_turns).reshape((SYSTEMS, EDGES, 1))
    src_slot = place_ends(jax.random.randint(arg_keys[5], (SYSTEMS, EDGES), 0, A_DEV), jax.random.fold_in(arg_keys[5], 1), 0, A_DEV - 1).astype(jnp.int32)
    tgt_slot = place_ends(jax.random.randint(arg_keys[6], (SYSTEMS, EDGES), 0, A_DEV), jax.random.fold_in(arg_keys[6], 1), 0, A_DEV - 1).astype(jnp.int32)
    rot_index = place_ends(jax.random.randint(arg_keys[7], (SYSTEMS, EDGES), 0, NROT), jax.random.fold_in(arg_keys[7], 1), 0, NROT - 1).astype(jnp.int32)
    rot_table = draw_rot_table(jax.random.fold_in(arg_keys[9], 71), 0)
    return dict(atoms=atoms, cotangent=cotangent, expert_weights=expert_weights, coefficients=coefficients, src_owner=src_owner, src_slot=src_slot, tgt_slot=tgt_slot, rot_index=rot_index, rot_table=rot_table)


precise = lax.Precision.HIGHEST
degree_spans = ((0, 1), (1, 4), (4, 9))


def per_degree(operand, matrices, flipped):
    pieces = []
    contracted = 1 if flipped else 0
    for degree in range(3):
        opening, closing = degree_spans[degree]
        segment = operand[:, opening:closing, :]
        flattened = segment.reshape(-1, segment.shape[-1])
        product = lax.dot_general(flattened, matrices[degree], (((1,), (contracted,)), ((), ())), preferred_element_type=jnp.float32)
        pieces.append(product.reshape(segment.shape[0], closing - opening, -1))
    return jnp.concatenate(pieces, axis=1)


def rotate(rotations, values, flipped):
    form = "eba,ebc->eac" if flipped else "eab,ebc->eac"
    return jnp.einsum(form, rotations, values.astype(jnp.float32), precision=precise)


def system_pass(atoms, cotangent, mixed, sources, targets, rot_index, rot_table):
    rotations = rot_table[rot_index]
    rotated = rotate(rotations, atoms[sources], False).astype(jnp.bfloat16)
    hidden = per_degree(rotated, mixed, False)
    gates = jax.nn.sigmoid(hidden[:, 0:1, :])
    msg_grads = rotate(rotations, cotangent[targets], False)
    leading = (jnp.arange(9) == 0).astype(jnp.float32)[None, :, None]
    gate_terms = jnp.sum(msg_grads * hidden, axis=1, keepdims=True) * gates * (1.0 - gates)
    hidden_grads = (msg_grads * gates + leading * gate_terms).astype(jnp.bfloat16)
    weight_terms = []
    rot_blocks = rotated.reshape(N_GRAPH, E_DEV, 9, C)
    grad_blocks = hidden_grads.reshape(N_GRAPH, E_DEV, 9, C)
    for degree in range(3):
        opening, closing = degree_spans[degree]
        lefts = rot_blocks[:, :, opening:closing, :].reshape(N_GRAPH, -1, C).astype(jnp.float32)
        rights = grad_blocks[:, :, opening:closing, :].reshape(N_GRAPH, -1, C).astype(jnp.float32)
        partial_value = jnp.einsum("gkc,gkd->gcd", lefts, rights, precision=precise).astype(jnp.bfloat16)
        partial_value = lax.optimization_barrier(partial_value)
        weight_terms.append(jnp.sum(partial_value.astype(jnp.float32), axis=0))
    system_grads = jnp.stack(weight_terms)
    rot_grads = per_degree(hidden_grads, mixed, True)
    edge_grads = rotate(rotations, rot_grads, True).astype(jnp.bfloat16)
    atom_grads = jax.ops.segment_sum(edge_grads.astype(jnp.float32), sources, num_segments=ATOMS)
    return atom_grads, system_grads


def reference(atoms, cotangent, expert_weights, coefficients, src_owner, src_slot, tgt_slot, rot_index, rot_table):
    shares = coefficients.astype(jnp.float32) / 1024.0
    mixed = jnp.einsum("sk,klab->slab", shares, expert_weights.astype(jnp.float32), precision=precise).astype(jnp.bfloat16)
    sources = (src_owner[:, :, 0] * A_DEV + src_slot).astype(jnp.int32)
    offsets = (jnp.arange(EDGES, dtype=jnp.int32) // E_DEV) * A_DEV
    targets = (offsets[None, :] + tgt_slot).astype(jnp.int32)

    def per_system(items):
        return system_pass(items[0], items[1], items[2], items[3], items[4], items[5], rot_table)

    grad_atoms, system_grads = lax.map(per_system, (atoms, cotangent, mixed, sources, targets, rot_index))
    grad_experts = jnp.einsum("sk,slab->klab", shares, system_grads, precision=precise)
    return grad_atoms, grad_experts
```

```python
import jax
import jax.numpy as jnp
from jax import lax
from jax.experimental import pallas as pl
from jax.experimental.pallas import tpu as pltpu
from jax.sharding import PartitionSpec as P

F32, BF16, I32 = jnp.float32, jnp.bfloat16, jnp.int32
NX, NZ, NY = 4, 8, 8
SPANS = ((0, 1), (1, 4), (4, 9))
DEGREE = (0, 1, 1, 1, 2, 2, 2, 2, 2)
MESH = pl.DeviceIdType.MESH
NN = (((1,), (0,)), ((), ()))
NT = (((1,), (1,)), ((), ()))

(PH_CORE, PH_Y, PH_YX, PH_ATX, PH_ATR, PH_ATL, PH_COX, PH_COZ, PH_MZ, PH_MC,
 PH_GZ, PH_GX, PH_SZ, PH_SYX, PH_FW, PH_END) = range(16)
NEAR = (-2, -1, 0, 1, 2)
ENTRY = {}
for _opening, _closing in SPANS:
    for _i in range(_opening, _closing):
        for _b in range(_opening, _closing):
            ENTRY[_i, _b] = len(ENTRY)


def dot(a, b, dims=NN):
    return lax.dot_general(a, b, dims, preferred_element_type=F32)


def one_hot(test):
    return jnp.where(test, 1.0, 0.0).astype(BF16)


def grid_of(rows, columns):
    shape = (rows, columns)
    return lax.broadcasted_iota(I32, shape, 0), lax.broadcasted_iota(I32, shape, 1)


def split48(index):
    block = jnp.where(index >= 48, 1, 0) + jnp.where(index >= 96, 1, 0) + jnp.where(index >= 144, 1, 0)
    return block, index - 48 * block


def kernel(
    coef, w_hbm, at_hbm, co_hbm, owner_hbm, slot_hbm, tslot_hbm, turn_hbm, rt_hbm,
    ga_ref, ge_ref,
    w_own, w_sib, at_in, co_in, index_in, rt_in, rt35,
    ybuf, yrecv, yxbuf, yxrecv, mx, mzbuf, wc, mc,
    at48, atx, a_ref, co80, cox, cobuf, corecv,
    expand, fold, spread, perm, unperm, order, gather16, same, rot2,
    hs, cs, hh, ch, grads_at, turns, oh, u_ref, g_acc, gbuf, grecv, gxbuf, gxrecv,
    sgt, sgbuf, sgrecv, sg4, sgx, forwarded, endbuf, endrecv,
    load_sem, send_sem, recv_sem,
):
    grp, graph = lax.axis_index("grp"), lax.axis_index("graph")
    y, core = lax.div(grp, 2), lax.rem(grp, 2)
    x, z = lax.div(graph, NZ), lax.rem(graph, NZ)

    def device(dy=None, dx=None, dz=None, other=False):
        along = y if dy is None else lax.rem(y + dy + NY, NY)
        across = x if dx is None else lax.rem(x + dx, NX)
        up = z if dz is None else lax.rem(z + dz, NZ)
        return {"grp": along * 2 + (1 - core if other else core), "graph": across * NZ + up}

    def remote(phase, slot, source, target, place):
        return pltpu.make_async_remote_copy(
            src_ref=source, dst_ref=target, send_sem=send_sem.at[phase, slot],
            recv_sem=recv_sem.at[phase, slot], device_id=place, device_id_type=MESH,
        )

    def each(count, body):
        def step(d, carry):
            body(d)
            return carry

        lax.fori_loop(1, count, step, 0)

    def arrived(phase, slot, ref):
        pltpu.make_async_copy(ref, ref, recv_sem.at[phase, slot]).wait()

    def left(phase, slot, ref):
        pltpu.make_async_copy(ref, ref, send_sem.at[phase, slot]).wait()

    loads = [
        pltpu.make_async_copy(source, target, load_sem.at[k])
        for k, (source, target) in enumerate((
            (w_hbm, w_own), (at_hbm, at_in), (co_hbm, co_in), (owner_hbm, index_in.at[0]),
            (slot_hbm, index_in.at[1]), (tslot_hbm, index_in.at[2]), (turn_hbm, index_in.at[3]),
            (rt_hbm, rt_in)))
    ]
    for load in loads:
        load.start()

    barrier = pltpu.get_barrier_semaphore()

    def greet(place):
        pl.semaphore_signal(barrier, inc=1, device_id=place, device_id_type=MESH)

    greet(device(other=True))
    for dy in NEAR:
        if dy:
            greet(device(dy=dy))
        each(NX, lambda d: greet(device(dy=dy, dx=d)))
    each(NZ, lambda d: greet(device(dz=d)))

    row, column = grid_of(144, 192)
    block, within = split48(column)
    order[...] = one_hot(
        ((within >> 2) == (row >> 4)) & (((row >> 2) & 3) == block) & ((within & 3) == (row & 3)))
    row, column = grid_of(16, 192)
    block, within = split48(column)
    gather16[...] = one_hot(row == block * 4 + (within & 3))
    row, column = grid_of(192, 16)
    block, within = split48(row)
    expand[...] = one_hot(column == block * 4 + (within & 3))
    row, column = grid_of(192, 256)
    block, within = split48(row)
    same[...] = jnp.where((within >> 2) == (column >> 4), 1.0, 0.0)
    for t in range(NZ):
        row, column = grid_of(128, 256)
        spread[t] = one_hot(((row >> 4) == t) & ((row & 15) == (column & 15)))
        row, column = grid_of(256, 128)
        fold[t] = one_hot(((column >> 4) == t) & ((row & 15) == (column & 15)))
        for l in range(3):
            row, column = grid_of(128, 128)
            perm[l, :, t * 128:(t + 1) * 128] = one_hot(
                ((row >> 4) == t) & ((column >> 4) == l) & ((row & 15) == (column & 15)))
            unperm[t, :, l * 128:(l + 1) * 128] = one_hot(
                ((column >> 4) == t) & ((row >> 4) == l) & ((row & 15) == (column & 15)))

    for load in loads:
        load.wait()

    for b in range(9):
        co80[0, b * 4:b * 4 + 4, :] = co_in[b].astype(F32)
        at48[0, b * 4:b * 4 + 4, :] = at_in[b].astype(F32)
    at48[0, 36:48, :] = jnp.zeros((12, 512), F32)
    co80[0, 36:48, :] = jnp.zeros((12, 512), F32)

    def place(owner, slot):
        return (owner & 7) * 16 + (owner >> 3) * 4 + slot

    row = lax.broadcasted_iota(I32, (16, 128), 0)
    codes = jnp.where(row == 0, place(index_in[0], index_in[1]), 0)
    codes = jnp.where(row == 1, place(graph, index_in[2]), codes)
    codes = jnp.where(row == 2, index_in[3], codes).astype(F32).astype(BF16)
    for xb in range(NX):
        at = slice(xb * 128, (xb + 1) * 128)
        atx_out = at48[0, :, at].astype(BF16)
        cox_out = co80[0, :, at].astype(BF16)
        atx[NX, xb] = atx_out
        cox[NX + xb, 0:48, :] = cox_out
        cox[NX + xb, 48:64, :] = codes

    pl.semaphore_wait(barrier, 1 + 4 + 5 * (NX - 1) + (NZ - 1))

    core_copy = remote(PH_CORE, 0, w_own, w_sib, device(other=True))
    core_copy.start()
    each(NX, lambda d: remote(PH_ATX, 0, atx.at[NX], atx.at[x], device(dx=d)).start())
    each(NX, lambda d: remote(
        PH_COX, 0, cox.at[NX + lax.rem(x + d, NX)], cox.at[x], device(dx=d)).start())
    atx[x] = atx[NX]
    cox[x] = cox[NX + x]

    core_copy.wait_recv()

    def share(dy, expert):
        return coef[lax.rem(y + dy + NY, NY) * 2 + core, expert].astype(F32) * (1.0 / 1024.0)

    own_first, other_first = grp * 2, (y * 2 + 1 - core) * 2

    def partial_of(dy, xb):
        at = slice(xb * 128, (xb + 1) * 128)
        total = None
        for ref, first in ((w_own, own_first), (w_sib, other_first)):
            for e in range(2):
                term = share(dy, first + e) * ref[e, :, :, at].astype(F32)
                total = term if total is None else total + term
        return total

    steps = ((0, -4, -2), (1, 3, 1), (2, -3, -1))
    for slot, dy, hop in steps:
        for xb in range(NX):
            ybuf[slot, xb] = partial_of(dy, xb).astype(BF16)
        remote(PH_Y, slot, ybuf.at[slot], yrecv.at[slot], device(dy=hop)).start()

    def yx_send(k):
        dy = NEAR[k]
        if dy:
            remote(PH_YX, k, yxbuf.at[k, x], yxrecv.at[k, x], device(dy=dy)).start()
        else:
            yxrecv[k, x] = yxbuf[k, x]
        each(NX, lambda d: remote(
            PH_YX, k, yxbuf.at[k, lax.rem(x + d, NX)], yxrecv.at[k, x], device(dy=dy, dx=d)).start())

    for k in (1, 3, 2):
        for xb in range(NX):
            yxbuf[k, xb] = partial_of(NEAR[k], xb).astype(BF16)
        yx_send(k)

    arrived(PH_ATX, 0, atx.at[pl.ds(0, NX - 1)])
    for xb in range(NX):
        stacked = jnp.concatenate([atx[s, xb] for s in range(NX)], axis=0)
        a_ref[z, :, :, xb * 128:(xb + 1) * 128] = dot(order[...], stacked).astype(BF16).reshape(9, 16, 128)

    def right_copy(s):
        slot = lax.rem(z - s + NZ, NZ)
        return remote(PH_ATR, s, a_ref.at[slot], a_ref.at[slot], device(dz=1))

    def left_copy(s):
        slot = lax.rem(z + s, NZ)
        return remote(PH_ATL, s, a_ref.at[slot], a_ref.at[slot], device(dz=NZ - 1))

    arrived(PH_COX, 0, cox.at[pl.ds(0, NX - 1)])
    stacked = jnp.concatenate([cox[s, 0:48] for s in range(NX)], axis=0)
    for t in range(NZ):
        wide = (dot(stacked, spread[t]) * same[...]).astype(BF16)
        packed = dot(gather16[...], wide).astype(BF16)
        cobuf[t, 0] = packed[:, 0:128]
        cobuf[t, 1] = packed[:, 128:256]
        for s in range(NX):
            cobuf[t, 2 + s] = cox[s, 48:64]
    each(NZ, lambda d: remote(
        PH_COZ, 0, cobuf.at[lax.rem(z + d, NZ)], corecv.at[z], device(dz=d)).start())
    corecv[z] = cobuf[z]
    right_copy(0).start()
    left_copy(0).start()

    for slot in range(3):
        arrived(PH_Y, slot, yrecv.at[slot])
    for xb in range(NX):
        yxbuf[0, xb] = (partial_of(-2, xb) + yrecv[0, xb].astype(F32) + yrecv[2, xb].astype(F32)).astype(BF16)
    yx_send(0)
    for xb in range(NX):
        yxbuf[4, xb] = (partial_of(2, xb) + yrecv[1, xb].astype(F32)).astype(BF16)
    yx_send(4)

    for i in range(9):
        opening, closing = SPANS[DEGREE[i]]
        first = ENTRY[i, opening]
        rt35[first:first + closing - opening, :] = rt_in[i, opening:closing, :]
    rt35[35:40, :] = jnp.zeros((5, 64), F32)
    table = rt35[...]
    high = table.astype(BF16)
    rot2[:, 0:64] = high
    rot2[:, 64:128] = (table - high.astype(F32)).astype(BF16)

    arrived(PH_COZ, 0, corecv.at[pl.ds(0, NZ - 1)])
    for half in range(2):
        tall = jnp.transpose(corecv[:, half].reshape(128, 128).astype(F32)).astype(BF16)
        rows = 128 if half == 0 else 16
        cs[half * 128:half * 128 + rows, :] = tall[0:rows]

    def turned(entries, values, opening, closing, i):
        total = entries[i, opening] * values(opening)
        for b in range(opening + 1, closing):
            total = total + entries[i, b] * values(b)
        return total

    def entries_of(t, at):
        return {key: turns[t, k:k + 1, at] for key, k in ENTRY.items()}

    def prepare(t, carry):
        lanes = lax.broadcasted_iota(I32, (128, 128), 0).astype(F32)
        folded = (lax.broadcasted_iota(I32, (128, 128), 0) & 63).astype(F32)
        for q in range(NX):
            at = slice(q * 128, (q + 1) * 128)
            codes = corecv[t, 2 + q].astype(F32)
            oh[t, :, at] = one_hot(lanes == codes[0:1])
            oh[NZ, :, at] = one_hot(lanes == codes[1:2])
            oh[NZ + 1, :, at] = one_hot(folded == codes[2:3])
        ch[...] = dot(cs[...], oh[NZ])
        turns[t] = dot(rot2[...], oh[NZ + 1])
        for q in range(NX):
            at = slice(q * 128, (q + 1) * 128)
            entries = entries_of(t, at)
            for opening, closing in SPANS:
                for i in range(opening, closing):
                    grads_at[t, i * 16:(i + 1) * 16, at] = turned(
                        entries, lambda b: ch[b * 16:(b + 1) * 16, at], opening, closing, i)
        return carry

    def pass_on(s):
        right_copy(s - 1).wait_recv()
        right_copy(s).start()
        left_copy(s - 1).wait_recv()
        if s < 3:
            left_copy(s).start()

    pass_on(1)
    lax.fori_loop(0, 3, prepare, 0)
    pass_on(2)
    lax.fori_loop(3, 5, prepare, 0)

    for k, dy in enumerate(NEAR):
        arrived(PH_YX, k, yxrecv.at[k] if dy else yxrecv.at[k, pl.ds(0, NX - 1)])
    packed = jnp.zeros((64, 1024), F32)
    for l in range(3):
        for s in range(NX):
            total = yxrecv[0, s, l].astype(F32)
            for k in range(1, 5):
                total = total + yxrecv[k, s, l].astype(F32)
            mx[s, l] = total.astype(BF16)
        packed = packed + dot(mx[:, l].reshape(64, 128), perm[l])
    packed = packed.astype(BF16)
    for t in range(NZ):
        mzbuf[t] = packed[:, t * 128:(t + 1) * 128].reshape(NX, 16, 128)
    each(NZ, lambda d: remote(
        PH_MZ, 0, mzbuf.at[lax.rem(z + d, NZ)], wc.at[z], device(dz=d)).start())
    wc[z] = mzbuf[z]
    mc[z] = mx[...]
    pass_on(3)
    lax.fori_loop(5, 8, prepare, 0)
    right_copy(3).wait_recv()
    arrived(PH_MZ, 0, wc.at[pl.ds(0, NZ - 1)])
    each(NZ, lambda d: remote(PH_MC, 0, mx, mc.at[z], device(dz=d)).start())

    columns16 = jnp.concatenate(
        [jnp.concatenate([wc[t, s] for t in range(NZ)], axis=0) for s in range(NX)], axis=0)
    flipped = jnp.transpose(columns16.astype(F32)).astype(BF16)
    for b in range(9):
        l = DEGREE[b]
        hs[b * 16:(b + 1) * 16, :] = dot(
            flipped[l * 16:(l + 1) * 16], a_ref[:, b].reshape(128, 512), NT).astype(BF16)

    g_acc[...] = jnp.zeros(g_acc.shape, F32)

    def edges(t, carry):
        hh[...] = dot(hs[...], oh[t])
        for q in range(NX):
            at = slice(q * 128, (q + 1) * 128)
            entries = entries_of(t, at)
            grads, inner, gate = [], None, None
            for opening, closing in SPANS:
                for i in range(opening, closing):
                    hidden = turned(entries, lambda b: hh[b * 16:(b + 1) * 16, at], opening, closing, i)
                    grad = grads_at[t, i * 16:(i + 1) * 16, at]
                    if i == 0:
                        gate = jax.nn.sigmoid(hidden)
                    inner = grad * hidden if inner is None else inner + grad * hidden
                    grads.append(grad * gate)
            grads[0] = grads[0] + inner * gate * (1.0 - gate)
            for opening, closing in SPANS:
                for b in range(opening, closing):
                    total = entries[opening, b] * grads[opening]
                    for i in range(opening + 1, closing):
                        total = total + entries[i, b] * grads[i]
                    u_ref[b * 16:(b + 1) * 16, at] = total.astype(BF16)
        g_acc[...] += dot(u_ref[...], oh[t], NT)
        return carry

    lax.fori_loop(0, NZ, edges, 0)

    sums = g_acc[...]
    narrow = sums.astype(BF16)
    sgt[48:128, :] = jnp.zeros((80, 512), F32)
    for l, (opening, closing) in enumerate(SPANS):
        total = jnp.zeros((16, 512), F32)
        for b in range(opening, closing):
            total = total + dot(narrow[b * 16:(b + 1) * 16], a_ref[:, b].reshape(128, 512))
        sgt[l * 16:(l + 1) * 16, :] = total
    tall = jnp.transpose(sgt[...]).astype(BF16)
    for t in range(NZ):
        for s in range(NX):
            first = s * 128 + t * 16
            sgbuf[t, s] = tall[first:first + 16]
    each(NZ, lambda d: remote(
        PH_SZ, 0, sgbuf.at[lax.rem(z + d, NZ)], sgrecv.at[z], device(dz=d)).start())
    sgrecv[z] = sgbuf[z]
    turned_sums = jnp.transpose(
        jnp.concatenate([sums, jnp.zeros((112, 128), F32)], axis=0)).astype(BF16)
    for t in range(NZ):
        gbuf[t] = turned_sums[t * 16:(t + 1) * 16]
    each(NZ, lambda d: remote(
        PH_GZ, 0, gbuf.at[lax.rem(z + d, NZ)], grecv.at[z], device(dz=d)).start())
    grecv[z] = gbuf[z]

    arrived(PH_SZ, 0, sgrecv.at[pl.ds(0, NZ - 1)])
    rows = dot(sgrecv[0].reshape(64, 128), unperm[0])
    for t in range(1, NZ):
        rows = rows + dot(sgrecv[t].reshape(64, 128), unperm[t])
    for s in range(NX):
        for l in range(3):
            sg4[s, l] = rows[s * 16:(s + 1) * 16, l * 128:(l + 1) * 128].astype(BF16)

    for k in (0, 4, 1, 3, 2):
        dy = NEAR[k]
        if dy:
            remote(PH_SYX, k, sg4.at[x], sgx.at[k, x], device(dy=dy)).start()
        else:
            sgx[k, x] = sg4[x]
        each(NX, lambda d: remote(
            PH_SYX, k, sg4.at[lax.rem(x + d, NX)], sgx.at[k, x], device(dy=dy, dx=d)).start())

    arrived(PH_GZ, 0, grecv.at[pl.ds(0, NZ - 1)])
    held = jnp.zeros((192, 128), F32)
    for t in range(NZ):
        wide = (dot(expand[...], grecv[t]) * same[...]).astype(BF16)
        held = held + dot(wide, fold[t])

    arrived(PH_SYX, 0, sgx.at[0])
    arrived(PH_SYX, 4, sgx.at[4])
    onward = ((0, 0, -2), (1, 4, 1), (2, 0, -1))
    for slot, k, hop in onward:
        remote(PH_FW, slot, sgx.at[k], forwarded.at[slot], device(dy=hop)).start()

    arrived(PH_MC, 0, mc.at[pl.ds(0, NZ - 1)])
    coefficient = split48(lax.broadcasted_iota(I32, (192, 128), 0))[1] >> 2
    parts = jnp.zeros((192, 512), F32)
    for l, (opening, closing) in enumerate(SPANS):
        inside = (coefficient >= opening) & (coefficient < closing)
        maps = jnp.concatenate(
            [jnp.concatenate([mc[t, s, l] for t in range(NZ)], axis=0) for s in range(NX)], axis=0)
        parts = parts + dot(jnp.where(inside, held, 0.0).astype(BF16), maps, NT)
    for s in range(NX):
        gxbuf[s] = parts[s * 48:(s + 1) * 48].astype(BF16)
    each(NX, lambda d: remote(
        PH_GX, 0, gxbuf.at[lax.rem(x + d, NX)], gxrecv.at[d], device(dx=d)).start())
    gxrecv[0] = gxbuf[x]
    for k in (1, 2, 3):
        arrived(PH_SYX, k, sgx.at[k] if NEAR[k] else sgx.at[k, pl.ds(0, NX - 1)])
    arrived(PH_GX, 0, gxrecv.at[pl.ds(0, NX - 1)])
    total = gxrecv[0].astype(F32)
    for s in range(1, NX):
        total = total + gxrecv[s].astype(F32)
    for b in range(9):
        ga_ref[b] = total[b * 4:b * 4 + 4]

    for slot in range(3):
        arrived(PH_FW, slot, forwarded.at[slot])

    def expert_sum(expert, s):
        total = None
        for k, dy in enumerate(NEAR):
            term = share(-dy, expert) * sgx[k, s].astype(F32)
            total = term if total is None else total + term
        for slot, dy in ((0, 4), (1, -3), (2, 3)):
            total = total + share(dy, expert) * forwarded[slot, s].astype(F32)
        return total

    for e in range(2):
        for s in range(NX):
            endbuf[e, s] = expert_sum(other_first + e, s).astype(BF16)
    end_copy = remote(PH_END, 0, endbuf, endrecv, device(other=True))
    end_copy.start()
    for e in range(2):
        for s in range(NX):
            ge_ref[e, :, :, s * 128:(s + 1) * 128] = expert_sum(own_first + e, s)
    end_copy.wait_recv()
    for e in range(2):
        for s in range(NX):
            ge_ref[e, :, :, s * 128:(s + 1) * 128] += endrecv[e, s].astype(F32)

    core_copy.wait_send()
    end_copy.wait_send()
    for s in range(4):
        right_copy(s).wait_send()
    for s in range(3):
        left_copy(s).wait_send()
    for slot in range(3):
        left(PH_Y, slot, ybuf.at[slot])
        left(PH_FW, slot, forwarded.at[slot])
    for k, dy in enumerate(NEAR):
        left(PH_YX, k, yxbuf.at[k] if dy else yxbuf.at[k, pl.ds(0, NX - 1)])
        left(PH_SYX, k, sg4 if dy else sg4.at[pl.ds(0, NX - 1)])
    left(PH_ATX, 0, atx.at[pl.ds(0, NX - 1)])
    left(PH_COX, 0, cox.at[pl.ds(0, NX - 1)])
    left(PH_GX, 0, gxbuf.at[pl.ds(0, NX - 1)])
    left(PH_COZ, 0, cobuf.at[pl.ds(0, NZ - 1)])
    left(PH_MZ, 0, mzbuf.at[pl.ds(0, NZ - 1)])
    left(PH_MC, 0, mc.at[pl.ds(0, NZ - 1)])
    left(PH_SZ, 0, sgbuf.at[pl.ds(0, NZ - 1)])
    left(PH_GZ, 0, gbuf.at[pl.ds(0, NZ - 1)])


def shards(
    atoms, cotangent, expert_weights, coefficients, src_owner, src_slot, tgt_slot, rot_index, rot_table
):
    hbm = pl.BlockSpec(memory_space=pltpu.HBM)
    vmem = pl.BlockSpec(memory_space=pltpu.VMEM)
    smem = pl.BlockSpec(memory_space=pltpu.SMEM)

    def b16(*shape):
        return pltpu.VMEM(shape, BF16)

    def f32(*shape):
        return pltpu.VMEM(shape, F32)

    grad_atoms, grad_experts = pl.pallas_call(
        kernel,
        out_shape=(
            jax.ShapeDtypeStruct((9, 4, 512), F32),
            jax.ShapeDtypeStruct((2, 3, 16, 512), F32),
        ),
        in_specs=[smem] + [hbm] * 8,
        out_specs=(vmem, vmem),
        scratch_shapes=[
            b16(2, 3, 16, 512),
            b16(2, 3, 16, 512),
            b16(9, 4, 512),
            b16(9, 4, 512),
            pltpu.VMEM((4, 1, 128), I32),
            f32(9, 9, 64),
            f32(40, 64),
            b16(3, NX, 3, 16, 128),
            b16(3, NX, 3, 16, 128),
            b16(5, NX, 3, 16, 128),
            b16(5, NX, 3, 16, 128),
            b16(NX, 3, 16, 128),
            b16(NZ, NX, 16, 128),
            b16(NZ, NX, 16, 128),
            b16(NZ, NX, 3, 16, 128),
            f32(1, 48, 512),
            b16(NX + 1, NX, 48, 128),
            b16(NZ, 9, 16, 512),
            f32(1, 48, 512),
            b16(2 * NX, 64, 128),
            b16(NZ, 6, 16, 128),
            b16(NZ, 6, 16, 128),
            b16(192, 16),
            b16(NZ, 256, 128),
            b16(NZ, 128, 256),
            b16(3, 128, 1024),
            b16(NZ, 128, 384),
            b16(144, 192),
            b16(16, 192),
            f32(192, 256),
            b16(40, 128),
            b16(144, 128),
            b16(144, 128),
            f32(144, 512),
            f32(144, 512),
            f32(NZ, 144, 512),
            f32(NZ, 40, 512),
            b16(NZ + 2, 128, 512),
            b16(144, 512),
            f32(144, 128),
            b16(NZ, 16, 256),
            b16(NZ, 16, 256),
            b16(NX, 48, 512),
            b16(NX, 48, 512),
            f32(128, 512),
            b16(NZ, NX, 16, 128),
            b16(NZ, NX, 16, 128),
            b16(NX, 3, 16, 128),
            b16(5, NX, 3, 16, 128),
            b16(3, NX, 3, 16, 128),
            b16(2, NX, 3, 16, 128),
            b16(2, NX, 3, 16, 128),
            pltpu.SemaphoreType.DMA((8,)),
            pltpu.SemaphoreType.DMA((16, 5)),
            pltpu.SemaphoreType.DMA((16, 5)),
        ],
        compiler_params=pltpu.CompilerParams(
            collective_id=0, has_side_effects=True, vmem_limit_bytes=60 * 1024 * 1024
        ),
        cost_estimate=pl.CostEstimate(
            flops=2_000_000_000, bytes_accessed=1_000_000, transcendentals=65536
        ),
    )(
        coefficients, expert_weights, atoms[0].transpose(1, 0, 2), cotangent[0].transpose(1, 0, 2),
        src_owner.reshape(1, -1), src_slot, tgt_slot, rot_index, rot_table.transpose(1, 2, 0),
    )
    return grad_atoms.transpose(1, 0, 2)[None], grad_experts


def solution(mesh):
    placed = (
        P("grp", "graph", None, None),
        P("grp", "graph", None, None),
        P("grp", None, "graph", None),
        P(),
        P("grp", "graph", None),
        P("grp", "graph"),
        P("grp", "graph"),
        P("grp", "graph"),
        P(),
    )
    return jax.shard_map(
        shards,
        mesh=mesh,
        in_specs=placed,
        out_specs=(P("grp", "graph", None, None), P("grp", None, "graph", None)),
        check_vma=False,
    )
```

```python
import jax
import jax.numpy as jnp
from jax import lax
from jax.experimental import pallas as pl
from jax.experimental.pallas import tpu as pltpu
from jax.sharding import PartitionSpec as P

F32, BF16, I32 = jnp.float32, jnp.bfloat16, jnp.int32
NX, NZ, NY = 4, 8, 8
SPANS = ((0, 1), (1, 4), (4, 9))
DEGREE = (0, 1, 1, 1, 2, 2, 2, 2, 2)
MESH = pl.DeviceIdType.MESH
NN = (((1,), (0,)), ((), ()))
NT = (((1,), (1,)), ((), ()))

(PH_CORE, PH_Y, PH_YX, PH_ATX, PH_ATR, PH_ATL, PH_COX, PH_COZ, PH_MZ, PH_MC,
 PH_GZ, PH_GX, PH_SZ, PH_SYX, PH_FW, PH_END, PH_MCL) = range(17)
NEAR = (-2, -1, 0, 1, 2)
ENTRY = {}
for _opening, _closing in SPANS:
    for _i in range(_opening, _closing):
        for _b in range(_opening, _closing):
            ENTRY[_i, _b] = len(ENTRY)


def dot(a, b, dims=NN):
    return lax.dot_general(a, b, dims, preferred_element_type=F32)


def one_hot(test):
    return jnp.where(test, 1.0, 0.0).astype(BF16)


def grid_of(rows, columns):
    shape = (rows, columns)
    return lax.broadcasted_iota(I32, shape, 0), lax.broadcasted_iota(I32, shape, 1)


def split48(index):
    block = jnp.where(index >= 48, 1, 0) + jnp.where(index >= 96, 1, 0) + jnp.where(index >= 144, 1, 0)
    return block, index - 48 * block


def kernel(
    coef, w_hbm, at_hbm, co_hbm, owner_hbm, slot_hbm, tslot_hbm, turn_hbm, rt_hbm,
    ga_ref, ge_ref,
    w_own, w_sib, at_in, co_in, index_in, rt_in, rt35,
    ybuf, yrecv, yxbuf, yxrecv, mx, mzbuf, wc, mc, maps16,
    at48, atx, a_ref, co80, cox, cobuf, corecv,
    expand, fold, spread, perm, unperm, order, gather16, same, rot2,
    hs, cs, hh, ch, grads_at, turns, oh, u_ref, g_acc, narrow, gbuf, grecv, gxbuf, gxrecv,
    sgt, sgbuf, sgrecv, sg4, sgx, forwarded, endbuf, endrecv,
    load_sem, send_sem, recv_sem,
):
    grp, graph = lax.axis_index("grp"), lax.axis_index("graph")
    y, core = lax.div(grp, 2), lax.rem(grp, 2)
    x, z = lax.div(graph, NZ), lax.rem(graph, NZ)

    def device(dy=None, dx=None, dz=None, other=False):
        along = y if dy is None else lax.rem(y + dy + NY, NY)
        across = x if dx is None else lax.rem(x + dx, NX)
        up = z if dz is None else lax.rem(z + dz, NZ)
        return {"grp": along * 2 + (1 - core if other else core), "graph": across * NZ + up}

    def remote(phase, slot, source, target, place):
        return pltpu.make_async_remote_copy(
            src_ref=source, dst_ref=target, send_sem=send_sem.at[phase, slot],
            recv_sem=recv_sem.at[phase, slot], device_id=place, device_id_type=MESH,
        )

    def each(count, body, first=1):
        def step(d, carry):
            body(d)
            return carry

        lax.fori_loop(first, count, step, 0)

    def lanes(k):
        return pl.ds(pl.multiple_of(k * 128, 128), 128)

    def arrived(phase, slot, ref):
        pltpu.make_async_copy(ref, ref, recv_sem.at[phase, slot]).wait()

    def left(phase, slot, ref):
        pltpu.make_async_copy(ref, ref, send_sem.at[phase, slot]).wait()

    loads = [
        pltpu.make_async_copy(source, target, load_sem.at[k])
        for k, (source, target) in enumerate((
            (w_hbm, w_own), (at_hbm, at_in), (co_hbm, co_in), (owner_hbm, index_in.at[0]),
            (slot_hbm, index_in.at[1]), (tslot_hbm, index_in.at[2]), (turn_hbm, index_in.at[3]),
            (rt_hbm, rt_in)))
    ]
    for load in loads:
        load.start()

    barrier = pltpu.get_barrier_semaphore()

    def greet(place):
        pl.semaphore_signal(barrier, inc=1, device_id=place, device_id_type=MESH)

    greet(device(other=True))
    each(5 * NX, lambda k: pl.when(k != 2 * NX)(
        lambda: greet(device(dy=lax.div(k, NX) - 2, dx=lax.rem(k, NX)))), 0)
    each(NZ, lambda d: greet(device(dz=d)))

    loads[0].wait()
    pl.semaphore_wait(barrier, 1 + 4 + 5 * (NX - 1) + (NZ - 1))
    core_copy = remote(PH_CORE, 0, w_own, w_sib, device(other=True))
    core_copy.start()

    loads[1].wait()
    for b in range(9):
        at48[0, b * 4:b * 4 + 4, :] = at_in[b].astype(F32)
    at48[0, 36:48, :] = jnp.zeros((12, 512), F32)
    for xb in range(NX):
        own_rows = at48[0, :, xb * 128:(xb + 1) * 128].astype(BF16)
        atx[NX, xb] = own_rows
        atx[x, xb] = own_rows
    each(NX, lambda d: remote(PH_ATX, 0, atx.at[NX], atx.at[x], device(dx=d)).start())

    core_copy.wait_recv()

    def share(dy, expert):
        return coef[lax.rem(y + dy + NY, NY) * 2 + core, expert].astype(F32) * (1.0 / 1024.0)

    own_first, other_first = grp * 2, (y * 2 + 1 - core) * 2

    def partial_of(dy, xb):
        at = lanes(xb)
        total = None
        for ref, first in ((w_own, own_first), (w_sib, other_first)):
            for e in range(2):
                term = share(dy, first + e) * ref[e, :, :, at].astype(F32)
                total = term if total is None else total + term
        return total

    halves = (pl.ds(0, 2), pl.ds(2, 2))
    def fill_y(k):
        slot = lax.div(k, NX)
        dy = jnp.where(slot == 0, -4, jnp.where(slot == 1, 3, -3))
        ybuf[slot, lax.rem(k, NX)] = partial_of(dy, lax.rem(k, NX)).astype(BF16)

    each(3 * NX, fill_y, 0)
    for h in range(2):
        remote(PH_Y, 3 * h, ybuf.at[0, halves[h]], yrecv.at[0, halves[h]], device(dy=(-2, 2)[h])).start()
    for slot, hop in ((1, 1), (2, -1)):
        remote(PH_Y, slot, ybuf.at[slot], yrecv.at[slot], device(dy=hop)).start()

    def yx_send(k, source, target, phase):
        dy = k - 2

        def piece(d):
            to = lax.rem(x + d, NX)

            @pl.when((k != 2) | (d != 0))
            def _():
                remote(phase, k, source(k, to), target.at[k, x], device(dy=dy, dx=d)).start()

        each(NX, piece, 0)

    def near_block(k):
        def fill(xb):
            yxbuf[k, xb] = partial_of(k - 2, xb).astype(BF16)

        each(NX, fill, 0)
        yx_send(k, lambda slot, to: yxbuf.at[slot, to], yxrecv, PH_YX)

    each(4, near_block, 1)
    yxrecv[2, x] = yxbuf[2, x]

    for load in loads[2:]:
        load.wait()
    for b in range(9):
        co80[0, b * 4:b * 4 + 4, :] = co_in[b].astype(F32)
    co80[0, 36:48, :] = jnp.zeros((12, 512), F32)

    def place(owner, slot):
        return (owner & 7) * 16 + (owner >> 3) * 4 + slot

    row = lax.broadcasted_iota(I32, (16, 128), 0)
    codes = jnp.where(row == 0, place(index_in[0], index_in[1]), 0)
    codes = jnp.where(row == 1, place(graph, index_in[2]), codes)
    codes = jnp.where(row == 2, index_in[3], codes).astype(F32).astype(BF16)
    for xb in range(NX):
        cox[NX + xb, 0:48, :] = co80[0, :, xb * 128:(xb + 1) * 128].astype(BF16)
        cox[NX + xb, 48:64, :] = codes
    each(NX, lambda d: remote(
        PH_COX, 0, cox.at[NX + lax.rem(x + d, NX)], cox.at[x], device(dx=d)).start())
    cox[x] = cox[NX + x]

    row, column = grid_of(144, 192)
    block, within = split48(column)
    order[...] = one_hot(
        ((within >> 2) == (row >> 4)) & (((row >> 2) & 3) == block) & ((within & 3) == (row & 3)))

    arrived(PH_ATX, 0, atx.at[pl.ds(0, NX - 1)])
    for xb in range(NX):
        stacked = jnp.concatenate([atx[s, xb] for s in range(NX)], axis=0)
        a_ref[z, :, :, xb * 128:(xb + 1) * 128] = dot(order[...], stacked).astype(BF16).reshape(9, 16, 128)

    row, column = grid_of(16, 192)
    block, within = split48(column)
    gather16[...] = one_hot(row == block * 4 + (within & 3))
    row, column = grid_of(192, 16)
    block, within = split48(row)
    expand[...] = one_hot(column == block * 4 + (within & 3))
    row, column = grid_of(192, 256)
    block, within = split48(row)
    same[...] = jnp.where((within >> 2) == (column >> 4), 1.0, 0.0)

    def selections(t):
        row, column = grid_of(128, 256)
        spread[t] = one_hot(((row >> 4) == t) & ((row & 15) == (column & 15)))
        row, column = grid_of(256, 128)
        fold[t] = one_hot(((column >> 4) == t) & ((row & 15) == (column & 15)))
        row, column = grid_of(128, 128)
        same16 = (row & 15) == (column & 15)

        def pair(k):
            mark = jnp.where(k >= 3, k + 1, k)
            perm[k, :, lanes(t)] = one_hot(((row >> 4) == t) & ((column >> 4) == mark) & same16)
            unperm[t, :, lanes(k)] = one_hot(((column >> 4) == t) & ((row >> 4) == mark) & same16)

        each(6, pair, 0)

    each(NZ, selections, 0)

    def right_copy(s):
        slot = lax.rem(z - s + NZ, NZ)
        return remote(PH_ATR, s, a_ref.at[slot], a_ref.at[slot], device(dz=1))

    def left_copy(s):
        slot = lax.rem(z + s, NZ)
        return remote(PH_ATL, s, a_ref.at[slot], a_ref.at[slot], device(dz=NZ - 1))

    arrived(PH_COX, 0, cox.at[pl.ds(0, NX - 1)])
    stacked = jnp.concatenate([cox[s, 0:48] for s in range(NX)], axis=0)

    def pack_cotangent(t):
        wide = (dot(stacked, spread[t]) * same[...]).astype(BF16)
        packed = dot(gather16[...], wide).astype(BF16)
        cobuf[t, 0] = packed[:, 0:128]
        cobuf[t, 1] = packed[:, 128:256]
        for s in range(NX):
            cobuf[t, 2 + s] = cox[s, 48:64]

    each(NZ, pack_cotangent, 0)
    each(NZ, lambda d: remote(
        PH_COZ, 0, cobuf.at[lax.rem(z + d, NZ)], corecv.at[z], device(dz=d)).start())
    corecv[z] = cobuf[z]
    right_copy(0).start()
    left_copy(0).start()

    for h in range(2):
        arrived(PH_Y, 3 * h, yrecv.at[0, halves[h]])
    for slot in (1, 2):
        arrived(PH_Y, slot, yrecv.at[slot])

    def far_block(h):
        k = 4 * h

        def fill(xb):
            total = partial_of(k - 2, xb) + yrecv[2 - h, xb].astype(F32)
            through = jnp.where(lax.div(xb, 2) == h, 1.0, 0.0)
            yxbuf[k, xb] = (total + through * yrecv[0, xb].astype(F32)).astype(BF16)

        each(NX, fill, 0)
        yx_send(k, lambda slot, to: yxbuf.at[slot, to], yxrecv, PH_YX)

    each(2, far_block, 0)

    for i in range(9):
        opening, closing = SPANS[DEGREE[i]]
        first = ENTRY[i, opening]
        rt35[first:first + closing - opening, :] = rt_in[i, opening:closing, :]
    rt35[35:40, :] = jnp.zeros((5, 64), F32)
    table = rt35[...]
    high = table.astype(BF16)
    rot2[:, 0:64] = high
    rot2[:, 64:128] = (table - high.astype(F32)).astype(BF16)

    arrived(PH_COZ, 0, corecv.at[pl.ds(0, NZ - 1)])
    for half in range(2):
        tall = jnp.transpose(corecv[:, half].reshape(128, 128).astype(F32)).astype(BF16)
        rows = 128 if half == 0 else 16
        cs[half * 128:half * 128 + rows, :] = tall[0:rows]

    def turned(entries, values, opening, closing, i):
        total = entries[i, opening] * values(opening)
        for b in range(opening + 1, closing):
            total = total + entries[i, b] * values(b)
        return total

    def entries_of(t, at):
        return {key: turns[t, k:k + 1, at] for key, k in ENTRY.items()}

    def prepare(t):
        def places(q):
            at = lanes(q)
            row = lax.broadcasted_iota(I32, (128, 128), 0)
            codes = corecv[t, 2 + q].astype(F32)
            oh[t, :, at] = one_hot(row.astype(F32) == codes[0:1])
            oh[NZ, :, at] = one_hot(row.astype(F32) == codes[1:2])
            oh[NZ + 1, :, at] = one_hot((row & 63).astype(F32) == codes[2:3])

        def messages(q):
            at = lanes(q)
            entries = entries_of(t, at)
            for opening, closing in SPANS:
                for i in range(opening, closing):
                    grads_at[t, i * 16:(i + 1) * 16, at] = turned(
                        entries, lambda b: ch[b * 16:(b + 1) * 16, at], opening, closing, i)

        each(NX, places, 0)
        ch[...] = dot(cs[...], oh[NZ])
        turns[t] = dot(rot2[...], oh[NZ + 1])
        each(NX, messages, 0)

    def pass_on(right, left_way, s):
        right(s - 1).wait_recv()
        right(s).start()
        left_way(s - 1).wait_recv()

        @pl.when(s < 3)
        def _():
            left_way(s).start()

    def prepare_and_pass(t):
        @pl.when((lax.rem(t, 2) == 0) & (t < 6))
        def _():
            pass_on(right_copy, left_copy, lax.div(t, 2) + 1)

        prepare(t)

    each(4, prepare_and_pass, 0)

    for k, dy in enumerate(NEAR):
        arrived(PH_YX, k, yxrecv.at[k] if dy else yxrecv.at[k, pl.ds(0, NX - 1)])

    def mix(k):
        s, l = lax.div(k, 3), lax.rem(k, 3)
        total = yxrecv[0, s, l].astype(F32)
        for near in range(1, 5):
            total = total + yxrecv[near, s, l].astype(F32)
        mx[s, l] = total.astype(BF16)

    each(3 * NX, mix, 0)

    def pack_maps(k, total):
        h, l = lax.div(k, 3), lax.rem(k, 3)
        return total + dot(mx[pl.ds(2 * h, 2), l].reshape(32, 128), perm[k])

    packed = lax.fori_loop(0, 6, pack_maps, jnp.zeros((32, 1024), F32))
    packed = packed.astype(BF16)
    for t in range(NZ):
        mzbuf[t] = packed[:, t * 128:(t + 1) * 128].reshape(2, 16, 128)
    each(NZ, lambda d: remote(
        PH_MZ, 0, mzbuf.at[lax.rem(z + d, NZ)], wc.at[z], device(dz=d)).start())
    wc[z] = mzbuf[z]
    mc[z] = mx[...]
    each(8, prepare_and_pass, 4)
    right_copy(3).wait_recv()
    arrived(PH_MZ, 0, wc.at[pl.ds(0, NZ - 1)])

    def maps_right(s):
        slot = lax.rem(z - s + NZ, NZ)
        return remote(PH_MC, s, mc.at[slot], mc.at[slot], device(dz=1))

    def maps_left(s):
        slot = lax.rem(z + s, NZ)
        return remote(PH_MCL, s, mc.at[slot], mc.at[slot], device(dz=NZ - 1))

    maps_right(0).start()
    maps_left(0).start()

    columns16 = jnp.concatenate(
        [jnp.concatenate([wc[t, s] for t in range(NZ)], axis=0) for s in range(2)], axis=0)
    flipped = jnp.transpose(columns16.astype(F32)).astype(BF16)
    for l in range(3):
        for h in range(2):
            first = h * 64 + l * 16
            maps16[l, :, h * 256:(h + 1) * 256] = flipped[first:first + 16]

    def degree_of(b):
        return jnp.where(b >= 1, 1, 0) + jnp.where(b >= 4, 1, 0)

    def rows16(b):
        return pl.ds(pl.multiple_of(b * 16, 16), 16)

    def atom_maps(b):
        hs[rows16(b), :] = dot(maps16[degree_of(b)], a_ref[:, b].reshape(128, 512), NT).astype(BF16)

    each(9, atom_maps, 0)

    g_acc[...] = jnp.zeros(g_acc.shape, F32)

    def edges(t):
        hh[...] = dot(hs[...], oh[t])

        def group(q):
            at = lanes(q)
            entries = entries_of(t, at)
            grads, inner, gate = [], None, None
            for opening, closing in SPANS:
                for i in range(opening, closing):
                    hidden = turned(entries, lambda b: hh[b * 16:(b + 1) * 16, at], opening, closing, i)
                    grad = grads_at[t, i * 16:(i + 1) * 16, at]
                    if i == 0:
                        gate = jax.nn.sigmoid(hidden)
                    inner = grad * hidden if inner is None else inner + grad * hidden
                    grads.append(grad * gate)
            grads[0] = grads[0] + inner * gate * (1.0 - gate)
            for opening, closing in SPANS:
                for b in range(opening, closing):
                    total = entries[opening, b] * grads[opening]
                    for i in range(opening + 1, closing):
                        total = total + entries[i, b] * grads[i]
                    u_ref[b * 16:(b + 1) * 16, at] = total.astype(BF16)

        each(NX, group, 0)
        g_acc[...] += dot(u_ref[...], oh[t], NT)

        @pl.when((lax.rem(t, 2) == 1) & (t < 6))
        def _():
            pass_on(maps_right, maps_left, lax.div(t + 1, 2))

    each(NZ, edges, 0)

    sums = g_acc[...]
    narrow[...] = sums.astype(BF16)
    for h in range(2):
        sgt[h * 64 + 48:h * 64 + 64, :] = jnp.zeros((16, 256), F32)
    for l, (opening, closing) in enumerate(SPANS):
        total = lax.fori_loop(
            opening, closing,
            lambda b, total: total + dot(narrow[rows16(b), :], a_ref[:, b].reshape(128, 512)),
            jnp.zeros((16, 512), F32))
        for h in range(2):
            sgt[h * 64 + l * 16:h * 64 + (l + 1) * 16, :] = total[:, h * 256:(h + 1) * 256]
    tall = jnp.transpose(sgt[...]).astype(BF16)
    for t in range(NZ):
        for s in range(2):
            first = s * 128 + t * 16
            sgbuf[t, s] = tall[first:first + 16]
    each(NZ, lambda d: remote(
        PH_SZ, 0, sgbuf.at[lax.rem(z + d, NZ)], sgrecv.at[z], device(dz=d)).start())
    sgrecv[z] = sgbuf[z]
    turned_sums = jnp.transpose(
        jnp.concatenate([sums, jnp.zeros((112, 128), F32)], axis=0)).astype(BF16)
    for t in range(NZ):
        gbuf[t] = turned_sums[t * 16:(t + 1) * 16]
    each(NZ, lambda d: remote(
        PH_GZ, 0, gbuf.at[lax.rem(z + d, NZ)], grecv.at[z], device(dz=d)).start())
    grecv[z] = gbuf[z]

    arrived(PH_SZ, 0, sgrecv.at[pl.ds(0, NZ - 1)])
    rows = lax.fori_loop(
        0, NZ, lambda t, total: total + dot(sgrecv[t].reshape(32, 128), unperm[t]),
        jnp.zeros((32, 768), F32))
    for s in range(NX):
        for l in range(3):
            at = (s // 2 * 3 + l) * 128
            sg4[s, l] = rows[s % 2 * 16:s % 2 * 16 + 16, at:at + 128].astype(BF16)

    each(5, lambda k: yx_send(k, lambda slot, to: sg4.at[to], sgx, PH_SYX), 0)
    sgx[2, x] = sg4[x]

    arrived(PH_GZ, 0, grecv.at[pl.ds(0, NZ - 1)])

    def unpack(t, total):
        wide = (dot(expand[...], grecv[t]) * same[...]).astype(BF16)
        return total + dot(wide, fold[t])

    held = lax.fori_loop(0, NZ, unpack, jnp.zeros((192, 128), F32))

    arrived(PH_SYX, 0, sgx.at[0])
    arrived(PH_SYX, 4, sgx.at[4])
    for h, k, hop in ((0, 0, -2), (1, 4, 2)):
        remote(PH_FW, 3 * h, sgx.at[k, halves[h]], forwarded.at[0, halves[h]], device(dy=hop)).start()
    for slot, k, hop in ((1, 4, 1), (2, 0, -1)):
        remote(PH_FW, slot, sgx.at[k], forwarded.at[slot], device(dy=hop)).start()

    maps_right(3).wait_recv()
    coefficient = split48(lax.broadcasted_iota(I32, (192, 128), 0))[1] >> 2
    parts = jnp.zeros((192, 512), F32)
    for l, (opening, closing) in enumerate(SPANS):
        inside = (coefficient >= opening) & (coefficient < closing)
        maps = jnp.concatenate(
            [jnp.concatenate([mc[t, s, l] for t in range(NZ)], axis=0) for s in range(NX)], axis=0)
        parts = parts + dot(jnp.where(inside, held, 0.0).astype(BF16), maps, NT)
    for s in range(NX):
        gxbuf[s] = parts[s * 48:(s + 1) * 48].astype(BF16)
    each(NX, lambda d: remote(
        PH_GX, 0, gxbuf.at[lax.rem(x + d, NX)], gxrecv.at[d], device(dx=d)).start())
    gxrecv[0] = gxbuf[x]
    for k in (1, 2, 3):
        arrived(PH_SYX, k, sgx.at[k] if NEAR[k] else sgx.at[k, pl.ds(0, NX - 1)])
    arrived(PH_GX, 0, gxrecv.at[pl.ds(0, NX - 1)])
    total = gxrecv[0].astype(F32)
    for s in range(1, NX):
        total = total + gxrecv[s].astype(F32)
    for b in range(9):
        ga_ref[b] = total[b * 4:b * 4 + 4]

    for h in range(2):
        arrived(PH_FW, 3 * h, forwarded.at[0, halves[h]])
    for slot in (1, 2):
        arrived(PH_FW, slot, forwarded.at[slot])

    def expert_sum(expert, s):
        total = None
        for k, dy in enumerate(NEAR):
            term = share(-dy, expert) * sgx[k, s].astype(F32)
            total = term if total is None else total + term
        for slot, dy in ((0, 4), (1, -3), (2, 3)):
            total = total + share(dy, expert) * forwarded[slot, s].astype(F32)
        return total

    def other_half(k):
        e, s = lax.div(k, NX), lax.rem(k, NX)
        endbuf[e, s] = expert_sum(other_first + e, s).astype(BF16)

    def own_half(k):
        e, s = lax.div(k, NX), lax.rem(k, NX)
        ge_ref[e, :, :, lanes(s)] = expert_sum(own_first + e, s)

    def both_halves(k):
        e, s = lax.div(k, NX), lax.rem(k, NX)
        ge_ref[e, :, :, lanes(s)] += endrecv[e, s].astype(F32)

    each(2 * NX, other_half, 0)
    end_copy = remote(PH_END, 0, endbuf, endrecv, device(other=True))
    end_copy.start()
    each(2 * NX, own_half, 0)
    end_copy.wait_recv()
    each(2 * NX, both_halves, 0)

    core_copy.wait_send()
    end_copy.wait_send()
    for s in range(4):
        right_copy(s).wait_send()
        maps_right(s).wait_send()
    for s in range(3):
        left_copy(s).wait_send()
        maps_left(s).wait_send()
    for phase, ref in ((PH_Y, ybuf), (PH_FW, forwarded)):
        for h in range(2):
            left(phase, 3 * h, ref.at[0, halves[h]])
        for slot in (1, 2):
            left(phase, slot, ref.at[slot])
    for k, dy in enumerate(NEAR):
        left(PH_YX, k, yxbuf.at[k] if dy else yxbuf.at[k, pl.ds(0, NX - 1)])
        left(PH_SYX, k, sg4 if dy else sg4.at[pl.ds(0, NX - 1)])
    left(PH_ATX, 0, atx.at[pl.ds(0, NX - 1)])
    left(PH_COX, 0, cox.at[pl.ds(0, NX - 1)])
    left(PH_GX, 0, gxbuf.at[pl.ds(0, NX - 1)])
    left(PH_COZ, 0, cobuf.at[pl.ds(0, NZ - 1)])
    left(PH_MZ, 0, mzbuf.at[pl.ds(0, NZ - 1)])
    left(PH_SZ, 0, sgbuf.at[pl.ds(0, NZ - 1)])
    left(PH_GZ, 0, gbuf.at[pl.ds(0, NZ - 1)])


def shards(
    atoms, cotangent, expert_weights, coefficients, src_owner, src_slot, tgt_slot, rot_index, rot_table
):
    hbm = pl.BlockSpec(memory_space=pltpu.HBM)
    vmem = pl.BlockSpec(memory_space=pltpu.VMEM)
    smem = pl.BlockSpec(memory_space=pltpu.SMEM)

    def b16(*shape):
        return pltpu.VMEM(shape, BF16)

    def f32(*shape):
        return pltpu.VMEM(shape, F32)

    grad_atoms, grad_experts = pl.pallas_call(
        kernel,
        out_shape=(
            jax.ShapeDtypeStruct((9, 4, 512), F32),
            jax.ShapeDtypeStruct((2, 3, 16, 512), F32),
        ),
        in_specs=[smem] + [hbm] * 8,
        out_specs=(vmem, vmem),
        scratch_shapes=[
            b16(2, 3, 16, 512),
            b16(2, 3, 16, 512),
            b16(9, 4, 512),
            b16(9, 4, 512),
            pltpu.VMEM((4, 1, 128), I32),
            f32(9, 9, 64),
            f32(40, 64),
            b16(3, NX, 3, 16, 128),
            b16(3, NX, 3, 16, 128),
            b16(5, NX, 3, 16, 128),
            b16(5, NX, 3, 16, 128),
            b16(NX, 3, 16, 128),
            b16(NZ, 2, 16, 128),
            b16(NZ, 2, 16, 128),
            b16(NZ, NX, 3, 16, 128),
            b16(3, 16, 512),
            f32(1, 48, 512),
            b16(NX + 1, NX, 48, 128),
            b16(NZ, 9, 16, 512),
            f32(1, 48, 512),
            b16(2 * NX, 64, 128),
            b16(NZ, 6, 16, 128),
            b16(NZ, 6, 16, 128),
            b16(192, 16),
            b16(NZ, 256, 128),
            b16(NZ, 128, 256),
            b16(6, 128, 1024),
            b16(NZ, 128, 768),
            b16(144, 192),
            b16(16, 192),
            f32(192, 256),
            b16(40, 128),
            b16(144, 128),
            b16(144, 128),
            f32(144, 512),
            f32(144, 512),
            f32(NZ, 144, 512),
            f32(NZ, 40, 512),
            b16(NZ + 2, 128, 512),
            b16(144, 512),
            f32(144, 128),
            b16(144, 128),
            b16(NZ, 16, 256),
            b16(NZ, 16, 256),
            b16(NX, 48, 512),
            b16(NX, 48, 512),
            f32(128, 256),
            b16(NZ, 2, 16, 128),
            b16(NZ, 2, 16, 128),
            b16(NX, 3, 16, 128),
            b16(5, NX, 3, 16, 128),
            b16(3, NX, 3, 16, 128),
            b16(2, NX, 3, 16, 128),
            b16(2, NX, 3, 16, 128),
            pltpu.SemaphoreType.DMA((8,)),
            pltpu.SemaphoreType.DMA((17, 5)),
            pltpu.SemaphoreType.DMA((17, 5)),
        ],
        compiler_params=pltpu.CompilerParams(
            collective_id=0, has_side_effects=True, vmem_limit_bytes=60 * 1024 * 1024
        ),
        cost_estimate=pl.CostEstimate(
            flops=2_000_000_000, bytes_accessed=1_000_000, transcendentals=65536
        ),
    )(
        coefficients, expert_weights, atoms[0].transpose(1, 0, 2), cotangent[0].transpose(1, 0, 2),
        src_owner.reshape(1, -1), src_slot, tgt_slot, rot_index, rot_table.transpose(1, 2, 0),
    )
    return grad_atoms.transpose(1, 0, 2)[None], grad_experts


def solution(mesh):
    placed = (
        P("grp", "graph", None, None),
        P("grp", "graph", None, None),
        P("grp", None, "graph", None),
        P(),
        P("grp", "graph", None),
        P("grp", "graph"),
        P("grp", "graph"),
        P("grp", "graph"),
        P(),
    )
    return jax.shard_map(
        shards,
        mesh=mesh,
        in_specs=placed,
        out_specs=(P("grp", "graph", None, None), P("grp", None, "graph", None)),
        check_vma=False,
    )
```

```python
import jax
import jax.numpy as jnp
from jax import lax
from jax.experimental import pallas as pl
from jax.experimental.pallas import tpu as pltpu
from jax.sharding import PartitionSpec as P

F32, BF16, I32 = jnp.float32, jnp.bfloat16, jnp.int32
NX, NZ, NY = 4, 8, 8
SPANS = ((0, 1), (1, 4), (4, 9))
DEGREE = (0, 1, 1, 1, 2, 2, 2, 2, 2)
MESH = pl.DeviceIdType.MESH
NN = (((1,), (0,)), ((), ()))
NT = (((1,), (1,)), ((), ()))

(PH_CORE, PH_Y, PH_YX, PH_ATX, PH_ATR, PH_ATL, PH_COX, PH_COZ, PH_MZ, PH_MC,
 PH_GZ, PH_GX, PH_SZ, PH_SYX, PH_FW, PH_END, PH_MCL) = range(17)
NEAR = (-2, -1, 0, 1, 2)
ENTRY = {}
for _opening, _closing in SPANS:
    for _i in range(_opening, _closing):
        for _b in range(_opening, _closing):
            ENTRY[_i, _b] = len(ENTRY)


def dot(a, b, dims=NN):
    return lax.dot_general(a, b, dims, preferred_element_type=F32)


def one_hot(test):
    return jnp.where(test, 1.0, 0.0).astype(BF16)


def grid_of(rows, columns):
    shape = (rows, columns)
    return lax.broadcasted_iota(I32, shape, 0), lax.broadcasted_iota(I32, shape, 1)


def split48(index):
    block = jnp.where(index >= 48, 1, 0) + jnp.where(index >= 96, 1, 0) + jnp.where(index >= 144, 1, 0)
    return block, index - 48 * block


def kernel(
    coef, w_hbm, at_hbm, co_hbm, owner_hbm, slot_hbm, tslot_hbm, turn_hbm, rt_hbm,
    ga_ref, ge_ref,
    w_own, w_sib, at_in, co_in, index_in, rt_in, rt35,
    ybuf, yrecv, yxbuf, yxrecv, mx, mzbuf, wc, mc,
    at48, atx, a_ref, co80, cox, cobuf, corecv,
    expand, fold, spread, perm, unperm, order, gather16, same, rot2,
    hs, cs, hh, ch, grads_at, turns, oh, u_ref, g_acc, gbuf, grecv, gxbuf, gxrecv,
    sgt, sgbuf, sgrecv, sg4, sgx, forwarded, endbuf, endrecv,
    load_sem, send_sem, recv_sem,
):
    grp, graph = lax.axis_index("grp"), lax.axis_index("graph")
    y, core = lax.div(grp, 2), lax.rem(grp, 2)
    x, z = lax.div(graph, NZ), lax.rem(graph, NZ)

    def device(dy=None, dx=None, dz=None, other=False):
        along = y if dy is None else lax.rem(y + dy + NY, NY)
        across = x if dx is None else lax.rem(x + dx, NX)
        up = z if dz is None else lax.rem(z + dz, NZ)
        return {"grp": along * 2 + (1 - core if other else core), "graph": across * NZ + up}

    def remote(phase, slot, source, target, place):
        return pltpu.make_async_remote_copy(
            src_ref=source, dst_ref=target, send_sem=send_sem.at[phase, slot],
            recv_sem=recv_sem.at[phase, slot], device_id=place, device_id_type=MESH,
        )

    def each(count, body):
        def step(d, carry):
            body(d)
            return carry

        lax.fori_loop(1, count, step, 0)

    def arrived(phase, slot, ref):
        pltpu.make_async_copy(ref, ref, recv_sem.at[phase, slot]).wait()

    def left(phase, slot, ref):
        pltpu.make_async_copy(ref, ref, send_sem.at[phase, slot]).wait()

    loads = [
        pltpu.make_async_copy(source, target, load_sem.at[k])
        for k, (source, target) in enumerate((
            (w_hbm, w_own), (at_hbm, at_in), (co_hbm, co_in), (owner_hbm, index_in.at[0]),
            (slot_hbm, index_in.at[1]), (tslot_hbm, index_in.at[2]), (turn_hbm, index_in.at[3]),
            (rt_hbm, rt_in)))
    ]
    for load in loads:
        load.start()

    barrier = pltpu.get_barrier_semaphore()

    def greet(place):
        pl.semaphore_signal(barrier, inc=1, device_id=place, device_id_type=MESH)

    greet(device(other=True))
    for dy in NEAR:
        if dy:
            greet(device(dy=dy))
        each(NX, lambda d: greet(device(dy=dy, dx=d)))
    each(NZ, lambda d: greet(device(dz=d)))

    row, column = grid_of(144, 192)
    block, within = split48(column)
    order[...] = one_hot(
        ((within >> 2) == (row >> 4)) & (((row >> 2) & 3) == block) & ((within & 3) == (row & 3)))
    row, column = grid_of(16, 192)
    block, within = split48(column)
    gather16[...] = one_hot(row == block * 4 + (within & 3))
    row, column = grid_of(192, 16)
    block, within = split48(row)
    expand[...] = one_hot(column == block * 4 + (within & 3))
    row, column = grid_of(192, 256)
    block, within = split48(row)
    same[...] = jnp.where((within >> 2) == (column >> 4), 1.0, 0.0)
    for t in range(NZ):
        row, column = grid_of(128, 256)
        spread[t] = one_hot(((row >> 4) == t) & ((row & 15) == (column & 15)))
        row, column = grid_of(256, 128)
        fold[t] = one_hot(((column >> 4) == t) & ((row & 15) == (column & 15)))
        row, column = grid_of(128, 128)
        same16 = (row & 15) == (column & 15)
        for h in range(2):
            for l in range(3):
                perm[l, h, :, t * 128:(t + 1) * 128] = one_hot(
                    ((row >> 4) == t) & ((column >> 4) == h * 4 + l) & same16)
                unperm[t, :, (h * 3 + l) * 128:(h * 3 + l + 1) * 128] = one_hot(
                    ((column >> 4) == t) & ((row >> 4) == h * 4 + l) & same16)

    for load in loads:
        load.wait()

    for b in range(9):
        co80[0, b * 4:b * 4 + 4, :] = co_in[b].astype(F32)
        at48[0, b * 4:b * 4 + 4, :] = at_in[b].astype(F32)
    at48[0, 36:48, :] = jnp.zeros((12, 512), F32)
    co80[0, 36:48, :] = jnp.zeros((12, 512), F32)

    def place(owner, slot):
        return (owner & 7) * 16 + (owner >> 3) * 4 + slot

    row = lax.broadcasted_iota(I32, (16, 128), 0)
    codes = jnp.where(row == 0, place(index_in[0], index_in[1]), 0)
    codes = jnp.where(row == 1, place(graph, index_in[2]), codes)
    codes = jnp.where(row == 2, index_in[3], codes).astype(F32).astype(BF16)
    for xb in range(NX):
        at = slice(xb * 128, (xb + 1) * 128)
        atx_out = at48[0, :, at].astype(BF16)
        cox_out = co80[0, :, at].astype(BF16)
        atx[NX, xb] = atx_out
        cox[NX + xb, 0:48, :] = cox_out
        cox[NX + xb, 48:64, :] = codes

    pl.semaphore_wait(barrier, 1 + 4 + 5 * (NX - 1) + (NZ - 1))

    core_copy = remote(PH_CORE, 0, w_own, w_sib, device(other=True))
    core_copy.start()
    each(NX, lambda d: remote(PH_ATX, 0, atx.at[NX], atx.at[x], device(dx=d)).start())
    each(NX, lambda d: remote(
        PH_COX, 0, cox.at[NX + lax.rem(x + d, NX)], cox.at[x], device(dx=d)).start())
    atx[x] = atx[NX]
    cox[x] = cox[NX + x]

    core_copy.wait_recv()

    def share(dy, expert):
        return coef[lax.rem(y + dy + NY, NY) * 2 + core, expert].astype(F32) * (1.0 / 1024.0)

    own_first, other_first = grp * 2, (y * 2 + 1 - core) * 2

    def partial_of(dy, xb):
        at = slice(xb * 128, (xb + 1) * 128)
        total = None
        for ref, first in ((w_own, own_first), (w_sib, other_first)):
            for e in range(2):
                term = share(dy, first + e) * ref[e, :, :, at].astype(F32)
                total = term if total is None else total + term
        return total

    halves = (pl.ds(0, 2), pl.ds(2, 2))
    for xb in range(NX):
        ybuf[0, xb] = partial_of(-4, xb).astype(BF16)
        if xb % 2:
            h = xb // 2
            remote(PH_Y, 3 * h, ybuf.at[0, halves[h]], yrecv.at[0, halves[h]],
                   device(dy=(-2, 2)[h])).start()
    for slot, dy, hop in ((1, 3, 1), (2, -3, -1)):
        for xb in range(NX):
            ybuf[slot, xb] = partial_of(dy, xb).astype(BF16)
        remote(PH_Y, slot, ybuf.at[slot], yrecv.at[slot], device(dy=hop)).start()

    def yx_send(k):
        dy = NEAR[k]
        if dy:
            remote(PH_YX, k, yxbuf.at[k, x], yxrecv.at[k, x], device(dy=dy)).start()
        else:
            yxrecv[k, x] = yxbuf[k, x]
        each(NX, lambda d: remote(
            PH_YX, k, yxbuf.at[k, lax.rem(x + d, NX)], yxrecv.at[k, x], device(dy=dy, dx=d)).start())

    for k in (1, 3, 2):
        for xb in range(NX):
            yxbuf[k, xb] = partial_of(NEAR[k], xb).astype(BF16)
        yx_send(k)

    arrived(PH_ATX, 0, atx.at[pl.ds(0, NX - 1)])
    for xb in range(NX):
        stacked = jnp.concatenate([atx[s, xb] for s in range(NX)], axis=0)
        a_ref[z, :, :, xb * 128:(xb + 1) * 128] = dot(order[...], stacked).astype(BF16).reshape(9, 16, 128)

    def right_copy(s):
        slot = lax.rem(z - s + NZ, NZ)
        return remote(PH_ATR, s, a_ref.at[slot], a_ref.at[slot], device(dz=1))

    def left_copy(s):
        slot = lax.rem(z + s, NZ)
        return remote(PH_ATL, s, a_ref.at[slot], a_ref.at[slot], device(dz=NZ - 1))

    arrived(PH_COX, 0, cox.at[pl.ds(0, NX - 1)])
    stacked = jnp.concatenate([cox[s, 0:48] for s in range(NX)], axis=0)
    for t in range(NZ):
        wide = (dot(stacked, spread[t]) * same[...]).astype(BF16)
        packed = dot(gather16[...], wide).astype(BF16)
        cobuf[t, 0] = packed[:, 0:128]
        cobuf[t, 1] = packed[:, 128:256]
        for s in range(NX):
            cobuf[t, 2 + s] = cox[s, 48:64]
    each(NZ, lambda d: remote(
        PH_COZ, 0, cobuf.at[lax.rem(z + d, NZ)], corecv.at[z], device(dz=d)).start())
    corecv[z] = cobuf[z]
    right_copy(0).start()
    left_copy(0).start()

    for h in range(2):
        arrived(PH_Y, 3 * h, yrecv.at[0, halves[h]])
    for slot in (1, 2):
        arrived(PH_Y, slot, yrecv.at[slot])
    for k, dy, slot in ((0, -2, 2), (4, 2, 1)):
        for xb in range(NX):
            total = partial_of(dy, xb) + yrecv[slot, xb].astype(F32)
            if (xb >= 2) == (k == 4):
                total = total + yrecv[0, xb].astype(F32)
            yxbuf[k, xb] = total.astype(BF16)
        yx_send(k)

    for i in range(9):
        opening, closing = SPANS[DEGREE[i]]
        first = ENTRY[i, opening]
        rt35[first:first + closing - opening, :] = rt_in[i, opening:closing, :]
    rt35[35:40, :] = jnp.zeros((5, 64), F32)
    table = rt35[...]
    high = table.astype(BF16)
    rot2[:, 0:64] = high
    rot2[:, 64:128] = (table - high.astype(F32)).astype(BF16)

    arrived(PH_COZ, 0, corecv.at[pl.ds(0, NZ - 1)])
    for half in range(2):
        tall = jnp.transpose(corecv[:, half].reshape(128, 128).astype(F32)).astype(BF16)
        rows = 128 if half == 0 else 16
        cs[half * 128:half * 128 + rows, :] = tall[0:rows]

    def turned(entries, values, opening, closing, i):
        total = entries[i, opening] * values(opening)
        for b in range(opening + 1, closing):
            total = total + entries[i, b] * values(b)
        return total

    def entries_of(t, at):
        return {key: turns[t, k:k + 1, at] for key, k in ENTRY.items()}

    def prepare(t, carry):
        lanes = lax.broadcasted_iota(I32, (128, 128), 0).astype(F32)
        folded = (lax.broadcasted_iota(I32, (128, 128), 0) & 63).astype(F32)
        for q in range(NX):
            at = slice(q * 128, (q + 1) * 128)
            codes = corecv[t, 2 + q].astype(F32)
            oh[t, :, at] = one_hot(lanes == codes[0:1])
            oh[NZ, :, at] = one_hot(lanes == codes[1:2])
            oh[NZ + 1, :, at] = one_hot(folded == codes[2:3])
        ch[...] = dot(cs[...], oh[NZ])
        turns[t] = dot(rot2[...], oh[NZ + 1])
        for q in range(NX):
            at = slice(q * 128, (q + 1) * 128)
            entries = entries_of(t, at)
            for opening, closing in SPANS:
                for i in range(opening, closing):
                    grads_at[t, i * 16:(i + 1) * 16, at] = turned(
                        entries, lambda b: ch[b * 16:(b + 1) * 16, at], opening, closing, i)
        return carry

    def pass_on(s):
        right_copy(s - 1).wait_recv()
        right_copy(s).start()
        left_copy(s - 1).wait_recv()
        if s < 3:
            left_copy(s).start()

    pass_on(1)
    lax.fori_loop(0, 3, prepare, 0)
    pass_on(2)
    lax.fori_loop(3, 5, prepare, 0)

    for k, dy in enumerate(NEAR):
        arrived(PH_YX, k, yxrecv.at[k] if dy else yxrecv.at[k, pl.ds(0, NX - 1)])
    packed = jnp.zeros((32, 1024), F32)
    for l in range(3):
        for s in range(NX):
            total = yxrecv[0, s, l].astype(F32)
            for k in range(1, 5):
                total = total + yxrecv[k, s, l].astype(F32)
            mx[s, l] = total.astype(BF16)
        for h in range(2):
            packed = packed + dot(mx[2 * h:2 * h + 2, l].reshape(32, 128), perm[l, h])
    packed = packed.astype(BF16)
    for t in range(NZ):
        mzbuf[t] = packed[:, t * 128:(t + 1) * 128].reshape(2, 16, 128)
    each(NZ, lambda d: remote(
        PH_MZ, 0, mzbuf.at[lax.rem(z + d, NZ)], wc.at[z], device(dz=d)).start())
    wc[z] = mzbuf[z]
    mc[z] = mx[...]
    pass_on(3)
    lax.fori_loop(5, 8, prepare, 0)
    right_copy(3).wait_recv()
    arrived(PH_MZ, 0, wc.at[pl.ds(0, NZ - 1)])
    each(NZ, lambda d: remote(PH_MC, 0, mx, mc.at[z], device(dz=d)).start())

    columns16 = jnp.concatenate(
        [jnp.concatenate([wc[t, s] for t in range(NZ)], axis=0) for s in range(2)], axis=0)
    flipped = jnp.transpose(columns16.astype(F32)).astype(BF16)
    for b in range(9):
        l = DEGREE[b]
        maps = jnp.concatenate([flipped[h * 64 + l * 16:h * 64 + (l + 1) * 16] for h in range(2)], axis=1)
        hs[b * 16:(b + 1) * 16, :] = dot(maps, a_ref[:, b].reshape(128, 512), NT).astype(BF16)


    def edges(t):
        hh[t] = dot(hs[...], oh[t])
        for q in range(NX):
            at = slice(q * 128, (q + 1) * 128)
            entries = entries_of(t, at)
            grads, inner, gate = [], None, None
            for opening, closing in SPANS:
                for i in range(opening, closing):
                    hidden = turned(entries, lambda b: hh[t, b * 16:(b + 1) * 16, at], opening, closing, i)
                    grad = grads_at[t, i * 16:(i + 1) * 16, at]
                    if i == 0:
                        gate = jax.nn.sigmoid(hidden)
                    inner = grad * hidden if inner is None else inner + grad * hidden
                    grads.append(grad * gate)
            grads[0] = grads[0] + inner * gate * (1.0 - gate)
            for opening, closing in SPANS:
                for b in range(opening, closing):
                    total = entries[opening, b] * grads[opening]
                    for i in range(opening + 1, closing):
                        total = total + entries[i, b] * grads[i]
                    u_ref[t, b * 16:(b + 1) * 16, at] = total.astype(BF16)

    for t in range(NZ):
        edges(t)
    wide_u = jnp.concatenate([u_ref[t] for t in range(NZ)], axis=1)
    g_acc[...] = dot(wide_u, jnp.concatenate([oh[t] for t in range(NZ)], axis=1), NT)

    sums = g_acc[...]
    narrow = sums.astype(BF16)
    for h in range(2):
        sgt[h * 64 + 48:h * 64 + 64, :] = jnp.zeros((16, 256), F32)
    for l, (opening, closing) in enumerate(SPANS):
        total = jnp.zeros((16, 512), F32)
        for b in range(opening, closing):
            total = total + dot(narrow[b * 16:(b + 1) * 16], a_ref[:, b].reshape(128, 512))
        for h in range(2):
            sgt[h * 64 + l * 16:h * 64 + (l + 1) * 16, :] = total[:, h * 256:(h + 1) * 256]
    tall = jnp.transpose(sgt[...]).astype(BF16)
    for t in range(NZ):
        for s in range(2):
            first = s * 128 + t * 16
            sgbuf[t, s] = tall[first:first + 16]
    each(NZ, lambda d: remote(
        PH_SZ, 0, sgbuf.at[lax.rem(z + d, NZ)], sgrecv.at[z], device(dz=d)).start())
    sgrecv[z] = sgbuf[z]
    turned_sums = jnp.transpose(
        jnp.concatenate([sums, jnp.zeros((112, 128), F32)], axis=0)).astype(BF16)
    for t in range(NZ):
        gbuf[t] = turned_sums[t * 16:(t + 1) * 16]
    each(NZ, lambda d: remote(
        PH_GZ, 0, gbuf.at[lax.rem(z + d, NZ)], grecv.at[z], device(dz=d)).start())
    grecv[z] = gbuf[z]

    arrived(PH_SZ, 0, sgrecv.at[pl.ds(0, NZ - 1)])
    rows = dot(sgrecv[0].reshape(32, 128), unperm[0])
    for t in range(1, NZ):
        rows = rows + dot(sgrecv[t].reshape(32, 128), unperm[t])
    for s in range(NX):
        for l in range(3):
            at = (s // 2 * 3 + l) * 128
            sg4[s, l] = rows[s % 2 * 16:s % 2 * 16 + 16, at:at + 128].astype(BF16)

    for k in (0, 4, 1, 3, 2):
        dy = NEAR[k]
        if dy:
            remote(PH_SYX, k, sg4.at[x], sgx.at[k, x], device(dy=dy)).start()
        else:
            sgx[k, x] = sg4[x]
        each(NX, lambda d: remote(
            PH_SYX, k, sg4.at[lax.rem(x + d, NX)], sgx.at[k, x], device(dy=dy, dx=d)).start())

    arrived(PH_GZ, 0, grecv.at[pl.ds(0, NZ - 1)])
    held = jnp.zeros((192, 128), F32)
    for t in range(NZ):
        wide = (dot(expand[...], grecv[t]) * same[...]).astype(BF16)
        held = held + dot(wide, fold[t])

    arrived(PH_SYX, 0, sgx.at[0])
    arrived(PH_SYX, 4, sgx.at[4])
    for h, k, hop in ((0, 0, -2), (1, 4, 2)):
        remote(PH_FW, 3 * h, sgx.at[k, halves[h]], forwarded.at[0, halves[h]], device(dy=hop)).start()
    for slot, k, hop in ((1, 4, 1), (2, 0, -1)):
        remote(PH_FW, slot, sgx.at[k], forwarded.at[slot], device(dy=hop)).start()

    arrived(PH_MC, 0, mc.at[pl.ds(0, NZ - 1)])
    coefficient = split48(lax.broadcasted_iota(I32, (192, 128), 0))[1] >> 2
    parts = jnp.zeros((192, 512), F32)
    for l, (opening, closing) in enumerate(SPANS):
        inside = (coefficient >= opening) & (coefficient < closing)
        maps = jnp.concatenate(
            [jnp.concatenate([mc[t, s, l] for t in range(NZ)], axis=0) for s in range(NX)], axis=0)
        parts = parts + dot(jnp.where(inside, held, 0.0).astype(BF16), maps, NT)
    for s in range(NX):
        gxbuf[s] = parts[s * 48:(s + 1) * 48].astype(BF16)
    each(NX, lambda d: remote(
        PH_GX, 0, gxbuf.at[lax.rem(x + d, NX)], gxrecv.at[d], device(dx=d)).start())
    gxrecv[0] = gxbuf[x]
    for k in (1, 2, 3):
        arrived(PH_SYX, k, sgx.at[k] if NEAR[k] else sgx.at[k, pl.ds(0, NX - 1)])
    arrived(PH_GX, 0, gxrecv.at[pl.ds(0, NX - 1)])
    total = gxrecv[0].astype(F32)
    for s in range(1, NX):
        total = total + gxrecv[s].astype(F32)
    for b in range(9):
        ga_ref[b] = total[b * 4:b * 4 + 4]

    for h in range(2):
        arrived(PH_FW, 3 * h, forwarded.at[0, halves[h]])
    for slot in (1, 2):
        arrived(PH_FW, slot, forwarded.at[slot])

    def expert_sum(expert, s):
        total = None
        for k, dy in enumerate(NEAR):
            term = share(-dy, expert) * sgx[k, s].astype(F32)
            total = term if total is None else total + term
        for slot, dy in ((0, 4), (1, -3), (2, 3)):
            total = total + share(dy, expert) * forwarded[slot, s].astype(F32)
        return total

    for e in range(2):
        for s in range(NX):
            endbuf[e, s] = expert_sum(other_first + e, s).astype(BF16)
    end_copy = remote(PH_END, 0, endbuf, endrecv, device(other=True))
    end_copy.start()
    for e in range(2):
        for s in range(NX):
            ge_ref[e, :, :, s * 128:(s + 1) * 128] = expert_sum(own_first + e, s)
    end_copy.wait_recv()
    for e in range(2):
        for s in range(NX):
            ge_ref[e, :, :, s * 128:(s + 1) * 128] += endrecv[e, s].astype(F32)

    core_copy.wait_send()
    end_copy.wait_send()
    for s in range(4):
        right_copy(s).wait_send()
    for s in range(3):
        left_copy(s).wait_send()
    for phase, ref in ((PH_Y, ybuf), (PH_FW, forwarded)):
        for h in range(2):
            left(phase, 3 * h, ref.at[0, halves[h]])
        for slot in (1, 2):
            left(phase, slot, ref.at[slot])
    for k, dy in enumerate(NEAR):
        left(PH_YX, k, yxbuf.at[k] if dy else yxbuf.at[k, pl.ds(0, NX - 1)])
        left(PH_SYX, k, sg4 if dy else sg4.at[pl.ds(0, NX - 1)])
    left(PH_ATX, 0, atx.at[pl.ds(0, NX - 1)])
    left(PH_COX, 0, cox.at[pl.ds(0, NX - 1)])
    left(PH_GX, 0, gxbuf.at[pl.ds(0, NX - 1)])
    left(PH_COZ, 0, cobuf.at[pl.ds(0, NZ - 1)])
    left(PH_MZ, 0, mzbuf.at[pl.ds(0, NZ - 1)])
    left(PH_MC, 0, mc.at[pl.ds(0, NZ - 1)])
    left(PH_SZ, 0, sgbuf.at[pl.ds(0, NZ - 1)])
    left(PH_GZ, 0, gbuf.at[pl.ds(0, NZ - 1)])


def shards(
    atoms, cotangent, expert_weights, coefficients, src_owner, src_slot, tgt_slot, rot_index, rot_table
):
    hbm = pl.BlockSpec(memory_space=pltpu.HBM)
    vmem = pl.BlockSpec(memory_space=pltpu.VMEM)
    smem = pl.BlockSpec(memory_space=pltpu.SMEM)

    def b16(*shape):
        return pltpu.VMEM(shape, BF16)

    def f32(*shape):
        return pltpu.VMEM(shape, F32)

    grad_atoms, grad_experts = pl.pallas_call(
        kernel,
        out_shape=(
            jax.ShapeDtypeStruct((9, 4, 512), F32),
            jax.ShapeDtypeStruct((2, 3, 16, 512), F32),
        ),
        in_specs=[smem] + [hbm] * 8,
        out_specs=(vmem, vmem),
        scratch_shapes=[
            b16(2, 3, 16, 512),
            b16(2, 3, 16, 512),
            b16(9, 4, 512),
            b16(9, 4, 512),
            pltpu.VMEM((4, 1, 128), I32),
            f32(9, 9, 64),
            f32(40, 64),
            b16(3, NX, 3, 16, 128),
            b16(3, NX, 3, 16, 128),
            b16(5, NX, 3, 16, 128),
            b16(5, NX, 3, 16, 128),
            b16(NX, 3, 16, 128),
            b16(NZ, 2, 16, 128),
            b16(NZ, 2, 16, 128),
            b16(NZ, NX, 3, 16, 128),
            f32(1, 48, 512),
            b16(NX + 1, NX, 48, 128),
            b16(NZ, 9, 16, 512),
            f32(1, 48, 512),
            b16(2 * NX, 64, 128),
            b16(NZ, 6, 16, 128),
            b16(NZ, 6, 16, 128),
            b16(192, 16),
            b16(NZ, 256, 128),
            b16(NZ, 128, 256),
            b16(3, 2, 128, 1024),
            b16(NZ, 128, 768),
            b16(144, 192),
            b16(16, 192),
            f32(192, 256),
            b16(40, 128),
            b16(144, 128),
            b16(144, 128),
            f32(NZ, 144, 512),
            f32(144, 512),
            f32(NZ, 144, 512),
            f32(NZ, 40, 512),
            b16(NZ + 2, 128, 512),
            b16(NZ, 144, 512),
            f32(144, 128),
            b16(NZ, 16, 256),
            b16(NZ, 16, 256),
            b16(NX, 48, 512),
            b16(NX, 48, 512),
            f32(128, 256),
            b16(NZ, 2, 16, 128),
            b16(NZ, 2, 16, 128),
            b16(NX, 3, 16, 128),
            b16(5, NX, 3, 16, 128),
            b16(3, NX, 3, 16, 128),
            b16(2, NX, 3, 16, 128),
            b16(2, NX, 3, 16, 128),
            pltpu.SemaphoreType.DMA((8,)),
            pltpu.SemaphoreType.DMA((17, 5)),
            pltpu.SemaphoreType.DMA((17, 5)),
        ],
        compiler_params=pltpu.CompilerParams(
            collective_id=0, has_side_effects=True, vmem_limit_bytes=60 * 1024 * 1024
        ),
        cost_estimate=pl.CostEstimate(
            flops=2_000_000_000, bytes_accessed=1_000_000, transcendentals=65536
        ),
    )(
        coefficients, expert_weights, atoms[0].transpose(1, 0, 2), cotangent[0].transpose(1, 0, 2),
        src_owner.reshape(1, -1), src_slot, tgt_slot, rot_index, rot_table.transpose(1, 2, 0),
    )
    return grad_atoms.transpose(1, 0, 2)[None], grad_experts


def solution(mesh):
    placed = (
        P("grp", "graph", None, None),
        P("grp", "graph", None, None),
        P("grp", None, "graph", None),
        P(),
        P("grp", "graph", None),
        P("grp", "graph"),
        P("grp", "graph"),
        P("grp", "graph"),
        P(),
    )
    return jax.shard_map(
        shards,
        mesh=mesh,
        in_specs=placed,
        out_specs=(P("grp", "graph", None, None), P("grp", None, "graph", None)),
        check_vma=False,
    )
```

```python
import jax
import jax.numpy as jnp
from jax import lax
from jax.experimental import pallas as pl
from jax.experimental.pallas import tpu as pltpu
from jax.sharding import PartitionSpec as P

F32, BF16, I32 = jnp.float32, jnp.bfloat16, jnp.int32
NX, NZ, NY = 4, 8, 8
SPANS = ((0, 1), (1, 4), (4, 9))
DEGREE = (0, 1, 1, 1, 2, 2, 2, 2, 2)
MESH = pl.DeviceIdType.MESH
NN = (((1,), (0,)), ((), ()))
NT = (((1,), (1,)), ((), ()))

(PH_CORE, PH_Y, PH_YX, PH_ATX, PH_ATR, PH_ATL, PH_COX, PH_COZ, PH_MZ, PH_MC,
 PH_GZ, PH_GX, PH_SZ, PH_SYX, PH_FW, PH_END, PH_MCL) = range(17)
NEAR = (-2, -1, 0, 1, 2)
ENTRY = {}
for _opening, _closing in SPANS:
    for _i in range(_opening, _closing):
        for _b in range(_opening, _closing):
            ENTRY[_i, _b] = len(ENTRY)


def dot(a, b, dims=NN):
    return lax.dot_general(a, b, dims, preferred_element_type=F32)


def one_hot(test):
    return jnp.where(test, 1.0, 0.0).astype(BF16)


def grid_of(rows, columns):
    shape = (rows, columns)
    return lax.broadcasted_iota(I32, shape, 0), lax.broadcasted_iota(I32, shape, 1)


def roll16(block, by):
    by = by * 16 % 128
    return pltpu.roll(block, by, 1) if by else block


def split48(index):
    block = jnp.where(index >= 48, 1, 0) + jnp.where(index >= 96, 1, 0) + jnp.where(index >= 144, 1, 0)
    return block, index - 48 * block


def kernel(
    coef, w_hbm, at_hbm, co_hbm, owner_hbm, slot_hbm, tslot_hbm, turn_hbm, rt_hbm,
    ga_ref, ge_ref,
    w_own, w_sib, at_in, co_in, index_in, rt_in, rt35,
    ybuf, yrecv, yxbuf, yxrecv, mx, mzbuf, wc, mc,
    at48, atx, a_ref, co80, cox, cobuf, corecv,
    expand, fold, spread, order, gather16, same, rot2,
    hs, cs, hh, ch, grads_at, turns, oh, u_ref, g_acc, gbuf, grecv, gxbuf, gxrecv,
    sgt, sgbuf, sgrecv, sg4, sgx, forwarded, endbuf, endrecv,
    load_sem, send_sem, recv_sem,
):
    grp, graph = lax.axis_index("grp"), lax.axis_index("graph")
    y, core = lax.div(grp, 2), lax.rem(grp, 2)
    x, z = lax.div(graph, NZ), lax.rem(graph, NZ)

    def device(dy=None, dx=None, dz=None, other=False):
        along = y if dy is None else lax.rem(y + dy + NY, NY)
        across = x if dx is None else lax.rem(x + dx, NX)
        up = z if dz is None else lax.rem(z + dz, NZ)
        return {"grp": along * 2 + (1 - core if other else core), "graph": across * NZ + up}

    def remote(phase, slot, source, target, place):
        return pltpu.make_async_remote_copy(
            src_ref=source, dst_ref=target, send_sem=send_sem.at[phase, slot],
            recv_sem=recv_sem.at[phase, slot], device_id=place, device_id_type=MESH,
        )

    def each(count, body):
        def step(d, carry):
            body(d)
            return carry

        lax.fori_loop(1, count, step, 0)

    def arrived(phase, slot, ref):
        pltpu.make_async_copy(ref, ref, recv_sem.at[phase, slot]).wait()

    def left(phase, slot, ref):
        pltpu.make_async_copy(ref, ref, send_sem.at[phase, slot]).wait()

    loads = [
        pltpu.make_async_copy(source, target, load_sem.at[k])
        for k, (source, target) in enumerate((
            (w_hbm, w_own), (at_hbm, at_in), (co_hbm, co_in), (owner_hbm, index_in.at[0]),
            (slot_hbm, index_in.at[1]), (tslot_hbm, index_in.at[2]), (turn_hbm, index_in.at[3]),
            (rt_hbm, rt_in)))
    ]
    for load in loads:
        load.start()

    barrier = pltpu.get_barrier_semaphore()

    def greet(place):
        pl.semaphore_signal(barrier, inc=1, device_id=place, device_id_type=MESH)

    greet(device(other=True))
    for dy in NEAR:
        if dy:
            greet(device(dy=dy))
        each(NX, lambda d: greet(device(dy=dy, dx=d)))
    each(NZ, lambda d: greet(device(dz=d)))

    row, column = grid_of(144, 192)
    block, within = split48(column)
    order[...] = one_hot(
        ((within >> 2) == (row >> 4)) & (((row >> 2) & 3) == block) & ((within & 3) == (row & 3)))
    row, column = grid_of(16, 192)
    block, within = split48(column)
    gather16[...] = one_hot(row == block * 4 + (within & 3))
    row, column = grid_of(192, 256)
    block, within = split48(row)
    same[...] = jnp.where((within >> 2) == (column >> 4), 1.0, 0.0)
    for t in range(NZ):
        row, column = grid_of(128, 256)
        spread[t] = one_hot(((row >> 4) == t) & ((row & 15) == (column & 15)))

    for load in loads:
        load.wait()

    for b in range(9):
        co80[0, b * 4:b * 4 + 4, :] = co_in[b].astype(F32)
        at48[0, b * 4:b * 4 + 4, :] = at_in[b].astype(F32)
    at48[0, 36:48, :] = jnp.zeros((12, 512), F32)
    co80[0, 36:48, :] = jnp.zeros((12, 512), F32)

    def place(owner, slot):
        return (owner & 7) * 16 + (owner >> 3) * 4 + slot

    row = lax.broadcasted_iota(I32, (16, 128), 0)
    codes = jnp.where(row == x * 4, place(index_in[0], index_in[1]), 0)
    codes = jnp.where(row == x * 4 + 1, place(graph, index_in[2]), codes)
    codes = jnp.where(row == x * 4 + 2, index_in[3], codes).astype(F32).astype(BF16)
    for xb in range(NX):
        at = slice(xb * 128, (xb + 1) * 128)
        atx_out = at48[0, :, at].astype(BF16)
        cox_out = co80[0, :, at].astype(BF16)
        atx[NX, xb] = atx_out
        cox[NX + xb, 0:48, :] = cox_out
        cox[NX + xb, 48:64, :] = codes

    pl.semaphore_wait(barrier, 1 + 4 + 5 * (NX - 1) + (NZ - 1))

    core_copy = remote(PH_CORE, 0, w_own, w_sib, device(other=True))
    core_copy.start()
    each(NX, lambda d: remote(PH_ATX, 0, atx.at[NX], atx.at[x], device(dx=d)).start())
    each(NX, lambda d: remote(
        PH_COX, 0, cox.at[NX + lax.rem(x + d, NX)], cox.at[x], device(dx=d)).start())
    atx[x] = atx[NX]
    cox[x] = cox[NX + x]

    core_copy.wait_recv()

    def share(dy, expert):
        return coef[lax.rem(y + dy + NY, NY) * 2 + core, expert].astype(F32) * (1.0 / 1024.0)

    own_first, other_first = grp * 2, (y * 2 + 1 - core) * 2

    def partial_of(dy, xb):
        at = slice(xb * 128, (xb + 1) * 128)
        total = None
        for ref, first in ((w_own, own_first), (w_sib, other_first)):
            for e in range(2):
                term = share(dy, first + e) * ref[e, :, :, at].astype(F32)
                total = term if total is None else total + term
        return total

    halves = (pl.ds(0, 2), pl.ds(2, 2))
    for xb in range(NX):
        ybuf[0, xb] = partial_of(-4, xb).astype(BF16)
        if xb % 2:
            h = xb // 2
            remote(PH_Y, 3 * h, ybuf.at[0, halves[h]], yrecv.at[0, halves[h]],
                   device(dy=(-2, 2)[h])).start()
    for slot, dy, hop in ((1, 3, 1), (2, -3, -1)):
        for xb in range(NX):
            ybuf[slot, xb] = partial_of(dy, xb).astype(BF16)
        remote(PH_Y, slot, ybuf.at[slot], yrecv.at[slot], device(dy=hop)).start()

    def yx_send(k):
        dy = NEAR[k]
        if dy:
            remote(PH_YX, k, yxbuf.at[k, x], yxrecv.at[k, x], device(dy=dy)).start()
        else:
            yxrecv[k, x] = yxbuf[k, x]
        each(NX, lambda d: remote(
            PH_YX, k, yxbuf.at[k, lax.rem(x + d, NX)], yxrecv.at[k, x], device(dy=dy, dx=d)).start())

    for k in (1, 3, 2):
        for xb in range(NX):
            yxbuf[k, xb] = partial_of(NEAR[k], xb).astype(BF16)
        yx_send(k)

    arrived(PH_ATX, 0, atx.at[pl.ds(0, NX - 1)])
    for xb in range(NX):
        stacked = jnp.concatenate([atx[s, xb] for s in range(NX)], axis=0)
        a_ref[z, :, :, xb * 128:(xb + 1) * 128] = dot(order[...], stacked).astype(BF16).reshape(9, 16, 128)

    def right_copy(s):
        block = a_ref.at[lax.rem(z - s + NZ, NZ)]
        block = block.at[pl.ds(0, 5)] if s == 3 else block
        return remote(PH_ATR, s, block, block, device(dz=1))

    def left_copy(s):
        block = a_ref.at[lax.rem(z + s, NZ)]
        block = block.at[pl.ds(5, 4)] if s == 3 else block
        return remote(PH_ATL, s, block, block, device(dz=NZ - 1))

    right_copy(0).start()
    left_copy(0).start()

    arrived(PH_COX, 0, cox.at[pl.ds(0, NX - 1)])
    stacked = jnp.concatenate([cox[s, 0:48] for s in range(NX)], axis=0)
    codes = cox[0, 48:64].astype(F32)
    for s in range(1, NX):
        codes = codes + cox[s, 48:64].astype(F32)
    codes = codes.astype(BF16)
    for t in range(NZ):
        wide = (dot(stacked, spread[t]) * same[...]).astype(BF16)
        packed = dot(gather16[...], wide).astype(BF16)
        cobuf[t, 0] = packed[:, 0:128]
        cobuf[t, 1] = packed[:, 128:256]
        cobuf[t, 2] = codes
    each(NZ, lambda d: remote(
        PH_COZ, 0, cobuf.at[lax.rem(z + d, NZ)], corecv.at[z], device(dz=d)).start())
    corecv[z] = cobuf[z]

    for h in range(2):
        arrived(PH_Y, 3 * h, yrecv.at[0, halves[h]])
    for slot in (1, 2):
        arrived(PH_Y, slot, yrecv.at[slot])
    for k, dy, slot in ((0, -2, 2), (4, 2, 1)):
        for xb in range(NX):
            total = partial_of(dy, xb) + yrecv[slot, xb].astype(F32)
            if (xb >= 2) == (k == 4):
                total = total + yrecv[0, xb].astype(F32)
            yxbuf[k, xb] = total.astype(BF16)
        yx_send(k)

    for i in range(9):
        opening, closing = SPANS[DEGREE[i]]
        first = ENTRY[i, opening]
        rt35[first:first + closing - opening, :] = rt_in[i, opening:closing, :]
    rt35[35:40, :] = jnp.zeros((5, 64), F32)
    table = rt35[...]
    high = table.astype(BF16)
    rot2[:, 0:64] = high
    rot2[:, 64:128] = (table - high.astype(F32)).astype(BF16)

    arrived(PH_COZ, 0, corecv.at[pl.ds(0, NZ - 1)])
    for half in range(2):
        tall = jnp.transpose(corecv[:, half].reshape(128, 128).astype(F32)).astype(BF16)
        rows = 128 if half == 0 else 16
        cs[half * 128:half * 128 + rows, :] = tall[0:rows]

    def turned(entries, values, opening, closing, i):
        total = entries[i, opening] * values(opening)
        for b in range(opening + 1, closing):
            total = total + entries[i, b] * values(b)
        return total

    def entries_of(t, at):
        return {key: turns[t, k:k + 1, at] for key, k in ENTRY.items()}

    def prepare(t, carry):
        lanes = lax.broadcasted_iota(I32, (128, 128), 0).astype(F32)
        folded = (lax.broadcasted_iota(I32, (128, 128), 0) & 63).astype(F32)
        for q in range(NX):
            at = slice(q * 128, (q + 1) * 128)
            codes = corecv[t, 2].astype(F32)
            oh[t, :, at] = one_hot(lanes == codes[q * 4:q * 4 + 1])
            oh[NZ, :, at] = one_hot(lanes == codes[q * 4 + 1:q * 4 + 2])
            oh[NZ + 1, :, at] = one_hot(folded == codes[q * 4 + 2:q * 4 + 3])
        ch[...] = dot(cs[...], oh[NZ])
        turns[t] = dot(rot2[...], oh[NZ + 1])
        for q in range(NX):
            at = slice(q * 128, (q + 1) * 128)
            entries = entries_of(t, at)
            for opening, closing in SPANS:
                for i in range(opening, closing):
                    grads_at[t, i * 16:(i + 1) * 16, at] = turned(
                        entries, lambda b: ch[b * 16:(b + 1) * 16, at], opening, closing, i)
        return carry

    def pass_on(s):
        right_copy(s - 1).wait_recv()
        right_copy(s).start()
        left_copy(s - 1).wait_recv()
        left_copy(s).start()

    pass_on(1)
    lax.fori_loop(0, 3, prepare, 0)

    for k, dy in enumerate(NEAR):
        arrived(PH_YX, k, yxrecv.at[k] if dy else yxrecv.at[k, pl.ds(0, NX - 1)])
    slot = lax.broadcasted_iota(I32, (32, 128), 1) >> 4
    packed = [jnp.zeros((32, 128), F32) for t in range(NZ)]
    for l in range(3):
        for s in range(NX):
            total = yxrecv[0, s, l].astype(F32)
            for k in range(1, 5):
                total = total + yxrecv[k, s, l].astype(F32)
            mx[s, l] = total.astype(BF16)
        for h in range(2):
            block = mx[2 * h:2 * h + 2, l].reshape(32, 128).astype(F32)
            for t in range(NZ):
                shifted = roll16(block, h * 4 + l - t)
                packed[t] = jnp.where(slot == h * 4 + l, shifted, packed[t])
    for t in range(NZ):
        mzbuf[t] = packed[t].astype(BF16).reshape(2, 16, 128)
    each(NZ, lambda d: remote(
        PH_MZ, 0, mzbuf.at[lax.rem(z + d, NZ)], wc.at[z], device(dz=d)).start())
    wc[z] = mzbuf[z]
    mc[z] = mx[...]
    pass_on(2)
    lax.fori_loop(3, 5, prepare, 0)
    pass_on(3)
    lax.fori_loop(5, 8, prepare, 0)
    right_copy(3).wait_recv()
    left_copy(3).wait_recv()
    arrived(PH_MZ, 0, wc.at[pl.ds(0, NZ - 1)])
    each(NZ, lambda d: remote(PH_MC, 0, mx, mc.at[z], device(dz=d)).start())

    columns16 = jnp.concatenate(
        [jnp.concatenate([wc[t, s] for t in range(NZ)], axis=0) for s in range(2)], axis=0)
    flipped = jnp.transpose(columns16.astype(F32)).astype(BF16)
    for b in range(9):
        l = DEGREE[b]
        maps = jnp.concatenate([flipped[h * 64 + l * 16:h * 64 + (l + 1) * 16] for h in range(2)], axis=1)
        hs[b * 16:(b + 1) * 16, :] = dot(maps, a_ref[:, b].reshape(128, 512), NT).astype(BF16)


    def edges(t):
        hh[t] = dot(hs[...], oh[t])
        for q in range(NX):
            at = slice(q * 128, (q + 1) * 128)
            entries = entries_of(t, at)
            grads, inner, gate = [], None, None
            for opening, closing in SPANS:
                for i in range(opening, closing):
                    hidden = turned(entries, lambda b: hh[t, b * 16:(b + 1) * 16, at], opening, closing, i)
                    grad = grads_at[t, i * 16:(i + 1) * 16, at]
                    if i == 0:
                        gate = jax.nn.sigmoid(hidden)
                    inner = grad * hidden if inner is None else inner + grad * hidden
                    grads.append(grad * gate)
            grads[0] = grads[0] + inner * gate * (1.0 - gate)
            for opening, closing in SPANS:
                for b in range(opening, closing):
                    total = entries[opening, b] * grads[opening]
                    for i in range(opening + 1, closing):
                        total = total + entries[i, b] * grads[i]
                    u_ref[t, b * 16:(b + 1) * 16, at] = total.astype(BF16)

    for t in range(NZ):
        edges(t)
    wide_u = jnp.concatenate([u_ref[t] for t in range(NZ)], axis=1)
    g_acc[...] = dot(wide_u, jnp.concatenate([oh[t] for t in range(NZ)], axis=1), NT)

    sums = g_acc[...]
    narrow = sums.astype(BF16)
    for h in range(2):
        sgt[h * 64 + 48:h * 64 + 64, :] = jnp.zeros((16, 256), F32)
    for l, (opening, closing) in enumerate(SPANS):
        total = jnp.zeros((16, 512), F32)
        for b in range(opening, closing):
            total = total + dot(narrow[b * 16:(b + 1) * 16], a_ref[:, b].reshape(128, 512))
        for h in range(2):
            sgt[h * 64 + l * 16:h * 64 + (l + 1) * 16, :] = total[:, h * 256:(h + 1) * 256]
    tall = jnp.transpose(sgt[...]).astype(BF16)
    for t in range(NZ):
        for s in range(2):
            first = s * 128 + t * 16
            sgbuf[t, s] = tall[first:first + 16]
    each(NZ, lambda d: remote(
        PH_SZ, 0, sgbuf.at[lax.rem(z + d, NZ)], sgrecv.at[z], device(dz=d)).start())
    sgrecv[z] = sgbuf[z]
    turned_sums = jnp.transpose(
        jnp.concatenate([sums, jnp.zeros((112, 128), F32)], axis=0)).astype(BF16)
    for t in range(NZ):
        gbuf[t] = turned_sums[t * 16:(t + 1) * 16]
    each(NZ, lambda d: remote(
        PH_GZ, 0, gbuf.at[lax.rem(z + d, NZ)], grecv.at[z], device(dz=d)).start())
    grecv[z] = gbuf[z]

    row, column = grid_of(192, 16)
    block, within = split48(row)
    expand[...] = one_hot(column == block * 4 + (within & 3))
    for t in range(NZ):
        row, column = grid_of(256, 128)
        fold[t] = one_hot(((column >> 4) == t) & ((row & 15) == (column & 15)))

    arrived(PH_SZ, 0, sgrecv.at[pl.ds(0, NZ - 1)])
    blocks = [sgrecv[t].reshape(32, 128).astype(F32) for t in range(NZ)]
    for l in range(3):
        for h in range(2):
            total = jnp.zeros((32, 128), F32)
            for t in range(NZ):
                total = jnp.where(slot == t, roll16(blocks[t], t - (h * 4 + l)), total)
            total = total.astype(BF16)
            sg4[2 * h, l] = total[0:16]
            sg4[2 * h + 1, l] = total[16:32]

    for k in (0, 4, 1, 3, 2):
        dy = NEAR[k]
        if dy:
            remote(PH_SYX, k, sg4.at[x], sgx.at[k, x], device(dy=dy)).start()
        else:
            sgx[k, x] = sg4[x]
        each(NX, lambda d: remote(
            PH_SYX, k, sg4.at[lax.rem(x + d, NX)], sgx.at[k, x], device(dy=dy, dx=d)).start())

    arrived(PH_GZ, 0, grecv.at[pl.ds(0, NZ - 1)])
    held = jnp.zeros((192, 128), F32)
    for t in range(NZ):
        wide = (dot(expand[...], grecv[t]) * same[...]).astype(BF16)
        held = held + dot(wide, fold[t])

    arrived(PH_SYX, 0, sgx.at[0])
    arrived(PH_SYX, 4, sgx.at[4])
    for h, k, hop in ((0, 0, -2), (1, 4, 2)):
        remote(PH_FW, 3 * h, sgx.at[k, halves[h]], forwarded.at[0, halves[h]], device(dy=hop)).start()
    for slot, k, hop in ((1, 4, 1), (2, 0, -1)):
        remote(PH_FW, slot, sgx.at[k], forwarded.at[slot], device(dy=hop)).start()

    arrived(PH_MC, 0, mc.at[pl.ds(0, NZ - 1)])
    coefficient = split48(lax.broadcasted_iota(I32, (192, 128), 0))[1] >> 2
    parts = jnp.zeros((192, 512), F32)
    for l, (opening, closing) in enumerate(SPANS):
        inside = (coefficient >= opening) & (coefficient < closing)
        maps = jnp.concatenate(
            [jnp.concatenate([mc[t, s, l] for t in range(NZ)], axis=0) for s in range(NX)], axis=0)
        parts = parts + dot(jnp.where(inside, held, 0.0).astype(BF16), maps, NT)
    for s in range(NX):
        gxbuf[s] = parts[s * 48:(s + 1) * 48].astype(BF16)
    each(NX, lambda d: remote(
        PH_GX, 0, gxbuf.at[lax.rem(x + d, NX)], gxrecv.at[d], device(dx=d)).start())
    gxrecv[0] = gxbuf[x]
    for k in (1, 2, 3):
        arrived(PH_SYX, k, sgx.at[k] if NEAR[k] else sgx.at[k, pl.ds(0, NX - 1)])
    arrived(PH_GX, 0, gxrecv.at[pl.ds(0, NX - 1)])
    total = gxrecv[0].astype(F32)
    for s in range(1, NX):
        total = total + gxrecv[s].astype(F32)
    for b in range(9):
        ga_ref[b] = total[b * 4:b * 4 + 4]

    for h in range(2):
        arrived(PH_FW, 3 * h, forwarded.at[0, halves[h]])
    for slot in (1, 2):
        arrived(PH_FW, slot, forwarded.at[slot])

    def expert_sum(expert, s):
        total = None
        for k, dy in enumerate(NEAR):
            term = share(-dy, expert) * sgx[k, s].astype(F32)
            total = term if total is None else total + term
        for slot, dy in ((0, 4), (1, -3), (2, 3)):
            total = total + share(dy, expert) * forwarded[slot, s].astype(F32)
        return total

    for e in range(2):
        for s in range(NX):
            endbuf[e, s] = expert_sum(other_first + e, s).astype(BF16)
    end_copy = remote(PH_END, 0, endbuf, endrecv, device(other=True))
    end_copy.start()
    for e in range(2):
        for s in range(NX):
            ge_ref[e, :, :, s * 128:(s + 1) * 128] = expert_sum(own_first + e, s)
    end_copy.wait_recv()
    for e in range(2):
        for s in range(NX):
            ge_ref[e, :, :, s * 128:(s + 1) * 128] += endrecv[e, s].astype(F32)

    core_copy.wait_send()
    end_copy.wait_send()
    for s in range(4):
        right_copy(s).wait_send()
        left_copy(s).wait_send()
    for phase, ref in ((PH_Y, ybuf), (PH_FW, forwarded)):
        for h in range(2):
            left(phase, 3 * h, ref.at[0, halves[h]])
        for slot in (1, 2):
            left(phase, slot, ref.at[slot])
    for k, dy in enumerate(NEAR):
        left(PH_YX, k, yxbuf.at[k] if dy else yxbuf.at[k, pl.ds(0, NX - 1)])
        left(PH_SYX, k, sg4 if dy else sg4.at[pl.ds(0, NX - 1)])
    left(PH_ATX, 0, atx.at[pl.ds(0, NX - 1)])
    left(PH_COX, 0, cox.at[pl.ds(0, NX - 1)])
    left(PH_GX, 0, gxbuf.at[pl.ds(0, NX - 1)])
    left(PH_COZ, 0, cobuf.at[pl.ds(0, NZ - 1)])
    left(PH_MZ, 0, mzbuf.at[pl.ds(0, NZ - 1)])
    left(PH_MC, 0, mc.at[pl.ds(0, NZ - 1)])
    left(PH_SZ, 0, sgbuf.at[pl.ds(0, NZ - 1)])
    left(PH_GZ, 0, gbuf.at[pl.ds(0, NZ - 1)])


def shards(
    atoms, cotangent, expert_weights, coefficients, src_owner, src_slot, tgt_slot, rot_index, rot_table
):
    hbm = pl.BlockSpec(memory_space=pltpu.HBM)
    vmem = pl.BlockSpec(memory_space=pltpu.VMEM)
    smem = pl.BlockSpec(memory_space=pltpu.SMEM)

    def b16(*shape):
        return pltpu.VMEM(shape, BF16)

    def f32(*shape):
        return pltpu.VMEM(shape, F32)

    grad_atoms, grad_experts = pl.pallas_call(
        kernel,
        out_shape=(
            jax.ShapeDtypeStruct((9, 4, 512), F32),
            jax.ShapeDtypeStruct((2, 3, 16, 512), F32),
        ),
        in_specs=[smem] + [hbm] * 8,
        out_specs=(vmem, vmem),
        scratch_shapes=[
            b16(2, 3, 16, 512),
            b16(2, 3, 16, 512),
            b16(9, 4, 512),
            b16(9, 4, 512),
            pltpu.VMEM((4, 1, 128), I32),
            f32(9, 9, 64),
            f32(40, 64),
            b16(3, NX, 3, 16, 128),
            b16(3, NX, 3, 16, 128),
            b16(5, NX, 3, 16, 128),
            b16(5, NX, 3, 16, 128),
            b16(NX, 3, 16, 128),
            b16(NZ, 2, 16, 128),
            b16(NZ, 2, 16, 128),
            b16(NZ, NX, 3, 16, 128),
            f32(1, 48, 512),
            b16(NX + 1, NX, 48, 128),
            b16(NZ, 9, 16, 512),
            f32(1, 48, 512),
            b16(2 * NX, 64, 128),
            b16(NZ, 3, 16, 128),
            b16(NZ, 3, 16, 128),
            b16(192, 16),
            b16(NZ, 256, 128),
            b16(NZ, 128, 256),
            b16(144, 192),
            b16(16, 192),
            f32(192, 256),
            b16(40, 128),
            b16(144, 128),
            b16(144, 128),
            f32(NZ, 144, 512),
            f32(144, 512),
            f32(NZ, 144, 512),
            f32(NZ, 40, 512),
            b16(NZ + 2, 128, 512),
            b16(NZ, 144, 512),
            f32(144, 128),
            b16(NZ, 16, 256),
            b16(NZ, 16, 256),
            b16(NX, 48, 512),
            b16(NX, 48, 512),
            f32(128, 256),
            b16(NZ, 2, 16, 128),
            b16(NZ, 2, 16, 128),
            b16(NX, 3, 16, 128),
            b16(5, NX, 3, 16, 128),
            b16(3, NX, 3, 16, 128),
            b16(2, NX, 3, 16, 128),
            b16(2, NX, 3, 16, 128),
            pltpu.SemaphoreType.DMA((8,)),
            pltpu.SemaphoreType.DMA((17, 5)),
            pltpu.SemaphoreType.DMA((17, 5)),
        ],
        compiler_params=pltpu.CompilerParams(
            collective_id=0, has_side_effects=True, vmem_limit_bytes=60 * 1024 * 1024
        ),
        cost_estimate=pl.CostEstimate(
            flops=2_000_000_000, bytes_accessed=1_000_000, transcendentals=65536
        ),
    )(
        coefficients, expert_weights, atoms[0].transpose(1, 0, 2), cotangent[0].transpose(1, 0, 2),
        src_owner.reshape(1, -1), src_slot, tgt_slot, rot_index, rot_table.transpose(1, 2, 0),
    )
    return grad_atoms.transpose(1, 0, 2)[None], grad_experts


def solution(mesh):
    placed = (
        P("grp", "graph", None, None),
        P("grp", "graph", None, None),
        P("grp", None, "graph", None),
        P(),
        P("grp", "graph", None),
        P("grp", "graph"),
        P("grp", "graph"),
        P("grp", "graph"),
        P(),
    )
    return jax.shard_map(
        shards,
        mesh=mesh,
        in_specs=placed,
        out_specs=(P("grp", "graph", None, None), P("grp", None, "graph", None)),
        check_vma=False,
    )
```

```python
import jax
import jax.numpy as jnp
from jax import lax
from jax.experimental import pallas as pl
from jax.experimental.pallas import tpu as pltpu
from jax.sharding import PartitionSpec as P

F32, BF16, I32 = jnp.float32, jnp.bfloat16, jnp.int32
NX, NZ, NY = 4, 8, 8
SPANS = ((0, 1), (1, 4), (4, 9))
DEGREE = (0, 1, 1, 1, 2, 2, 2, 2, 2)
MESH = pl.DeviceIdType.MESH
NN = (((1,), (0,)), ((), ()))
NT = (((1,), (1,)), ((), ()))

(PH_CORE, PH_Y, PH_YX, PH_ATX, PH_ATR, PH_ATL, PH_COX, PH_COZ, PH_MZ, PH_MC,
 PH_GZ, PH_GX, PH_SZ, PH_SYX, PH_FW, PH_END, PH_ATR1, PH_ATL1, PH_AX) = range(19)
NEAR = (-2, -1, 0, 1, 2)
ENTRY = {}
for _opening, _closing in SPANS:
    for _i in range(_opening, _closing):
        for _b in range(_opening, _closing):
            ENTRY[_i, _b] = len(ENTRY)


def dot(a, b, dims=NN):
    return lax.dot_general(a, b, dims, preferred_element_type=F32)


def one_hot(test):
    return jnp.where(test, 1.0, 0.0).astype(BF16)


def grid_of(rows, columns):
    shape = (rows, columns)
    return lax.broadcasted_iota(I32, shape, 0), lax.broadcasted_iota(I32, shape, 1)


def roll16(block, by):
    by = by * 16 % 128
    return pltpu.roll(block, by, 1) if by else block


def split48(index):
    block = jnp.where(index >= 48, 1, 0) + jnp.where(index >= 96, 1, 0) + jnp.where(index >= 144, 1, 0)
    return block, index - 48 * block


def kernel(
    coef, w_hbm, at_hbm, co_hbm, owner_hbm, slot_hbm, tslot_hbm, turn_hbm, rt_hbm,
    ga_ref, ge_ref,
    w_own, w_sib, at_in, co_in, index_in, rt_in, rt35,
    ybuf, yrecv, yxbuf, yxrecv, mx, mzbuf, wc, mc,
    at48, atx, a_ref, co80, cox, cobuf, corecv,
    expand, fold, spread, order, gather16, same, rot2,
    hs, cs, hh, ch, grads_at, turns, oh, u_ref, g_acc, gbuf, grecv, gxbuf, gxrecv,
    sgt, sgbuf, sgrecv, sg4, sgx, forwarded, near_sum, endbuf, endrecv,
    load_sem, send_sem, recv_sem,
):
    grp, graph = lax.axis_index("grp"), lax.axis_index("graph")
    y, core = lax.div(grp, 2), lax.rem(grp, 2)
    x, z = lax.div(graph, NZ), lax.rem(graph, NZ)

    def device(dy=None, dx=None, dz=None, other=False):
        along = y if dy is None else lax.rem(y + dy + NY, NY)
        across = x if dx is None else lax.rem(x + dx, NX)
        up = z if dz is None else lax.rem(z + dz, NZ)
        return {"grp": along * 2 + (1 - core if other else core), "graph": across * NZ + up}

    def remote(phase, slot, source, target, place):
        return pltpu.make_async_remote_copy(
            src_ref=source, dst_ref=target, send_sem=send_sem.at[phase, slot],
            recv_sem=recv_sem.at[phase, slot], device_id=place, device_id_type=MESH,
        )

    def each(count, body):
        for d in range(1, count):
            body(d)

    def arrived(phase, slot, ref):
        pltpu.make_async_copy(ref, ref, recv_sem.at[phase, slot]).wait()

    def left(phase, slot, ref):
        pltpu.make_async_copy(ref, ref, send_sem.at[phase, slot]).wait()

    loads = [
        pltpu.make_async_copy(source, target, load_sem.at[k])
        for k, (source, target) in enumerate((
            (w_hbm, w_own), (at_hbm, at_in), (co_hbm, co_in), (owner_hbm, index_in.at[0]),
            (slot_hbm, index_in.at[1]), (tslot_hbm, index_in.at[2]), (turn_hbm, index_in.at[3]),
            (rt_hbm, rt_in)))
    ]
    for load in loads:
        load.start()

    barrier = pltpu.get_barrier_semaphore()

    def greet(place):
        pl.semaphore_signal(barrier, inc=1, device_id=place, device_id_type=MESH)

    greet(device(other=True))
    for dy in NEAR:
        if dy:
            greet(device(dy=dy))
        each(NX, lambda d: greet(device(dy=dy, dx=d)))
    each(NZ, lambda d: greet(device(dz=d)))

    row, column = grid_of(144, 192)
    block, within = split48(column)
    order[...] = one_hot(
        ((within >> 2) == (row >> 4)) & (((row >> 2) & 3) == block) & ((within & 3) == (row & 3)))
    row, column = grid_of(16, 192)
    block, within = split48(column)
    gather16[...] = one_hot(row == block * 4 + (within & 3))
    row, column = grid_of(192, 256)
    block, within = split48(row)
    same[...] = jnp.where((within >> 2) == (column >> 4), 1.0, 0.0)
    for t in range(NZ):
        row, column = grid_of(128, 256)
        spread[t] = one_hot(((row >> 4) == t) & ((row & 15) == (column & 15)))

    for load in loads:
        load.wait()

    for b in range(9):
        co80[0, b * 4:b * 4 + 4, :] = co_in[b].astype(F32)
        at48[0, b * 4:b * 4 + 4, :] = at_in[b].astype(F32)
    at48[0, 36:48, :] = jnp.zeros((12, 512), F32)
    co80[0, 36:48, :] = jnp.zeros((12, 512), F32)

    def place(owner, slot):
        return (owner & 7) * 16 + (owner >> 3) * 4 + slot

    row = lax.broadcasted_iota(I32, (16, 128), 0)
    codes = jnp.where(row == x * 4, place(index_in[0], index_in[1]), 0)
    codes = jnp.where(row == x * 4 + 1, place(graph, index_in[2]), codes)
    codes = jnp.where(row == x * 4 + 2, index_in[3], codes).astype(F32).astype(BF16)
    for xb in range(NX):
        at = slice(xb * 128, (xb + 1) * 128)
        atx_out = at48[0, :, at].astype(BF16)
        cox_out = co80[0, :, at].astype(BF16)
        atx[NX, xb] = atx_out
        cox[NX + xb, 0:48, :] = cox_out
        cox[NX + xb, 48:64, :] = codes

    pl.semaphore_wait(barrier, 1 + 4 + 5 * (NX - 1) + (NZ - 1))

    core_copy = remote(PH_CORE, 0, w_own, w_sib, device(other=True))
    core_copy.start()
    each(NX, lambda d: remote(PH_ATX, 0, atx.at[NX], atx.at[x], device(dx=d)).start())
    each(NX, lambda d: remote(
        PH_COX, 0, cox.at[NX + lax.rem(x + d, NX)], cox.at[x], device(dx=d)).start())
    atx[x] = atx[NX]
    cox[x] = cox[NX + x]

    core_copy.wait_recv()

    def share(dy, expert):
        return coef[lax.rem(y + dy + NY, NY) * 2 + core, expert].astype(F32) * (1.0 / 1024.0)

    own_first, other_first = grp * 2, (y * 2 + 1 - core) * 2

    def partial_of(dy, xb):
        at = slice(xb * 128, (xb + 1) * 128)
        total = None
        for ref, first in ((w_own, own_first), (w_sib, other_first)):
            for e in range(2):
                term = share(dy, first + e) * ref[e, :, :, at].astype(F32)
                total = term if total is None else total + term
        return total

    halves = (pl.ds(0, 2), pl.ds(2, 2))
    for xb in range(NX):
        ybuf[0, xb] = partial_of(-4, xb).astype(BF16)
        if xb % 2:
            h = xb // 2
            remote(PH_Y, 3 * h, ybuf.at[0, halves[h]], yrecv.at[0, halves[h]],
                   device(dy=(-2, 2)[h])).start()
    for slot, dy, hop in ((1, 3, 1), (2, -3, -1)):
        for xb in range(NX):
            ybuf[slot, xb] = partial_of(dy, xb).astype(BF16)
        remote(PH_Y, slot, ybuf.at[slot], yrecv.at[slot], device(dy=hop)).start()

    def yx_send(k):
        dy = NEAR[k]
        if dy:
            remote(PH_YX, k, yxbuf.at[k, x], yxrecv.at[k, x], device(dy=dy)).start()
        else:
            yxrecv[k, x] = yxbuf[k, x]
        each(NX, lambda d: remote(
            PH_YX, k, yxbuf.at[k, lax.rem(x + d, NX)], yxrecv.at[k, x], device(dy=dy, dx=d)).start())

    for k in (1, 3, 2):
        for xb in range(NX):
            yxbuf[k, xb] = partial_of(NEAR[k], xb).astype(BF16)
        yx_send(k)

    arrived(PH_ATX, 0, atx.at[pl.ds(0, NX - 1)])
    for xb in range(NX):
        stacked = jnp.concatenate([atx[s, xb] for s in range(NX)], axis=0)
        a_ref[z, :, :, xb * 128:(xb + 1) * 128] = dot(order[...], stacked).astype(BF16).reshape(9, 16, 128)

    def z_hop(way, s):
        slot = lax.rem(z + (s if way else NZ - s), NZ)
        common = pl.ds(0, 5) if s < 3 else (pl.ds(3, 2) if way else pl.ds(0, 3))
        parts = [(PH_ATL if way else PH_ATR, common)]
        if s < 3 or way:
            parts.append((PH_ATL1 if way else PH_ATR1, pl.ds(5 + x, 1)))
        return [
            remote(phase, s, a_ref.at[slot, part], a_ref.at[slot, part], device(dz=NZ - 1 if way else 1))
            for phase, part in parts
        ]

    def along_x(slot):
        block = a_ref.at[slot, pl.ds(5 + x, 1)]
        each(NX, lambda d: remote(PH_AX, 0, block, block, device(dx=d)).start())

    for way in range(2):
        for copy in z_hop(way, 0):
            copy.start()

    arrived(PH_COX, 0, cox.at[pl.ds(0, NX - 1)])
    stacked = jnp.concatenate([cox[s, 0:48] for s in range(NX)], axis=0)
    codes = cox[0, 48:64].astype(F32)
    for s in range(1, NX):
        codes = codes + cox[s, 48:64].astype(F32)
    codes = codes.astype(BF16)
    for t in range(NZ):
        wide = (dot(stacked, spread[t]) * same[...]).astype(BF16)
        packed = dot(gather16[...], wide).astype(BF16)
        cobuf[t, 0] = packed[:, 0:128]
        cobuf[t, 1] = packed[:, 128:256]
        cobuf[t, 2] = codes
    each(NZ, lambda d: remote(
        PH_COZ, 0, cobuf.at[lax.rem(z + d, NZ)], corecv.at[z], device(dz=d)).start())
    corecv[z] = cobuf[z]

    for h in range(2):
        arrived(PH_Y, 3 * h, yrecv.at[0, halves[h]])
    for slot in (1, 2):
        arrived(PH_Y, slot, yrecv.at[slot])
    for k, dy, slot in ((0, -2, 2), (4, 2, 1)):
        for xb in range(NX):
            total = partial_of(dy, xb) + yrecv[slot, xb].astype(F32)
            if (xb >= 2) == (k == 4):
                total = total + yrecv[0, xb].astype(F32)
            yxbuf[k, xb] = total.astype(BF16)
        yx_send(k)

    for i in range(9):
        opening, closing = SPANS[DEGREE[i]]
        first = ENTRY[i, opening]
        rt35[first:first + closing - opening, :] = rt_in[i, opening:closing, :]
    rt35[35:40, :] = jnp.zeros((5, 64), F32)
    table = rt35[...]
    high = table.astype(BF16)
    rot2[:, 0:64] = high
    rot2[:, 64:128] = (table - high.astype(F32)).astype(BF16)

    arrived(PH_COZ, 0, corecv.at[pl.ds(0, NZ - 1)])
    for half in range(2):
        tall = jnp.transpose(corecv[:, half].reshape(128, 128).astype(F32)).astype(BF16)
        rows = 128 if half == 0 else 16
        cs[half * 128:half * 128 + rows, :] = tall[0:rows]

    def turned(entries, values, opening, closing, i):
        total = entries[i, opening] * values(opening)
        for b in range(opening + 1, closing):
            total = total + entries[i, b] * values(b)
        return total

    def entries_of(t, at):
        return {key: turns[t, k:k + 1, at] for key, k in ENTRY.items()}

    def prepare(t):
        lanes = lax.broadcasted_iota(I32, (128, 128), 0).astype(F32)
        folded = (lax.broadcasted_iota(I32, (128, 128), 0) & 63).astype(F32)
        for q in range(NX):
            at = slice(q * 128, (q + 1) * 128)
            codes = corecv[t, 2].astype(F32)
            oh[t, :, at] = one_hot(lanes == codes[q * 4:q * 4 + 1])
            oh[NZ + t % 2, :, at] = one_hot(lanes == codes[q * 4 + 1:q * 4 + 2])
            oh[NZ + 2 + t % 2, :, at] = one_hot(folded == codes[q * 4 + 2:q * 4 + 3])
        ch[t % 2] = dot(cs[...], oh[NZ + t % 2])
        turns[t] = dot(rot2[...], oh[NZ + 2 + t % 2])
        for q in range(NX):
            at = slice(q * 128, (q + 1) * 128)
            entries = entries_of(t, at)
            for opening, closing in SPANS:
                for i in range(opening, closing):
                    grads_at[t, i * 16:(i + 1) * 16, at] = turned(
                        entries, lambda b: ch[t % 2, b * 16:(b + 1) * 16, at], opening, closing, i)

    def pass_on(s):
        for way in range(2):
            for copy in z_hop(way, s - 1):
                copy.wait_recv()
            for copy in z_hop(way, s):
                copy.start()
            along_x(lax.rem(z + (s if way else NZ - s), NZ))

    pass_on(1)
    for t in range(0, 3):
        prepare(t)

    for k, dy in enumerate(NEAR):
        arrived(PH_YX, k, yxrecv.at[k] if dy else yxrecv.at[k, pl.ds(0, NX - 1)])
    slot = lax.broadcasted_iota(I32, (32, 128), 1) >> 4
    packed = [jnp.zeros((32, 128), F32) for t in range(NZ)]
    for l in range(3):
        for s in range(NX):
            total = yxrecv[0, s, l].astype(F32)
            for k in range(1, 5):
                total = total + yxrecv[k, s, l].astype(F32)
            mx[s, l] = total.astype(BF16)
        for h in range(2):
            block = mx[2 * h:2 * h + 2, l].reshape(32, 128).astype(F32)
            for t in range(NZ):
                shifted = roll16(block, h * 4 + l - t)
                packed[t] = jnp.where(slot == h * 4 + l, shifted, packed[t])
    for t in range(NZ):
        mzbuf[t] = packed[t].astype(BF16).reshape(2, 16, 128)
    each(NZ, lambda d: remote(
        PH_MZ, 0, mzbuf.at[lax.rem(z + d, NZ)], wc.at[z], device(dz=d)).start())
    wc[z] = mzbuf[z]
    mc[z] = mx[...]
    pass_on(2)
    for t in range(3, 5):
        prepare(t)
    pass_on(3)
    for t in range(5, 8):
        prepare(t)
    for way in (1, 0):
        for copy in z_hop(way, 3):
            copy.wait_recv()
        if way:
            along_x(lax.rem(z + 4, NZ))
    arrived(PH_AX, 0, a_ref.at[pl.ds(0, NZ - 1), pl.ds(0, NX - 1)])
    arrived(PH_MZ, 0, wc.at[pl.ds(0, NZ - 1)])
    each(NZ, lambda d: remote(PH_MC, 0, mx, mc.at[z], device(dz=d)).start())

    columns16 = jnp.concatenate(
        [jnp.concatenate([wc[t, s] for t in range(NZ)], axis=0) for s in range(2)], axis=0)
    flipped = jnp.transpose(columns16.astype(F32)).astype(BF16)
    for b in range(9):
        l = DEGREE[b]
        maps = jnp.concatenate([flipped[h * 64 + l * 16:h * 64 + (l + 1) * 16] for h in range(2)], axis=1)
        hs[b * 16:(b + 1) * 16, :] = dot(maps, a_ref[:, b].reshape(128, 512), NT).astype(BF16)


    def edges(t):
        hh[t] = dot(hs[...], oh[t])
        for q in range(NX):
            at = slice(q * 128, (q + 1) * 128)
            entries = entries_of(t, at)
            grads, inner, gate = [], None, None
            for opening, closing in SPANS:
                for i in range(opening, closing):
                    hidden = turned(entries, lambda b: hh[t, b * 16:(b + 1) * 16, at], opening, closing, i)
                    grad = grads_at[t, i * 16:(i + 1) * 16, at]
                    if i == 0:
                        gate = jax.nn.sigmoid(hidden)
                    inner = grad * hidden if inner is None else inner + grad * hidden
                    grads.append(grad * gate)
            grads[0] = grads[0] + inner * gate * (1.0 - gate)
            for opening, closing in SPANS:
                for b in range(opening, closing):
                    total = entries[opening, b] * grads[opening]
                    for i in range(opening + 1, closing):
                        total = total + entries[i, b] * grads[i]
                    u_ref[t, b * 16:(b + 1) * 16, at] = total.astype(BF16)

    for t in range(NZ):
        edges(t)
    wide_u = jnp.concatenate([u_ref[t] for t in range(NZ)], axis=1)
    g_acc[...] = dot(wide_u, jnp.concatenate([oh[t] for t in range(NZ)], axis=1), NT)

    sums = g_acc[...]
    narrow = sums.astype(BF16)
    for h in range(2):
        sgt[h * 64 + 48:h * 64 + 64, :] = jnp.zeros((16, 256), F32)
    for l, (opening, closing) in enumerate(SPANS):
        total = jnp.zeros((16, 512), F32)
        for b in range(opening, closing):
            total = total + dot(narrow[b * 16:(b + 1) * 16], a_ref[:, b].reshape(128, 512))
        for h in range(2):
            sgt[h * 64 + l * 16:h * 64 + (l + 1) * 16, :] = total[:, h * 256:(h + 1) * 256]
    tall = jnp.transpose(sgt[...]).astype(BF16)
    for t in range(NZ):
        for s in range(2):
            first = s * 128 + t * 16
            sgbuf[t, s] = tall[first:first + 16]
    each(NZ, lambda d: remote(
        PH_SZ, 0, sgbuf.at[lax.rem(z + d, NZ)], sgrecv.at[z], device(dz=d)).start())
    sgrecv[z] = sgbuf[z]
    turned_sums = jnp.transpose(
        jnp.concatenate([sums, jnp.zeros((112, 128), F32)], axis=0)).astype(BF16)
    for t in range(NZ):
        gbuf[t] = turned_sums[t * 16:(t + 1) * 16]
    each(NZ, lambda d: remote(
        PH_GZ, 0, gbuf.at[lax.rem(z + d, NZ)], grecv.at[z], device(dz=d)).start())
    grecv[z] = gbuf[z]

    row, column = grid_of(192, 16)
    block, within = split48(row)
    expand[...] = one_hot(column == block * 4 + (within & 3))
    for t in range(NZ):
        row, column = grid_of(256, 128)
        fold[t] = one_hot(((column >> 4) == t) & ((row & 15) == (column & 15)))

    arrived(PH_SZ, 0, sgrecv.at[pl.ds(0, NZ - 1)])
    blocks = [sgrecv[t].reshape(32, 128).astype(F32) for t in range(NZ)]
    for l in range(3):
        for h in range(2):
            total = jnp.zeros((32, 128), F32)
            for t in range(NZ):
                total = jnp.where(slot == t, roll16(blocks[t], t - (h * 4 + l)), total)
            total = total.astype(BF16)
            sg4[2 * h, l] = total[0:16]
            sg4[2 * h + 1, l] = total[16:32]

    for k in (0, 4, 1, 3, 2):
        dy = NEAR[k]
        if dy:
            remote(PH_SYX, k, sg4.at[x], sgx.at[k, x], device(dy=dy)).start()
        else:
            sgx[k, x] = sg4[x]
        each(NX, lambda d: remote(
            PH_SYX, k, sg4.at[lax.rem(x + d, NX)], sgx.at[k, x], device(dy=dy, dx=d)).start())

    arrived(PH_GZ, 0, grecv.at[pl.ds(0, NZ - 1)])
    held = jnp.zeros((192, 128), F32)
    for t in range(NZ):
        wide = (dot(expand[...], grecv[t]) * same[...]).astype(BF16)
        held = held + dot(wide, fold[t])

    arrived(PH_SYX, 0, sgx.at[0])
    arrived(PH_SYX, 4, sgx.at[4])
    for h, k, hop in ((0, 0, -2), (1, 4, 2)):
        remote(PH_FW, 3 * h, sgx.at[k, halves[h]], forwarded.at[0, halves[h]], device(dy=hop)).start()
    for slot, k, hop in ((1, 4, 1), (2, 0, -1)):
        remote(PH_FW, slot, sgx.at[k], forwarded.at[slot], device(dy=hop)).start()

    arrived(PH_MC, 0, mc.at[pl.ds(0, NZ - 1)])
    coefficient = split48(lax.broadcasted_iota(I32, (192, 128), 0))[1] >> 2
    parts = jnp.zeros((192, 512), F32)
    for l, (opening, closing) in enumerate(SPANS):
        inside = (coefficient >= opening) & (coefficient < closing)
        maps = jnp.concatenate(
            [jnp.concatenate([mc[t, s, l] for t in range(NZ)], axis=0) for s in range(NX)], axis=0)
        parts = parts + dot(jnp.where(inside, held, 0.0).astype(BF16), maps, NT)
    for s in range(NX):
        gxbuf[s] = parts[s * 48:(s + 1) * 48].astype(BF16)
    each(NX, lambda d: remote(
        PH_GX, 0, gxbuf.at[lax.rem(x + d, NX)], gxrecv.at[d], device(dx=d)).start())
    gxrecv[0] = gxbuf[x]
    for k in (1, 2, 3):
        arrived(PH_SYX, k, sgx.at[k] if NEAR[k] else sgx.at[k, pl.ds(0, NX - 1)])
    for e in range(4):
        for s in range(NX):
            total = None
            for k, dy in enumerate(NEAR):
                term = share(-dy, (other_first if e < 2 else own_first) + e % 2) * sgx[k, s].astype(F32)
                total = term if total is None else total + term
            near_sum[e, s] = total
    arrived(PH_GX, 0, gxrecv.at[pl.ds(0, NX - 1)])
    total = gxrecv[0].astype(F32)
    for s in range(1, NX):
        total = total + gxrecv[s].astype(F32)
    for b in range(9):
        ga_ref[b] = total[b * 4:b * 4 + 4]

    for h in range(2):
        arrived(PH_FW, 3 * h, forwarded.at[0, halves[h]])
    for slot in (1, 2):
        arrived(PH_FW, slot, forwarded.at[slot])

    def expert_sum(e, expert, s):
        total = near_sum[e, s]
        for slot, dy in ((0, 4), (1, -3), (2, 3)):
            total = total + share(dy, expert) * forwarded[slot, s].astype(F32)
        return total

    for e in range(2):
        for s in range(NX):
            endbuf[e, s] = expert_sum(e, other_first + e, s).astype(BF16)
    end_copy = remote(PH_END, 0, endbuf, endrecv, device(other=True))
    end_copy.start()
    for e in range(2):
        for s in range(NX):
            ge_ref[e, :, :, s * 128:(s + 1) * 128] = expert_sum(e + 2, own_first + e, s)
    end_copy.wait_recv()
    for e in range(2):
        for s in range(NX):
            ge_ref[e, :, :, s * 128:(s + 1) * 128] += endrecv[e, s].astype(F32)

    core_copy.wait_send()
    end_copy.wait_send()
    for s in range(4):
        for way in range(2):
            for copy in z_hop(way, s):
                copy.wait_send()
    left(PH_AX, 0, a_ref.at[pl.ds(0, NZ - 1), pl.ds(0, NX - 1)])
    for phase, ref in ((PH_Y, ybuf), (PH_FW, forwarded)):
        for h in range(2):
            left(phase, 3 * h, ref.at[0, halves[h]])
        for slot in (1, 2):
            left(phase, slot, ref.at[slot])
    for k, dy in enumerate(NEAR):
        left(PH_YX, k, yxbuf.at[k] if dy else yxbuf.at[k, pl.ds(0, NX - 1)])
        left(PH_SYX, k, sg4 if dy else sg4.at[pl.ds(0, NX - 1)])
    left(PH_ATX, 0, atx.at[pl.ds(0, NX - 1)])
    left(PH_COX, 0, cox.at[pl.ds(0, NX - 1)])
    left(PH_GX, 0, gxbuf.at[pl.ds(0, NX - 1)])
    left(PH_COZ, 0, cobuf.at[pl.ds(0, NZ - 1)])
    left(PH_MZ, 0, mzbuf.at[pl.ds(0, NZ - 1)])
    left(PH_MC, 0, mc.at[pl.ds(0, NZ - 1)])
    left(PH_SZ, 0, sgbuf.at[pl.ds(0, NZ - 1)])
    left(PH_GZ, 0, gbuf.at[pl.ds(0, NZ - 1)])


def shards(
    atoms, cotangent, expert_weights, coefficients, src_owner, src_slot, tgt_slot, rot_index, rot_table
):
    hbm = pl.BlockSpec(memory_space=pltpu.HBM)
    vmem = pl.BlockSpec(memory_space=pltpu.VMEM)
    smem = pl.BlockSpec(memory_space=pltpu.SMEM)

    def b16(*shape):
        return pltpu.VMEM(shape, BF16)

    def f32(*shape):
        return pltpu.VMEM(shape, F32)

    grad_atoms, grad_experts = pl.pallas_call(
        kernel,
        out_shape=(
            jax.ShapeDtypeStruct((9, 4, 512), F32),
            jax.ShapeDtypeStruct((2, 3, 16, 512), F32),
        ),
        in_specs=[smem] + [hbm] * 8,
        out_specs=(vmem, vmem),
        scratch_shapes=[
            b16(2, 3, 16, 512),
            b16(2, 3, 16, 512),
            b16(9, 4, 512),
            b16(9, 4, 512),
            pltpu.VMEM((4, 1, 128), I32),
            f32(9, 9, 64),
            f32(40, 64),
            b16(3, NX, 3, 16, 128),
            b16(3, NX, 3, 16, 128),
            b16(5, NX, 3, 16, 128),
            b16(5, NX, 3, 16, 128),
            b16(NX, 3, 16, 128),
            b16(NZ, 2, 16, 128),
            b16(NZ, 2, 16, 128),
            b16(NZ, NX, 3, 16, 128),
            f32(1, 48, 512),
            b16(NX + 1, NX, 48, 128),
            b16(NZ, 9, 16, 512),
            f32(1, 48, 512),
            b16(2 * NX, 64, 128),
            b16(NZ, 3, 16, 128),
            b16(NZ, 3, 16, 128),
            b16(192, 16),
            b16(NZ, 256, 128),
            b16(NZ, 128, 256),
            b16(144, 192),
            b16(16, 192),
            f32(192, 256),
            b16(40, 128),
            b16(144, 128),
            b16(144, 128),
            f32(NZ, 144, 512),
            f32(2, 144, 512),
            f32(NZ, 144, 512),
            f32(NZ, 40, 512),
            b16(NZ + 4, 128, 512),
            b16(NZ, 144, 512),
            f32(144, 128),
            b16(NZ, 16, 256),
            b16(NZ, 16, 256),
            b16(NX, 48, 512),
            b16(NX, 48, 512),
            f32(128, 256),
            b16(NZ, 2, 16, 128),
            b16(NZ, 2, 16, 128),
            b16(NX, 3, 16, 128),
            b16(5, NX, 3, 16, 128),
            b16(3, NX, 3, 16, 128),
            f32(4, NX, 3, 16, 128),
            b16(2, NX, 3, 16, 128),
            b16(2, NX, 3, 16, 128),
            pltpu.SemaphoreType.DMA((8,)),
            pltpu.SemaphoreType.DMA((19, 5)),
            pltpu.SemaphoreType.DMA((19, 5)),
        ],
        compiler_params=pltpu.CompilerParams(
            collective_id=0, has_side_effects=True, vmem_limit_bytes=60 * 1024 * 1024
        ),
        cost_estimate=pl.CostEstimate(
            flops=2_000_000_000, bytes_accessed=1_000_000, transcendentals=65536
        ),
    )(
        coefficients, expert_weights, atoms[0].transpose(1, 0, 2), cotangent[0].transpose(1, 0, 2),
        src_owner.reshape(1, -1), src_slot, tgt_slot, rot_index, rot_table.transpose(1, 2, 0),
    )
    return grad_atoms.transpose(1, 0, 2)[None], grad_experts


def solution(mesh):
    placed = (
        P("grp", "graph", None, None),
        P("grp", "graph", None, None),
        P("grp", None, "graph", None),
        P(),
        P("grp", "graph", None),
        P("grp", "graph"),
        P("grp", "graph"),
        P("grp", "graph"),
        P(),
    )
    return jax.shard_map(
        shards,
        mesh=mesh,
        in_specs=placed,
        out_specs=(P("grp", "graph", None, None), P("grp", None, "graph", None)),
        check_vma=False,
    )
```

```python
import jax
import jax.numpy as jnp
from jax import lax
from jax.experimental import pallas as pl
from jax.experimental.pallas import tpu as pltpu
from jax.sharding import PartitionSpec as P

F32, BF16, I32 = jnp.float32, jnp.bfloat16, jnp.int32
NX, NZ, NY = 4, 8, 8
SPANS = ((0, 1), (1, 4), (4, 9))
DEGREE = (0, 1, 1, 1, 2, 2, 2, 2, 2)
MESH = pl.DeviceIdType.MESH
NN = (((1,), (0,)), ((), ()))
NT = (((1,), (1,)), ((), ()))

(PH_CORE, PH_Y, PH_YX, PH_ATX, PH_ATR, PH_ATL, PH_COX, PH_COZ, PH_MZ, PH_MC,
 PH_GZ, PH_GX, PH_SZ, PH_SYX, PH_FW, PH_END, PH_ATR1, PH_ATL1, PH_AX, PH_MCF) = range(20)
NEAR = (-2, -1, 0, 1, 2)
ENTRY = {}
for _opening, _closing in SPANS:
    for _i in range(_opening, _closing):
        for _b in range(_opening, _closing):
            ENTRY[_i, _b] = len(ENTRY)


def dot(a, b, dims=NN):
    return lax.dot_general(a, b, dims, preferred_element_type=F32)


def one_hot(test):
    return jnp.where(test, 1.0, 0.0).astype(BF16)


def grid_of(rows, columns):
    shape = (rows, columns)
    return lax.broadcasted_iota(I32, shape, 0), lax.broadcasted_iota(I32, shape, 1)


def roll16(block, by):
    by = by * 16 % 128
    return pltpu.roll(block, by, 1) if by else block


def split48(index):
    block = jnp.where(index >= 48, 1, 0) + jnp.where(index >= 96, 1, 0) + jnp.where(index >= 144, 1, 0)
    return block, index - 48 * block


def kernel(
    coef, w_hbm, at_hbm, co_hbm, owner_hbm, slot_hbm, tslot_hbm, turn_hbm, rt_hbm,
    ga_ref, ge_ref,
    w_own, w_sib, at_in, co_in, index_in, rt_in, rt35,
    ybuf, yrecv, yxbuf, yxrecv, mx, mzbuf, wc, mc,
    at48, atx, a_ref, co80, cox, cobuf, corecv,
    expand, fold, spread, order, gather16, same, rot2,
    hs, cs, hh, ch, grads_at, turns, oh, u_ref, g_acc, gbuf, grecv, gxbuf, gxrecv,
    sgt, sgbuf, sgrecv, sg4, sgx, forwarded, near_sum, endbuf, endrecv,
    load_sem, send_sem, recv_sem,
):
    grp, graph = lax.axis_index("grp"), lax.axis_index("graph")
    y, core = lax.div(grp, 2), lax.rem(grp, 2)
    x, z = lax.div(graph, NZ), lax.rem(graph, NZ)

    def device(dy=None, dx=None, dz=None, other=False):
        along = y if dy is None else lax.rem(y + dy + NY, NY)
        across = x if dx is None else lax.rem(x + dx, NX)
        up = z if dz is None else lax.rem(z + dz, NZ)
        return {"grp": along * 2 + (1 - core if other else core), "graph": across * NZ + up}

    def remote(phase, slot, source, target, place):
        return pltpu.make_async_remote_copy(
            src_ref=source, dst_ref=target, send_sem=send_sem.at[phase, slot],
            recv_sem=recv_sem.at[phase, slot], device_id=place, device_id_type=MESH,
        )

    def each(count, body):
        for d in range(1, count):
            body(d)

    def arrived(phase, slot, ref):
        pltpu.make_async_copy(ref, ref, recv_sem.at[phase, slot]).wait()

    def left(phase, slot, ref):
        pltpu.make_async_copy(ref, ref, send_sem.at[phase, slot]).wait()

    loads = [
        pltpu.make_async_copy(source, target, load_sem.at[k])
        for k, (source, target) in enumerate((
            (w_hbm, w_own), (at_hbm, at_in), (co_hbm, co_in), (owner_hbm, index_in.at[0]),
            (slot_hbm, index_in.at[1]), (tslot_hbm, index_in.at[2]), (turn_hbm, index_in.at[3]),
            (rt_hbm, rt_in)))
    ]
    for load in loads:
        load.start()

    barrier = pltpu.get_barrier_semaphore()

    def greet(place):
        pl.semaphore_signal(barrier, inc=1, device_id=place, device_id_type=MESH)

    greet(device(other=True))
    for dy in NEAR:
        if dy:
            greet(device(dy=dy))
        each(NX, lambda d: greet(device(dy=dy, dx=d)))
    each(NZ, lambda d: greet(device(dz=d)))

    loads[0].wait()
    pl.semaphore_wait(barrier, 1 + 4 + 5 * (NX - 1) + (NZ - 1))

    core_copy = remote(PH_CORE, 0, w_own, w_sib, device(other=True))
    core_copy.start()

    for load in loads[1:]:
        load.wait()

    for b in range(9):
        co80[0, b * 4:b * 4 + 4, :] = co_in[b].astype(F32)
        at48[0, b * 4:b * 4 + 4, :] = at_in[b].astype(F32)
    at48[0, 36:48, :] = jnp.zeros((12, 512), F32)
    co80[0, 36:48, :] = jnp.zeros((12, 512), F32)

    def place(owner, slot):
        return (owner & 7) * 16 + (owner >> 3) * 4 + slot

    row = lax.broadcasted_iota(I32, (16, 128), 0)
    codes = jnp.where(row == x * 4, place(index_in[0], index_in[1]), 0)
    codes = jnp.where(row == x * 4 + 1, place(graph, index_in[2]), codes)
    codes = jnp.where(row == x * 4 + 2, index_in[3], codes).astype(F32).astype(BF16)
    for xb in range(NX):
        at = slice(xb * 128, (xb + 1) * 128)
        atx_out = at48[0, :, at].astype(BF16)
        cox_out = co80[0, :, at].astype(BF16)
        atx[NX, xb] = atx_out
        cox[NX + xb, 0:48, :] = cox_out
        cox[NX + xb, 48:64, :] = codes

    each(NX, lambda d: remote(PH_ATX, 0, atx.at[NX], atx.at[x], device(dx=d)).start())
    each(NX, lambda d: remote(
        PH_COX, 0, cox.at[NX + lax.rem(x + d, NX)], cox.at[x], device(dx=d)).start())
    atx[x] = atx[NX]
    cox[x] = cox[NX + x]

    row, column = grid_of(144, 192)
    block, within = split48(column)
    order[...] = one_hot(
        ((within >> 2) == (row >> 4)) & (((row >> 2) & 3) == block) & ((within & 3) == (row & 3)))
    row, column = grid_of(16, 192)
    block, within = split48(column)
    gather16[...] = one_hot(row == block * 4 + (within & 3))
    row, column = grid_of(192, 256)
    block, within = split48(row)
    same[...] = jnp.where((within >> 2) == (column >> 4), 1.0, 0.0)
    for t in range(NZ):
        row, column = grid_of(128, 256)
        spread[t] = one_hot(((row >> 4) == t) & ((row & 15) == (column & 15)))

    core_copy.wait_recv()

    def share(dy, expert):
        return coef[lax.rem(y + dy + NY, NY) * 2 + core, expert].astype(F32) * (1.0 / 1024.0)

    own_first, other_first = grp * 2, (y * 2 + 1 - core) * 2

    def partial_of(dy, xb):
        at = slice(xb * 128, (xb + 1) * 128)
        total = None
        for ref, first in ((w_own, own_first), (w_sib, other_first)):
            for e in range(2):
                term = share(dy, first + e) * ref[e, :, :, at].astype(F32)
                total = term if total is None else total + term
        return total

    halves = (pl.ds(0, 2), pl.ds(2, 2))
    for xb in range(NX):
        ybuf[0, xb] = partial_of(-4, xb).astype(BF16)
        if xb % 2:
            h = xb // 2
            remote(PH_Y, 3 * h, ybuf.at[0, halves[h]], yrecv.at[0, halves[h]],
                   device(dy=(-2, 2)[h])).start()
    for slot, dy, hop in ((1, 3, 1), (2, -3, -1)):
        for xb in range(NX):
            ybuf[slot, xb] = partial_of(dy, xb).astype(BF16)
        remote(PH_Y, slot, ybuf.at[slot], yrecv.at[slot], device(dy=hop)).start()

    def yx_send(k):
        dy = NEAR[k]
        if dy:
            remote(PH_YX, k, yxbuf.at[k, x], yxrecv.at[k, x], device(dy=dy)).start()
        else:
            yxrecv[k, x] = yxbuf[k, x]
        each(NX, lambda d: remote(
            PH_YX, k, yxbuf.at[k, lax.rem(x + d, NX)], yxrecv.at[k, x], device(dy=dy, dx=d)).start())

    for k in (1, 3, 2):
        for xb in range(NX):
            yxbuf[k, xb] = partial_of(NEAR[k], xb).astype(BF16)
        yx_send(k)

    arrived(PH_ATX, 0, atx.at[pl.ds(0, NX - 1)])
    for xb in range(NX):
        stacked = jnp.concatenate([atx[s, xb] for s in range(NX)], axis=0)
        a_ref[z, :, :, xb * 128:(xb + 1) * 128] = dot(order[...], stacked).astype(BF16).reshape(9, 16, 128)

    def z_hop(way, s):
        slot = lax.rem(z + (s if way else NZ - s), NZ)
        common = pl.ds(0, 5) if s < 3 else (pl.ds(3, 2) if way else pl.ds(0, 3))
        parts = [(PH_ATL if way else PH_ATR, common)]
        if s < 3 or way:
            parts.append((PH_ATL1 if way else PH_ATR1, pl.ds(5 + x, 1)))
        return [
            remote(phase, s, a_ref.at[slot, part], a_ref.at[slot, part], device(dz=NZ - 1 if way else 1))
            for phase, part in parts
        ]

    def along_x(slot):
        block = a_ref.at[slot, pl.ds(5 + x, 1)]
        each(NX, lambda d: remote(PH_AX, 0, block, block, device(dx=d)).start())

    for way in range(2):
        for copy in z_hop(way, 0):
            copy.start()

    arrived(PH_COX, 0, cox.at[pl.ds(0, NX - 1)])
    stacked = jnp.concatenate([cox[s, 0:48] for s in range(NX)], axis=0)
    codes = cox[0, 48:64].astype(F32)
    for s in range(1, NX):
        codes = codes + cox[s, 48:64].astype(F32)
    codes = codes.astype(BF16)
    for t in range(NZ):
        wide = (dot(stacked, spread[t]) * same[...]).astype(BF16)
        packed = dot(gather16[...], wide).astype(BF16)
        cobuf[t, 0] = packed[:, 0:128]
        cobuf[t, 1] = packed[:, 128:256]
        cobuf[t, 2] = codes
    each(NZ, lambda d: remote(
        PH_COZ, 0, cobuf.at[lax.rem(z + d, NZ)], corecv.at[z], device(dz=d)).start())
    corecv[z] = cobuf[z]

    for h in range(2):
        arrived(PH_Y, 3 * h, yrecv.at[0, halves[h]])
    for slot in (1, 2):
        arrived(PH_Y, slot, yrecv.at[slot])
    for k, dy, slot in ((0, -2, 2), (4, 2, 1)):
        for xb in range(NX):
            total = partial_of(dy, xb) + yrecv[slot, xb].astype(F32)
            if (xb >= 2) == (k == 4):
                total = total + yrecv[0, xb].astype(F32)
            yxbuf[k, xb] = total.astype(BF16)
        yx_send(k)

    for i in range(9):
        opening, closing = SPANS[DEGREE[i]]
        first = ENTRY[i, opening]
        rt35[first:first + closing - opening, :] = rt_in[i, opening:closing, :]
    rt35[35:40, :] = jnp.zeros((5, 64), F32)
    table = rt35[...]
    high = table.astype(BF16)
    rot2[:, 0:64] = high
    rot2[:, 64:128] = (table - high.astype(F32)).astype(BF16)

    arrived(PH_COZ, 0, corecv.at[pl.ds(0, NZ - 1)])
    for half in range(2):
        tall = jnp.transpose(corecv[:, half].reshape(128, 128).astype(F32)).astype(BF16)
        rows = 128 if half == 0 else 16
        cs[half * 128:half * 128 + rows, :] = tall[0:rows]

    def turned(entries, values, opening, closing, i):
        total = entries[i, opening] * values(opening)
        for b in range(opening + 1, closing):
            total = total + entries[i, b] * values(b)
        return total

    def entries_of(t, at):
        return {key: turns[t, k:k + 1, at] for key, k in ENTRY.items()}

    def prepare(t):
        lanes = lax.broadcasted_iota(I32, (128, 128), 0).astype(F32)
        folded = (lax.broadcasted_iota(I32, (128, 128), 0) & 63).astype(F32)
        for q in range(NX):
            at = slice(q * 128, (q + 1) * 128)
            codes = corecv[t, 2].astype(F32)
            oh[t, :, at] = one_hot(lanes == codes[q * 4:q * 4 + 1])
            oh[NZ + t % 2, :, at] = one_hot(lanes == codes[q * 4 + 1:q * 4 + 2])
            oh[NZ + 2 + t % 2, :, at] = one_hot(folded == codes[q * 4 + 2:q * 4 + 3])
        ch[t % 2] = dot(cs[...], oh[NZ + t % 2])
        turns[t] = dot(rot2[...], oh[NZ + 2 + t % 2])
        for q in range(NX):
            at = slice(q * 128, (q + 1) * 128)
            entries = entries_of(t, at)
            for opening, closing in SPANS:
                for i in range(opening, closing):
                    grads_at[t, i * 16:(i + 1) * 16, at] = turned(
                        entries, lambda b: ch[t % 2, b * 16:(b + 1) * 16, at], opening, closing, i)

    def pass_on(s):
        for way in range(2):
            for copy in z_hop(way, s - 1):
                copy.wait_recv()
            for copy in z_hop(way, s):
                copy.start()
            along_x(lax.rem(z + (s if way else NZ - s), NZ))

    pass_on(1)
    for t in range(0, 3):
        prepare(t)

    for k, dy in enumerate(NEAR):
        arrived(PH_YX, k, yxrecv.at[k] if dy else yxrecv.at[k, pl.ds(0, NX - 1)])
    lane_slot = lax.broadcasted_iota(I32, (32, 128), 1) >> 4
    packed = [jnp.zeros((32, 128), F32) for t in range(NZ)]
    for l in range(3):
        for s in range(NX):
            total = yxrecv[0, s, l].astype(F32)
            for k in range(1, 5):
                total = total + yxrecv[k, s, l].astype(F32)
            mx[s, l] = total.astype(BF16)
        for h in range(2):
            block = mx[2 * h:2 * h + 2, l].reshape(32, 128).astype(F32)
            for t in range(NZ):
                shifted = roll16(block, h * 4 + l - t)
                packed[t] = jnp.where(lane_slot == h * 4 + l, shifted, packed[t])
    for t in range(NZ):
        mzbuf[t] = packed[t].astype(BF16).reshape(2, 16, 128)
    each(NZ, lambda d: remote(
        PH_MZ, 0, mzbuf.at[lax.rem(z + d, NZ)], wc.at[z], device(dz=d)).start())
    wc[z] = mzbuf[z]
    mc[z] = mx[...]
    pass_on(2)
    for t in range(3, 5):
        prepare(t)
    pass_on(3)
    for t in range(5, 8):
        prepare(t)
    for way in (1, 0):
        for copy in z_hop(way, 3):
            copy.wait_recv()
        if way:
            along_x(lax.rem(z + 4, NZ))
    arrived(PH_AX, 0, a_ref.at[pl.ds(0, NZ - 1), pl.ds(0, NX - 1)])
    arrived(PH_MZ, 0, wc.at[pl.ds(0, NZ - 1)])
    for k, dz in enumerate(NEAR):
        if dz:
            remote(PH_MC, k, mx, mc.at[z], device(dz=NZ + dz)).start()

    columns16 = jnp.concatenate(
        [jnp.concatenate([wc[t, s] for t in range(NZ)], axis=0) for s in range(2)], axis=0)
    flipped = jnp.transpose(columns16.astype(F32)).astype(BF16)
    for b in range(9):
        l = DEGREE[b]
        maps = jnp.concatenate([flipped[h * 64 + l * 16:h * 64 + (l + 1) * 16] for h in range(2)], axis=1)
        hs[b * 16:(b + 1) * 16, :] = dot(maps, a_ref[:, b].reshape(128, 512), NT).astype(BF16)


    def edges(t):
        hh[t] = dot(hs[...], oh[t])
        for q in range(NX):
            at = slice(q * 128, (q + 1) * 128)
            entries = entries_of(t, at)
            grads, inner, gate = [], None, None
            for opening, closing in SPANS:
                for i in range(opening, closing):
                    hidden = turned(entries, lambda b: hh[t, b * 16:(b + 1) * 16, at], opening, closing, i)
                    grad = grads_at[t, i * 16:(i + 1) * 16, at]
                    if i == 0:
                        gate = jax.nn.sigmoid(hidden)
                    inner = grad * hidden if inner is None else inner + grad * hidden
                    grads.append(grad * gate)
            grads[0] = grads[0] + inner * gate * (1.0 - gate)
            for opening, closing in SPANS:
                for b in range(opening, closing):
                    total = entries[opening, b] * grads[opening]
                    for i in range(opening + 1, closing):
                        total = total + entries[i, b] * grads[i]
                    u_ref[t, b * 16:(b + 1) * 16, at] = total.astype(BF16)

    for t in range(NZ):
        edges(t)
    wide_u = jnp.concatenate([u_ref[t] for t in range(NZ)], axis=1)
    g_acc[...] = dot(wide_u, jnp.concatenate([oh[t] for t in range(NZ)], axis=1), NT)

    sums = g_acc[...]
    narrow = sums.astype(BF16)
    for h in range(2):
        sgt[h * 64 + 48:h * 64 + 64, :] = jnp.zeros((16, 256), F32)
    for l, (opening, closing) in enumerate(SPANS):
        total = jnp.zeros((16, 512), F32)
        for b in range(opening, closing):
            total = total + dot(narrow[b * 16:(b + 1) * 16], a_ref[:, b].reshape(128, 512))
        for h in range(2):
            sgt[h * 64 + l * 16:h * 64 + (l + 1) * 16, :] = total[:, h * 256:(h + 1) * 256]
    tall = jnp.transpose(sgt[...]).astype(BF16)
    for t in range(NZ):
        for s in range(2):
            first = s * 128 + t * 16
            sgbuf[t, s] = tall[first:first + 16]
    each(NZ, lambda d: remote(
        PH_SZ, 0, sgbuf.at[lax.rem(z + d, NZ)], sgrecv.at[z], device(dz=d)).start())
    sgrecv[z] = sgbuf[z]
    turned_sums = jnp.transpose(
        jnp.concatenate([sums, jnp.zeros((112, 128), F32)], axis=0)).astype(BF16)
    for t in range(NZ):
        gbuf[t] = turned_sums[t * 16:(t + 1) * 16]
    each(NZ, lambda d: remote(
        PH_GZ, 0, gbuf.at[lax.rem(z + d, NZ)], grecv.at[z], device(dz=d)).start())
    grecv[z] = gbuf[z]

    below, above = mc.at[lax.rem(z + NZ - 2, NZ)], mc.at[lax.rem(z + 2, NZ)]
    arrived(PH_MC, 4, below)
    arrived(PH_MC, 0, above)
    for k, ref, dz in (
        (0, below, 1), (1, above, NZ - 1), (2, below.at[halves[0]], 2), (3, above.at[halves[1]], NZ - 2),
    ):
        remote(PH_MCF, k, ref, ref, device(dz=dz)).start()

    row, column = grid_of(192, 16)
    block, within = split48(row)
    expand[...] = one_hot(column == block * 4 + (within & 3))
    for t in range(NZ):
        row, column = grid_of(256, 128)
        fold[t] = one_hot(((column >> 4) == t) & ((row & 15) == (column & 15)))

    arrived(PH_SZ, 0, sgrecv.at[pl.ds(0, NZ - 1)])
    blocks = [sgrecv[t].reshape(32, 128).astype(F32) for t in range(NZ)]
    for l in range(3):
        for h in range(2):
            total = jnp.zeros((32, 128), F32)
            for t in range(NZ):
                total = jnp.where(lane_slot == t, roll16(blocks[t], t - (h * 4 + l)), total)
            total = total.astype(BF16)
            sg4[2 * h, l] = total[0:16]
            sg4[2 * h + 1, l] = total[16:32]

    for k in (0, 4, 1, 3, 2):
        dy = NEAR[k]
        if dy:
            remote(PH_SYX, k, sg4.at[x], sgx.at[k, x], device(dy=dy)).start()
        else:
            sgx[k, x] = sg4[x]
        each(NX, lambda d: remote(
            PH_SYX, k, sg4.at[lax.rem(x + d, NX)], sgx.at[k, x], device(dy=dy, dx=d)).start())

    arrived(PH_GZ, 0, grecv.at[pl.ds(0, NZ - 1)])
    held = jnp.zeros((192, 128), F32)
    for t in range(NZ):
        wide = (dot(expand[...], grecv[t]) * same[...]).astype(BF16)
        held = held + dot(wide, fold[t])

    arrived(PH_SYX, 0, sgx.at[0])
    arrived(PH_SYX, 4, sgx.at[4])
    for h, k, hop in ((0, 0, -2), (1, 4, 2)):
        remote(PH_FW, 3 * h, sgx.at[k, halves[h]], forwarded.at[0, halves[h]], device(dy=hop)).start()
    for slot, k, hop in ((1, 4, 1), (2, 0, -1)):
        remote(PH_FW, slot, sgx.at[k], forwarded.at[slot], device(dy=hop)).start()

    for k, dz in ((1, 1), (3, -1)):
        arrived(PH_MC, k, mc.at[lax.rem(z + NZ + dz, NZ)])
    arrived(PH_MCF, 0, mc.at[lax.rem(z + NZ - 3, NZ)])
    arrived(PH_MCF, 1, mc.at[lax.rem(z + 3, NZ)])
    for h in range(2):
        arrived(PH_MCF, 2 + h, mc.at[lax.rem(z + 4, NZ), halves[h]])
    coefficient = split48(lax.broadcasted_iota(I32, (192, 128), 0))[1] >> 2
    parts = jnp.zeros((192, 512), F32)
    for l, (opening, closing) in enumerate(SPANS):
        inside = (coefficient >= opening) & (coefficient < closing)
        maps = jnp.concatenate(
            [jnp.concatenate([mc[t, s, l] for t in range(NZ)], axis=0) for s in range(NX)], axis=0)
        parts = parts + dot(jnp.where(inside, held, 0.0).astype(BF16), maps, NT)
    for s in range(NX):
        gxbuf[s] = parts[s * 48:(s + 1) * 48].astype(BF16)
    each(NX, lambda d: remote(
        PH_GX, 0, gxbuf.at[lax.rem(x + d, NX)], gxrecv.at[d], device(dx=d)).start())
    gxrecv[0] = gxbuf[x]
    for k in (1, 2, 3):
        arrived(PH_SYX, k, sgx.at[k] if NEAR[k] else sgx.at[k, pl.ds(0, NX - 1)])
    for e in range(4):
        for s in range(NX):
            total = None
            for k, dy in enumerate(NEAR):
                term = share(-dy, (other_first if e < 2 else own_first) + e % 2) * sgx[k, s].astype(F32)
                total = term if total is None else total + term
            near_sum[e, s] = total
    arrived(PH_GX, 0, gxrecv.at[pl.ds(0, NX - 1)])
    total = gxrecv[0].astype(F32)
    for s in range(1, NX):
        total = total + gxrecv[s].astype(F32)
    for b in range(9):
        ga_ref[b] = total[b * 4:b * 4 + 4]

    for h in range(2):
        arrived(PH_FW, 3 * h, forwarded.at[0, halves[h]])
    for slot in (1, 2):
        arrived(PH_FW, slot, forwarded.at[slot])

    def expert_sum(e, expert, s):
        total = near_sum[e, s]
        for slot, dy in ((0, 4), (1, -3), (2, 3)):
            total = total + share(dy, expert) * forwarded[slot, s].astype(F32)
        return total

    for e in range(2):
        for s in range(NX):
            endbuf[e, s] = expert_sum(e, other_first + e, s).astype(BF16)
    end_copy = remote(PH_END, 0, endbuf, endrecv, device(other=True))
    end_copy.start()
    for e in range(2):
        for s in range(NX):
            ge_ref[e, :, :, s * 128:(s + 1) * 128] = expert_sum(e + 2, own_first + e, s)
    end_copy.wait_recv()
    for e in range(2):
        for s in range(NX):
            ge_ref[e, :, :, s * 128:(s + 1) * 128] += endrecv[e, s].astype(F32)

    core_copy.wait_send()
    end_copy.wait_send()
    for s in range(4):
        for way in range(2):
            for copy in z_hop(way, s):
                copy.wait_send()
    left(PH_AX, 0, a_ref.at[pl.ds(0, NZ - 1), pl.ds(0, NX - 1)])
    for phase, ref in ((PH_Y, ybuf), (PH_FW, forwarded)):
        for h in range(2):
            left(phase, 3 * h, ref.at[0, halves[h]])
        for slot in (1, 2):
            left(phase, slot, ref.at[slot])
    for k, dy in enumerate(NEAR):
        left(PH_YX, k, yxbuf.at[k] if dy else yxbuf.at[k, pl.ds(0, NX - 1)])
        left(PH_SYX, k, sg4 if dy else sg4.at[pl.ds(0, NX - 1)])
    left(PH_ATX, 0, atx.at[pl.ds(0, NX - 1)])
    left(PH_COX, 0, cox.at[pl.ds(0, NX - 1)])
    left(PH_GX, 0, gxbuf.at[pl.ds(0, NX - 1)])
    left(PH_COZ, 0, cobuf.at[pl.ds(0, NZ - 1)])
    left(PH_MZ, 0, mzbuf.at[pl.ds(0, NZ - 1)])
    for k in (0, 1, 3, 4):
        left(PH_MC, k, mx)
    for slot, ref in enumerate((mx, mx, mx.at[halves[0]], mx.at[halves[1]])):
        left(PH_MCF, slot, ref)
    left(PH_SZ, 0, sgbuf.at[pl.ds(0, NZ - 1)])
    left(PH_GZ, 0, gbuf.at[pl.ds(0, NZ - 1)])


def shards(
    atoms, cotangent, expert_weights, coefficients, src_owner, src_slot, tgt_slot, rot_index, rot_table
):
    hbm = pl.BlockSpec(memory_space=pltpu.HBM)
    vmem = pl.BlockSpec(memory_space=pltpu.VMEM)
    smem = pl.BlockSpec(memory_space=pltpu.SMEM)

    def b16(*shape):
        return pltpu.VMEM(shape, BF16)

    def f32(*shape):
        return pltpu.VMEM(shape, F32)

    grad_atoms, grad_experts = pl.pallas_call(
        kernel,
        out_shape=(
            jax.ShapeDtypeStruct((9, 4, 512), F32),
            jax.ShapeDtypeStruct((2, 3, 16, 512), F32),
        ),
        in_specs=[smem] + [hbm] * 8,
        out_specs=(vmem, vmem),
        scratch_shapes=[
            b16(2, 3, 16, 512),
            b16(2, 3, 16, 512),
            b16(9, 4, 512),
            b16(9, 4, 512),
            pltpu.VMEM((4, 1, 128), I32),
            f32(9, 9, 64),
            f32(40, 64),
            b16(3, NX, 3, 16, 128),
            b16(3, NX, 3, 16, 128),
            b16(5, NX, 3, 16, 128),
            b16(5, NX, 3, 16, 128),
            b16(NX, 3, 16, 128),
            b16(NZ, 2, 16, 128),
            b16(NZ, 2, 16, 128),
            b16(NZ, NX, 3, 16, 128),
            f32(1, 48, 512),
            b16(NX + 1, NX, 48, 128),
            b16(NZ, 9, 16, 512),
            f32(1, 48, 512),
            b16(2 * NX, 64, 128),
            b16(NZ, 3, 16, 128),
            b16(NZ, 3, 16, 128),
            b16(192, 16),
            b16(NZ, 256, 128),
            b16(NZ, 128, 256),
            b16(144, 192),
            b16(16, 192),
            f32(192, 256),
            b16(40, 128),
            b16(144, 128),
            b16(144, 128),
            f32(NZ, 144, 512),
            f32(2, 144, 512),
            f32(NZ, 144, 512),
            f32(NZ, 40, 512),
            b16(NZ + 4, 128, 512),
            b16(NZ, 144, 512),
            f32(144, 128),
            b16(NZ, 16, 256),
            b16(NZ, 16, 256),
            b16(NX, 48, 512),
            b16(NX, 48, 512),
            f32(128, 256),
            b16(NZ, 2, 16, 128),
            b16(NZ, 2, 16, 128),
            b16(NX, 3, 16, 128),
            b16(5, NX, 3, 16, 128),
            b16(3, NX, 3, 16, 128),
            f32(4, NX, 3, 16, 128),
            b16(2, NX, 3, 16, 128),
            b16(2, NX, 3, 16, 128),
            pltpu.SemaphoreType.DMA((8,)),
            pltpu.SemaphoreType.DMA((20, 5)),
            pltpu.SemaphoreType.DMA((20, 5)),
        ],
        compiler_params=pltpu.CompilerParams(
            collective_id=0, has_side_effects=True, vmem_limit_bytes=60 * 1024 * 1024
        ),
        cost_estimate=pl.CostEstimate(
            flops=2_000_000_000, bytes_accessed=1_000_000, transcendentals=65536
        ),
    )(
        coefficients, expert_weights, atoms[0].transpose(1, 0, 2), cotangent[0].transpose(1, 0, 2),
        src_owner.reshape(1, -1), src_slot, tgt_slot, rot_index, rot_table.transpose(1, 2, 0),
    )
    return grad_atoms.transpose(1, 0, 2)[None], grad_experts


def solution(mesh):
    placed = (
        P("grp", "graph", None, None),
        P("grp", "graph", None, None),
        P("grp", None, "graph", None),
        P(),
        P("grp", "graph", None),
        P("grp", "graph"),
        P("grp", "graph"),
        P("grp", "graph"),
        P(),
    )
    return jax.shard_map(
        shards,
        mesh=mesh,
        in_specs=placed,
        out_specs=(P("grp", "graph", None, None), P("grp", None, "graph", None)),
        check_vma=False,
    )
```

```python
import jax
import jax.numpy as jnp
from jax import lax
from jax.experimental import pallas as pl
from jax.experimental.pallas import tpu as pltpu
from jax.sharding import PartitionSpec as P

F32, BF16, I32 = jnp.float32, jnp.bfloat16, jnp.int32
NX, NZ, NY = 4, 8, 8
SPANS = ((0, 1), (1, 4), (4, 9))
DEGREE = (0, 1, 1, 1, 2, 2, 2, 2, 2)
MESH = pl.DeviceIdType.MESH
NN = (((1,), (0,)), ((), ()))
NT = (((1,), (1,)), ((), ()))

(PH_CORE, PH_Y, PH_YX, PH_ATX, PH_ATR, PH_ATL, PH_COX, PH_COZ, PH_MZ, PH_MC,
 PH_GZ, PH_GX, PH_SZ, PH_SYX, PH_FW, PH_END, PH_ATR1, PH_ATL1, PH_AX, PH_MCF) = range(20)
NEAR = (-2, -1, 0, 1, 2)
ENTRY = {}
for _opening, _closing in SPANS:
    for _i in range(_opening, _closing):
        for _b in range(_opening, _closing):
            ENTRY[_i, _b] = len(ENTRY)


def dot(a, b, dims=NN):
    return lax.dot_general(a, b, dims, preferred_element_type=F32)


def one_hot(test):
    return jnp.where(test, 1.0, 0.0).astype(BF16)


def grid_of(rows, columns):
    shape = (rows, columns)
    return lax.broadcasted_iota(I32, shape, 0), lax.broadcasted_iota(I32, shape, 1)


def roll16(block, by):
    by = by * 16 % 128
    return pltpu.roll(block, by, 1) if by else block


def split48(index):
    block = jnp.where(index >= 48, 1, 0) + jnp.where(index >= 96, 1, 0) + jnp.where(index >= 144, 1, 0)
    return block, index - 48 * block


def kernel(
    coef, w_hbm, at_hbm, co_hbm, owner_hbm, slot_hbm, tslot_hbm, turn_hbm, rt_hbm,
    ga_ref, ge_ref,
    w_own, w_sib, at_in, co_in, index_in, rt_in, rt35,
    ybuf, yrecv, yxbuf, yxrecv, mx, mzbuf, wc, mc,
    at48, atx, a_ref, co80, cox, cobuf, corecv,
    expand, fold, spread, order, gather16, same, rot2,
    hs, cs, hh, ch, grads_at, turns, oh, u_ref, g_acc, gbuf, grecv, gxbuf, gxrecv,
    sgt, sgbuf, sgrecv, sg4, sgx, forwarded, near_sum, endbuf, endrecv,
    load_sem, send_sem, recv_sem,
):
    grp, graph = lax.axis_index("grp"), lax.axis_index("graph")
    y, core = lax.div(grp, 2), lax.rem(grp, 2)
    x, z = lax.div(graph, NZ), lax.rem(graph, NZ)

    def device(dy=None, dx=None, dz=None, other=False):
        along = y if dy is None else lax.rem(y + dy + NY, NY)
        across = x if dx is None else lax.rem(x + dx, NX)
        up = z if dz is None else lax.rem(z + dz, NZ)
        return {"grp": along * 2 + (1 - core if other else core), "graph": across * NZ + up}

    def remote(phase, slot, source, target, place):
        return pltpu.make_async_remote_copy(
            src_ref=source, dst_ref=target, send_sem=send_sem.at[phase, slot],
            recv_sem=recv_sem.at[phase, slot], device_id=place, device_id_type=MESH,
        )

    def each(count, body):
        for d in range(1, count):
            body(d)

    def arrived(phase, slot, ref):
        pltpu.make_async_copy(ref, ref, recv_sem.at[phase, slot]).wait()

    def left(phase, slot, ref):
        pltpu.make_async_copy(ref, ref, send_sem.at[phase, slot]).wait()

    loads = [
        pltpu.make_async_copy(source, target, load_sem.at[k])
        for k, (source, target) in enumerate((
            (w_hbm, w_own), (at_hbm, at_in), (co_hbm, co_in), (owner_hbm, index_in.at[0]),
            (slot_hbm, index_in.at[1]), (tslot_hbm, index_in.at[2]), (turn_hbm, index_in.at[3]),
            (rt_hbm, rt_in)))
    ]
    for load in loads:
        load.start()

    barrier = pltpu.get_barrier_semaphore()

    def greet(place):
        pl.semaphore_signal(barrier, inc=1, device_id=place, device_id_type=MESH)

    greet(device(other=True))
    for dy in NEAR:
        if dy:
            greet(device(dy=dy))
        each(NX, lambda d: greet(device(dy=dy, dx=d)))
    each(NZ, lambda d: greet(device(dz=d)))

    loads[0].wait()
    pl.semaphore_wait(barrier, 1 + 4 + 5 * (NX - 1) + (NZ - 1))

    core_copy = remote(PH_CORE, 0, w_own, w_sib, device(other=True))
    core_copy.start()

    for load in loads[1:]:
        load.wait()

    for b in range(9):
        co80[0, b * 4:b * 4 + 4, :] = co_in[b].astype(F32)
        at48[0, b * 4:b * 4 + 4, :] = at_in[b].astype(F32)
    at48[0, 36:48, :] = jnp.zeros((12, 512), F32)
    co80[0, 36:48, :] = jnp.zeros((12, 512), F32)

    def place(owner, slot):
        return (owner & 7) * 16 + (owner >> 3) * 4 + slot

    row = lax.broadcasted_iota(I32, (16, 128), 0)
    codes = jnp.where(row == x * 4, place(index_in[0], index_in[1]), 0)
    codes = jnp.where(row == x * 4 + 1, place(graph, index_in[2]), codes)
    codes = jnp.where(row == x * 4 + 2, index_in[3], codes).astype(F32).astype(BF16)
    for xb in range(NX):
        at = slice(xb * 128, (xb + 1) * 128)
        atx_out = at48[0, :, at].astype(BF16)
        cox_out = co80[0, :, at].astype(BF16)
        atx[NX, xb] = atx_out
        cox[NX + xb, 0:48, :] = cox_out
        cox[NX + xb, 48:64, :] = codes

    each(NX, lambda d: remote(PH_ATX, 0, atx.at[NX], atx.at[x], device(dx=d)).start())
    each(NX, lambda d: remote(
        PH_COX, 0, cox.at[NX + lax.rem(x + d, NX)], cox.at[x], device(dx=d)).start())
    atx[x] = atx[NX]
    cox[x] = cox[NX + x]

    row, column = grid_of(144, 192)
    block, within = split48(column)
    order[...] = one_hot(
        ((within >> 2) == (row >> 4)) & (((row >> 2) & 3) == block) & ((within & 3) == (row & 3)))
    row, column = grid_of(16, 192)
    block, within = split48(column)
    gather16[...] = one_hot(row == block * 4 + (within & 3))
    row, column = grid_of(192, 256)
    block, within = split48(row)
    same[...] = jnp.where((within >> 2) == (column >> 4), 1.0, 0.0)
    for t in range(NZ):
        row, column = grid_of(128, 256)
        spread[t] = one_hot(((row >> 4) == t) & ((row & 15) == (column & 15)))

    core_copy.wait_recv()

    def share(dy, expert):
        return coef[lax.rem(y + dy + NY, NY) * 2 + core, expert].astype(F32) * (1.0 / 1024.0)

    own_first, other_first = grp * 2, (y * 2 + 1 - core) * 2

    def partial_of(dy, xb):
        at = slice(xb * 128, (xb + 1) * 128)
        total = None
        for ref, first in ((w_own, own_first), (w_sib, other_first)):
            for e in range(2):
                term = share(dy, first + e) * ref[e, :, :, at].astype(F32)
                total = term if total is None else total + term
        return total

    halves = (pl.ds(0, 2), pl.ds(2, 2))
    for xb in range(NX):
        ybuf[0, xb] = partial_of(-4, xb).astype(BF16)
        if xb % 2:
            h = xb // 2
            remote(PH_Y, 3 * h, ybuf.at[0, halves[h]], yrecv.at[0, halves[h]],
                   device(dy=(-2, 2)[h])).start()
    for slot, dy, hop in ((1, 3, 1), (2, -3, -1)):
        for xb in range(NX):
            ybuf[slot, xb] = partial_of(dy, xb).astype(BF16)
        remote(PH_Y, slot, ybuf.at[slot], yrecv.at[slot], device(dy=hop)).start()

    def yx_send(k):
        dy = NEAR[k]
        if dy:
            remote(PH_YX, k, yxbuf.at[k, x], yxrecv.at[k, x], device(dy=dy)).start()
        else:
            yxrecv[k, x] = yxbuf[k, x]
        each(NX, lambda d: remote(
            PH_YX, k, yxbuf.at[k, lax.rem(x + d, NX)], yxrecv.at[k, x], device(dy=dy, dx=d)).start())

    for k in (1, 3, 2):
        for xb in range(NX):
            yxbuf[k, xb] = partial_of(NEAR[k], xb).astype(BF16)
        yx_send(k)

    arrived(PH_ATX, 0, atx.at[pl.ds(0, NX - 1)])
    for xb in range(NX):
        stacked = jnp.concatenate([atx[s, xb] for s in range(NX)], axis=0)
        a_ref[z, :, :, xb * 128:(xb + 1) * 128] = dot(order[...], stacked).astype(BF16).reshape(9, 16, 128)

    def z_hop(way, s):
        slot = lax.rem(z + (s if way else NZ - s), NZ)
        common = pl.ds(0, 5) if s < 3 else (pl.ds(3, 2) if way else pl.ds(0, 3))
        parts = [(PH_ATL if way else PH_ATR, common)]
        if s < 3 or way:
            parts.append((PH_ATL1 if way else PH_ATR1, pl.ds(5 + x, 1)))
        return [
            remote(phase, s, a_ref.at[slot, part], a_ref.at[slot, part], device(dz=NZ - 1 if way else 1))
            for phase, part in parts
        ]

    def along_x(slot):
        block = a_ref.at[slot, pl.ds(5 + x, 1)]
        each(NX, lambda d: remote(PH_AX, 0, block, block, device(dx=d)).start())

    for way in range(2):
        for copy in z_hop(way, 0):
            copy.start()

    arrived(PH_COX, 0, cox.at[pl.ds(0, NX - 1)])
    stacked = jnp.concatenate([cox[s, 0:48] for s in range(NX)], axis=0)
    codes = cox[0, 48:64].astype(F32)
    for s in range(1, NX):
        codes = codes + cox[s, 48:64].astype(F32)
    codes = codes.astype(BF16)
    for t in range(NZ):
        wide = (dot(stacked, spread[t]) * same[...]).astype(BF16)
        packed = dot(gather16[...], wide).astype(BF16)
        cobuf[t, 0] = packed[:, 0:128]
        cobuf[t, 1] = packed[:, 128:256]
        cobuf[t, 2] = codes
    each(NZ, lambda d: remote(
        PH_COZ, 0, cobuf.at[lax.rem(z + d, NZ)], corecv.at[z], device(dz=d)).start())
    corecv[z] = cobuf[z]

    for h in range(2):
        arrived(PH_Y, 3 * h, yrecv.at[0, halves[h]])
    for slot in (1, 2):
        arrived(PH_Y, slot, yrecv.at[slot])
    for k, dy, slot in ((0, -2, 2), (4, 2, 1)):
        for xb in range(NX):
            total = partial_of(dy, xb) + yrecv[slot, xb].astype(F32)
            if (xb >= 2) == (k == 4):
                total = total + yrecv[0, xb].astype(F32)
            yxbuf[k, xb] = total.astype(BF16)
        yx_send(k)

    for i in range(9):
        opening, closing = SPANS[DEGREE[i]]
        first = ENTRY[i, opening]
        rt35[first:first + closing - opening, :] = rt_in[i, opening:closing, :]
    rt35[35:40, :] = jnp.zeros((5, 64), F32)
    table = rt35[...]
    high = table.astype(BF16)
    rot2[:, 0:64] = high
    rot2[:, 64:128] = (table - high.astype(F32)).astype(BF16)

    arrived(PH_COZ, 0, corecv.at[pl.ds(0, NZ - 1)])
    for half in range(2):
        tall = jnp.transpose(corecv[:, half].reshape(128, 128).astype(F32)).astype(BF16)
        rows = 128 if half == 0 else 16
        cs[half * 128:half * 128 + rows, :] = tall[0:rows]

    def turned(entries, values, opening, closing, i):
        total = entries[i, opening] * values(opening)
        for b in range(opening + 1, closing):
            total = total + entries[i, b] * values(b)
        return total

    def entries_of(t, at):
        return {key: turns[t, k:k + 1, at] for key, k in ENTRY.items()}

    def prepare(t):
        lanes = lax.broadcasted_iota(I32, (128, 128), 0).astype(F32)
        folded = (lax.broadcasted_iota(I32, (128, 128), 0) & 63).astype(F32)
        for q in range(NX):
            at = slice(q * 128, (q + 1) * 128)
            codes = corecv[t, 2].astype(F32)
            oh[t, :, at] = one_hot(lanes == codes[q * 4:q * 4 + 1])
            oh[NZ + t % 2, :, at] = one_hot(lanes == codes[q * 4 + 1:q * 4 + 2])
            oh[NZ + 2 + t % 2, :, at] = one_hot(folded == codes[q * 4 + 2:q * 4 + 3])
        ch[t % 2] = dot(cs[...], oh[NZ + t % 2])
        turns[t] = dot(rot2[...], oh[NZ + 2 + t % 2])
        for q in range(NX):
            at = slice(q * 128, (q + 1) * 128)
            entries = entries_of(t, at)
            for opening, closing in SPANS:
                for i in range(opening, closing):
                    grads_at[t, i * 16:(i + 1) * 16, at] = turned(
                        entries, lambda b: ch[t % 2, b * 16:(b + 1) * 16, at], opening, closing, i)

    def pass_on(s):
        for way in range(2):
            for copy in z_hop(way, s - 1):
                copy.wait_recv()
            for copy in z_hop(way, s):
                copy.start()
            along_x(lax.rem(z + (s if way else NZ - s), NZ))

    pass_on(1)
    for t in range(0, 3):
        prepare(t)

    for k, dy in enumerate(NEAR):
        arrived(PH_YX, k, yxrecv.at[k] if dy else yxrecv.at[k, pl.ds(0, NX - 1)])
    lane_slot = lax.broadcasted_iota(I32, (32, 128), 1) >> 4
    packed = [jnp.zeros((32, 128), F32) for t in range(NZ)]
    for l in range(3):
        for s in range(NX):
            total = yxrecv[0, s, l].astype(F32)
            for k in range(1, 5):
                total = total + yxrecv[k, s, l].astype(F32)
            mx[s, l] = total.astype(BF16)
        for h in range(2):
            block = mx[2 * h:2 * h + 2, l].reshape(32, 128).astype(F32)
            for t in range(NZ):
                shifted = roll16(block, h * 4 + l - t)
                packed[t] = jnp.where(lane_slot == h * 4 + l, shifted, packed[t])
    for t in range(NZ):
        mzbuf[t] = packed[t].astype(BF16).reshape(2, 16, 128)
    each(NZ, lambda d: remote(
        PH_MZ, 0, mzbuf.at[lax.rem(z + d, NZ)], wc.at[z], device(dz=d)).start())
    wc[z] = mzbuf[z]
    mc[z] = mx[...]
    pass_on(2)
    for t in range(3, 5):
        prepare(t)
    pass_on(3)
    for t in range(5, 8):
        prepare(t)
    for way in (1, 0):
        for copy in z_hop(way, 3):
            copy.wait_recv()
        if way:
            along_x(lax.rem(z + 4, NZ))
    arrived(PH_AX, 0, a_ref.at[pl.ds(0, NZ - 1), pl.ds(0, NX - 1)])
    arrived(PH_MZ, 0, wc.at[pl.ds(0, NZ - 1)])
    for k, dz in enumerate(NEAR):
        if dz:
            remote(PH_MC, k, mx, mc.at[z], device(dz=NZ + dz)).start()

    columns16 = jnp.concatenate(
        [jnp.concatenate([wc[t, s] for t in range(NZ)], axis=0) for s in range(2)], axis=0)
    flipped = jnp.transpose(columns16.astype(F32)).astype(BF16)
    for b in range(9):
        l = DEGREE[b]
        maps = jnp.concatenate([flipped[h * 64 + l * 16:h * 64 + (l + 1) * 16] for h in range(2)], axis=1)
        hs[b * 16:(b + 1) * 16, :] = dot(maps, a_ref[:, b].reshape(128, 512), NT).astype(BF16)


    def edges(t):
        hh[t] = dot(hs[...], oh[t])
        for q in range(NX):
            at = slice(q * 128, (q + 1) * 128)
            entries = entries_of(t, at)
            grads, inner, gate = [], None, None
            for opening, closing in SPANS:
                for i in range(opening, closing):
                    hidden = turned(entries, lambda b: hh[t, b * 16:(b + 1) * 16, at], opening, closing, i)
                    grad = grads_at[t, i * 16:(i + 1) * 16, at]
                    if i == 0:
                        gate = jax.nn.sigmoid(hidden)
                    inner = grad * hidden if inner is None else inner + grad * hidden
                    grads.append(grad * gate)
            grads[0] = grads[0] + inner * gate * (1.0 - gate)
            for opening, closing in SPANS:
                for b in range(opening, closing):
                    total = entries[opening, b] * grads[opening]
                    for i in range(opening + 1, closing):
                        total = total + entries[i, b] * grads[i]
                    u_ref[t, b * 16:(b + 1) * 16, at] = total.astype(BF16)

    for t in range(NZ):
        edges(t)
    wide_u = jnp.concatenate([u_ref[t] for t in range(NZ)], axis=1)
    g_acc[...] = dot(wide_u, jnp.concatenate([oh[t] for t in range(NZ)], axis=1), NT)

    sums = g_acc[...]
    narrow = sums.astype(BF16)
    for h in range(2):
        sgt[h * 64 + 48:h * 64 + 64, :] = jnp.zeros((16, 256), F32)
    for l, (opening, closing) in enumerate(SPANS):
        total = jnp.zeros((16, 512), F32)
        for b in range(opening, closing):
            total = total + dot(narrow[b * 16:(b + 1) * 16], a_ref[:, b].reshape(128, 512))
        for h in range(2):
            sgt[h * 64 + l * 16:h * 64 + (l + 1) * 16, :] = total[:, h * 256:(h + 1) * 256]
    tall = jnp.transpose(sgt[...]).astype(BF16)
    for t in range(NZ):
        for s in range(2):
            first = s * 128 + t * 16
            sgbuf[t, s] = tall[first:first + 16]
    each(NZ, lambda d: remote(
        PH_SZ, 0, sgbuf.at[lax.rem(z + d, NZ)], sgrecv.at[z], device(dz=d)).start())
    sgrecv[z] = sgbuf[z]
    turned_sums = jnp.transpose(
        jnp.concatenate([sums, jnp.zeros((112, 128), F32)], axis=0)).astype(BF16)
    for t in range(NZ):
        gbuf[t] = turned_sums[t * 16:(t + 1) * 16]
    each(NZ, lambda d: remote(
        PH_GZ, 0, gbuf.at[lax.rem(z + d, NZ)], grecv.at[z], device(dz=d)).start())
    grecv[z] = gbuf[z]

    below, above = mc.at[lax.rem(z + NZ - 2, NZ)], mc.at[lax.rem(z + 2, NZ)]
    arrived(PH_MC, 4, below)
    arrived(PH_MC, 0, above)
    for k, ref, dz in (
        (0, below, 1), (1, above, NZ - 1), (2, below.at[halves[0]], 2), (3, above.at[halves[1]], NZ - 2),
    ):
        remote(PH_MCF, k, ref, ref, device(dz=dz)).start()

    row, column = grid_of(192, 16)
    block, within = split48(row)
    expand[...] = one_hot(column == block * 4 + (within & 3))
    for t in range(NZ):
        row, column = grid_of(256, 128)
        fold[t] = one_hot(((column >> 4) == t) & ((row & 15) == (column & 15)))

    arrived(PH_SZ, 0, sgrecv.at[pl.ds(0, NZ - 1)])
    blocks = [sgrecv[t].reshape(32, 128).astype(F32) for t in range(NZ)]
    for l in range(3):
        for h in range(2):
            total = jnp.zeros((32, 128), F32)
            for t in range(NZ):
                total = jnp.where(lane_slot == t, roll16(blocks[t], t - (h * 4 + l)), total)
            total = total.astype(BF16)
            sg4[2 * h, l] = total[0:16]
            sg4[2 * h + 1, l] = total[16:32]

    for k in (0, 4, 1, 3, 2):
        dy = NEAR[k]
        if dy:
            remote(PH_SYX, k, sg4.at[x], sgx.at[k, x], device(dy=dy)).start()
        else:
            sgx[k, x] = sg4[x]
        each(NX, lambda d: remote(
            PH_SYX, k, sg4.at[lax.rem(x + d, NX)], sgx.at[k, x], device(dy=dy, dx=d)).start())

    arrived(PH_SYX, 0, sgx.at[0])
    arrived(PH_SYX, 4, sgx.at[4])
    for h, k, hop in ((0, 0, -2), (1, 4, 2)):
        remote(PH_FW, 3 * h, sgx.at[k, halves[h]], forwarded.at[0, halves[h]], device(dy=hop)).start()
    for slot, k, hop in ((1, 4, 1), (2, 0, -1)):
        remote(PH_FW, slot, sgx.at[k], forwarded.at[slot], device(dy=hop)).start()

    arrived(PH_GZ, 0, grecv.at[pl.ds(0, NZ - 1)])
    held = jnp.zeros((192, 128), F32)
    for t in range(NZ):
        wide = (dot(expand[...], grecv[t]) * same[...]).astype(BF16)
        held = held + dot(wide, fold[t])

    for k, dz in ((1, 1), (3, -1)):
        arrived(PH_MC, k, mc.at[lax.rem(z + NZ + dz, NZ)])
    arrived(PH_MCF, 0, mc.at[lax.rem(z + NZ - 3, NZ)])
    arrived(PH_MCF, 1, mc.at[lax.rem(z + 3, NZ)])
    for h in range(2):
        arrived(PH_MCF, 2 + h, mc.at[lax.rem(z + 4, NZ), halves[h]])
    coefficient = split48(lax.broadcasted_iota(I32, (192, 128), 0))[1] >> 2
    parts = jnp.zeros((192, 512), F32)
    for l, (opening, closing) in enumerate(SPANS):
        inside = (coefficient >= opening) & (coefficient < closing)
        maps = jnp.concatenate(
            [jnp.concatenate([mc[t, s, l] for t in range(NZ)], axis=0) for s in range(NX)], axis=0)
        parts = parts + dot(jnp.where(inside, held, 0.0).astype(BF16), maps, NT)
    for s in range(NX):
        gxbuf[s] = parts[s * 48:(s + 1) * 48].astype(BF16)
    each(NX, lambda d: remote(
        PH_GX, 0, gxbuf.at[lax.rem(x + d, NX)], gxrecv.at[d], device(dx=d)).start())
    gxrecv[0] = gxbuf[x]
    for k in (1, 2, 3):
        arrived(PH_SYX, k, sgx.at[k] if NEAR[k] else sgx.at[k, pl.ds(0, NX - 1)])
    for e in range(4):
        for s in range(NX):
            total = None
            for k, dy in enumerate(NEAR):
                term = share(-dy, (other_first if e < 2 else own_first) + e % 2) * sgx[k, s].astype(F32)
                total = term if total is None else total + term
            near_sum[e, s] = total
    arrived(PH_GX, 0, gxrecv.at[pl.ds(0, NX - 1)])
    total = gxrecv[0].astype(F32)
    for s in range(1, NX):
        total = total + gxrecv[s].astype(F32)
    for b in range(9):
        ga_ref[b] = total[b * 4:b * 4 + 4]

    for h in range(2):
        arrived(PH_FW, 3 * h, forwarded.at[0, halves[h]])
    for slot in (1, 2):
        arrived(PH_FW, slot, forwarded.at[slot])

    def expert_sum(e, expert, s):
        total = near_sum[e, s]
        for slot, dy in ((0, 4), (1, -3), (2, 3)):
            total = total + share(dy, expert) * forwarded[slot, s].astype(F32)
        return total

    for e in range(2):
        for s in range(NX):
            endbuf[e, s] = expert_sum(e, other_first + e, s).astype(BF16)
    end_copy = remote(PH_END, 0, endbuf, endrecv, device(other=True))
    end_copy.start()
    for e in range(2):
        for s in range(NX):
            ge_ref[e, :, :, s * 128:(s + 1) * 128] = expert_sum(e + 2, own_first + e, s)
    end_copy.wait_recv()
    for e in range(2):
        for s in range(NX):
            ge_ref[e, :, :, s * 128:(s + 1) * 128] += endrecv[e, s].astype(F32)

    core_copy.wait_send()
    end_copy.wait_send()
    for s in range(4):
        for way in range(2):
            for copy in z_hop(way, s):
                copy.wait_send()
    left(PH_AX, 0, a_ref.at[pl.ds(0, NZ - 1), pl.ds(0, NX - 1)])
    for phase, ref in ((PH_Y, ybuf), (PH_FW, forwarded)):
        for h in range(2):
            left(phase, 3 * h, ref.at[0, halves[h]])
        for slot in (1, 2):
            left(phase, slot, ref.at[slot])
    for k, dy in enumerate(NEAR):
        left(PH_YX, k, yxbuf.at[k] if dy else yxbuf.at[k, pl.ds(0, NX - 1)])
        left(PH_SYX, k, sg4 if dy else sg4.at[pl.ds(0, NX - 1)])
    left(PH_ATX, 0, atx.at[pl.ds(0, NX - 1)])
    left(PH_COX, 0, cox.at[pl.ds(0, NX - 1)])
    left(PH_GX, 0, gxbuf.at[pl.ds(0, NX - 1)])
    left(PH_COZ, 0, cobuf.at[pl.ds(0, NZ - 1)])
    left(PH_MZ, 0, mzbuf.at[pl.ds(0, NZ - 1)])
    for k in (0, 1, 3, 4):
        left(PH_MC, k, mx)
    for slot, ref in enumerate((mx, mx, mx.at[halves[0]], mx.at[halves[1]])):
        left(PH_MCF, slot, ref)
    left(PH_SZ, 0, sgbuf.at[pl.ds(0, NZ - 1)])
    left(PH_GZ, 0, gbuf.at[pl.ds(0, NZ - 1)])


def shards(
    atoms, cotangent, expert_weights, coefficients, src_owner, src_slot, tgt_slot, rot_index, rot_table
):
    hbm = pl.BlockSpec(memory_space=pltpu.HBM)
    vmem = pl.BlockSpec(memory_space=pltpu.VMEM)
    smem = pl.BlockSpec(memory_space=pltpu.SMEM)

    def b16(*shape):
        return pltpu.VMEM(shape, BF16)

    def f32(*shape):
        return pltpu.VMEM(shape, F32)

    grad_atoms, grad_experts = pl.pallas_call(
        kernel,
        out_shape=(
            jax.ShapeDtypeStruct((9, 4, 512), F32),
            jax.ShapeDtypeStruct((2, 3, 16, 512), F32),
        ),
        in_specs=[smem] + [hbm] * 8,
        out_specs=(vmem, vmem),
        scratch_shapes=[
            b16(2, 3, 16, 512),
            b16(2, 3, 16, 512),
            b16(9, 4, 512),
            b16(9, 4, 512),
            pltpu.VMEM((4, 1, 128), I32),
            f32(9, 9, 64),
            f32(40, 64),
            b16(3, NX, 3, 16, 128),
            b16(3, NX, 3, 16, 128),
            b16(5, NX, 3, 16, 128),
            b16(5, NX, 3, 16, 128),
            b16(NX, 3, 16, 128),
            b16(NZ, 2, 16, 128),
            b16(NZ, 2, 16, 128),
            b16(NZ, NX, 3, 16, 128),
            f32(1, 48, 512),
            b16(NX + 1, NX, 48, 128),
            b16(NZ, 9, 16, 512),
            f32(1, 48, 512),
            b16(2 * NX, 64, 128),
            b16(NZ, 3, 16, 128),
            b16(NZ, 3, 16, 128),
            b16(192, 16),
            b16(NZ, 256, 128),
            b16(NZ, 128, 256),
            b16(144, 192),
            b16(16, 192),
            f32(192, 256),
            b16(40, 128),
            b16(144, 128),
            b16(144, 128),
            f32(NZ, 144, 512),
            f32(2, 144, 512),
            f32(NZ, 144, 512),
            f32(NZ, 40, 512),
            b16(NZ + 4, 128, 512),
            b16(NZ, 144, 512),
            f32(144, 128),
            b16(NZ, 16, 256),
            b16(NZ, 16, 256),
            b16(NX, 48, 512),
            b16(NX, 48, 512),
            f32(128, 256),
            b16(NZ, 2, 16, 128),
            b16(NZ, 2, 16, 128),
            b16(NX, 3, 16, 128),
            b16(5, NX, 3, 16, 128),
            b16(3, NX, 3, 16, 128),
            f32(4, NX, 3, 16, 128),
            b16(2, NX, 3, 16, 128),
            b16(2, NX, 3, 16, 128),
            pltpu.SemaphoreType.DMA((8,)),
            pltpu.SemaphoreType.DMA((20, 5)),
            pltpu.SemaphoreType.DMA((20, 5)),
        ],
        compiler_params=pltpu.CompilerParams(
            collective_id=0, has_side_effects=True, vmem_limit_bytes=60 * 1024 * 1024
        ),
        cost_estimate=pl.CostEstimate(
            flops=2_000_000_000, bytes_accessed=1_000_000, transcendentals=65536
        ),
    )(
        coefficients, expert_weights, atoms[0].transpose(1, 0, 2), cotangent[0].transpose(1, 0, 2),
        src_owner.reshape(1, -1), src_slot, tgt_slot, rot_index, rot_table.transpose(1, 2, 0),
    )
    return grad_atoms.transpose(1, 0, 2)[None], grad_experts


def solution(mesh):
    placed = (
        P("grp", "graph", None, None),
        P("grp", "graph", None, None),
        P("grp", None, "graph", None),
        P(),
        P("grp", "graph", None),
        P("grp", "graph"),
        P("grp", "graph"),
        P("grp", "graph"),
        P(),
    )
    return jax.shard_map(
        shards,
        mesh=mesh,
        in_specs=placed,
        out_specs=(P("grp", "graph", None, None), P("grp", None, "graph", None)),
        check_vma=False,
    )
```
